32 devices in a mesh: gx: 4 (over y, core), gy: 4 (over z), gz: 2 (over x).
Axes of the slice: x: 2, y: 2, z: 4, core: 2. Of those that a mesh axis runs over, the one named last changes fastest.
Arguments:
- positions: float32 [4, 4, 2, 3, 512], P('gx', 'gy', 'gz'), may hold values from 0 to 1
- attributes: bfloat16 [4, 4, 2, 512, 128], P('gx', 'gy', 'gz'), may hold values from -6 to 6
- edge_center: int32 [4, 4, 2, 6144], P('gx', 'gy', 'gz'), may hold values from 0 to 511
- edge_other: int32 [4, 4, 2, 6144], P('gx', 'gy', 'gz'), may hold values from 0 to 2687
- edge_count: int32 [4, 4, 2], P('gx', 'gy', 'gz'), may hold values from 1536 to 6144, as said below
- rim_rows: int32 [4, 4, 2, 8, 128], P('gx', 'gy', 'gz'), may hold values from 0 to 511
- z_rows: int32 [4, 4, 2, 128], P('gx', 'gy', 'gz'), may hold values from 0 to 2559
- w_emb: bfloat16 [128, 256], replicated, may hold values from -0.5 to 0.5
- w_rbf: float32 [8, 256], replicated, may hold values from -2 to 2
- w_chan: bfloat16 [256, 64], replicated, may hold values from -0.375 to 0.375
- w_lat: bfloat16 [256, 256], replicated, may hold values from -0.375 to 0.375
- w_ten: bfloat16 [192, 256], replicated, may hold values from -0.4375 to 0.4375
- w_out: float32 [256], replicated, may hold values from -0.375 to 0.375
Outputs:
- atom_energy: float32 [4, 4, 2, 512], P('gx', 'gy', 'gz')
- forces: float32 [4, 4, 2, 3, 512], P('gx', 'gy', 'gz')
The draws below stay inside these ranges and needn't reach their ends.
Inputs may be any that keep to these rules, and one draw needn't show every extreme that they name: `edge_count`: a multiple of 128; a device's edge slots below its count are live; some device has 6144.
All inputs are finite; a program needn't handle non-finite values.
Results may differ from the reference program's by a relative error of at most 0.005.
Values may be sent and summed in bfloat16 or wider, within the bound.
No kernel may reach another device: no remote copies, remote signals or barrier semaphores. Data moves between devices by JAX's collectives and lax.ppermute only.
A program may use at most 64 MiB of HBM per device.

```python
import jax
import jax.numpy as jnp
from jax import lax

F = 256
CH = 64
ADIM = 128
NB = 8
ATOMS = 512
EDGES = 6144
RIM = 128
ZROWS = 128
TBL = 2688
N_GX = 4
N_GY = 4
N_GZ = 2


def draw_edge_count(key, part):
    blocks_all = EDGES // 128
    lowest = EDGES // 512
    devices = N_GX * N_GY * N_GZ
    key_first, key_second, key_third = jax.random.split(key, 3)
    draw_first = jax.random.randint(key_first, (devices,), lowest, blocks_all + 1)
    draw_second = jax.random.randint(key_second, (devices,), lowest, blocks_all + 1)
    picked = jnp.minimum(draw_first, draw_second)
    busiest = jax.random.randint(key_third, (), 0, devices)
    picked = jnp.where(jnp.arange(devices) == busiest, blocks_all, picked)
    return (picked * 128).reshape(N_GX, N_GY, N_GZ).astype(jnp.int32)


def with_ends(values, rng, smallest, largest):
    extent = values.shape
    index_at = [jax.random.randint(jax.random.fold_in(rng, axis), (), 0, extent[axis]) for axis in range(len(extent))]
    values = values.at[tuple(index_at)].set(smallest)
    longest = extent.index(max(extent))
    index_at[longest] = (index_at[longest] + 1) % extent[longest]
    return values.at[tuple(index_at)].set(largest)


def levels(own_key, extent, shards, least, high):
    loudness = 1.0
    for axis_at, blocks in shards:
        steps = jax.random.uniform(jax.random.fold_in(jax.random.fold_in(own_key, 6), axis_at), (blocks,), jnp.float32, least / len(shards), high / len(shards))
        loudness = loudness * jnp.repeat(jnp.exp(steps), extent[axis_at] // blocks).reshape((-1,) + (1,) * (len(extent) - 1 - axis_at))
    return loudness


def bell_draw(key, shape, deviation, reach, shards=(), dtype=jnp.bfloat16):
    entries = jax.random.normal(key, shape, jnp.float32) * deviation
    if len(shards) > 0:
        entries = levels(key, shape, shards, -0.22, 0.18) * entries
    return jnp.clip(entries, min=-reach, max=reach).astype(dtype)


def setup_inputs(seed: int = 0) -> dict:
    streams_of = jax.random.split(jax.random.key(seed), 14)
    positions = jnp.clip(1.0 * jax.random.uniform(streams_of[0], (N_GX, N_GY, N_GZ, 3, ATOMS), jnp.float32) ** levels(streams_of[0], (N_GX, N_GY, N_GZ, 3, ATOMS), ((0, 4), (1, 4), (2, 2)), -0.2, 0.2), 0.0, 1.0)
    attributes = bell_draw(streams_of[1], (N_GX, N_GY, N_GZ, ATOMS, ADIM), 1.0, 6.0, ((0, 4), (1, 4), (2, 2)))
    edge_center = with_ends(jax.random.randint(streams_of[2], (N_GX, N_GY, N_GZ, EDGES), 0, ATOMS), jax.random.fold_in(streams_of[2], 1), 0, ATOMS - 1).astype(jnp.int32)
    edge_other = with_ends(jax.random.randint(streams_of[3], (N_GX, N_GY, N_GZ, EDGES), 0, TBL), jax.random.fold_in(streams_of[3], 1), 0, TBL - 1).astype(jnp.int32)
    edge_count = draw_edge_count(jax.random.fold_in(streams_of[13], 71), 0)
    rim_rows = with_ends(jax.random.randint(streams_of[5], (N_GX, N_GY, N_GZ, 8, RIM), 0, ATOMS), jax.random.fold_in(streams_of[5], 1), 0, ATOMS - 1).astype(jnp.int32)
    z_rows = with_ends(jax.random.randint(streams_of[6], (N_GX, N_GY, N_GZ, ZROWS), 0, ATOMS + 16 * RIM), jax.random.fold_in(streams_of[6], 1), 0, (ATOMS + 16 * RIM) - 1).astype(jnp.int32)
    w_emb = bell_draw(streams_of[7], (ADIM, F), ADIM ** -0.5, 0.5)
    w_rbf = bell_draw(streams_of[8], (NB, F), NB ** -0.5, 2.0, (), jnp.float32)
    w_chan = bell_draw(streams_of[9], (F, CH), F ** -0.5, 0.375)
    w_lat = bell_draw(streams_of[10], (F, F), F ** -0.5, 0.375)
    w_ten = bell_draw(streams_of[11], (3 * CH, F), (3 * CH) ** -0.5, 0.4375)
    w_out = bell_draw(streams_of[12], (F,), F ** -0.5, 0.375, (), jnp.float32)
    return dict(positions=positions, attributes=attributes, edge_center=edge_center, edge_other=edge_other, edge_count=edge_count, rim_rows=rim_rows, z_rows=z_rows, w_emb=w_emb, w_rbf=w_rbf, w_chan=w_chan, w_lat=w_lat, w_ten=w_ten, w_out=w_out)


rim_cells = [(0, 0), (0, 1), (0, 2), (1, 0), (1, 2), (2, 0), (2, 1), (2, 2)]
cycle_cells = [(cycle_row, cycle_column) for cycle_row in range(5) for cycle_column in range(5) if cycle_row in (0, 4) or cycle_column in (0, 4)]

def source_of(position):
    if position == 0:
        return (-1, 2)
    if position == 4:
        return (1, 0)
    return (0, position - 1)

def embed_atoms(atom_rows, w_emb):
    return jax.nn.silu(jnp.dot(atom_rows, w_emb, preferred_element_type=jnp.float32)).astype(jnp.bfloat16)

def split_join(values):
    upper = lax.optimization_barrier(values.astype(jnp.bfloat16))
    lower = (values - upper.astype(jnp.float32)).astype(jnp.bfloat16)
    return upper.astype(jnp.float32) + lower.astype(jnp.float32)

def harmonics(directions):
    along_x, along_y, along_z = (directions[0], directions[1], directions[2])
    root_three = 3.0 ** 0.5
    return [jnp.ones_like(along_x), along_x, along_y, along_z, root_three * along_x * along_y, root_three * along_y * along_z, root_three * along_z * along_x, 0.5 * root_three * (along_x * along_x - along_y * along_y), 0.5 * (3.0 * along_z * along_z - 1.0)]

def latent_of(position_table, feature_table, centers, others, w_rbf):
    separation = position_table[:, others] - position_table[:, centers]
    squared = lax.optimization_barrier(jnp.sum(separation * separation, axis=0))
    distance = jnp.sqrt(squared + 0.25)
    directions = separation / distance[None, :]
    envelope = 1.0 / (1.0 + squared * squared / 16.0)
    radii = 0.5 + 0.4 * jnp.arange(w_rbf.shape[0]).astype(jnp.float32)
    radial = jnp.exp(-jnp.square((distance[None, :] - radii[:, None]) / 0.5)) * envelope[None, :]
    mixed = lax.dot_general(radial, w_rbf, (((0,), (0,)), ((), ())), precision=lax.Precision.HIGHEST, preferred_element_type=jnp.float32)
    mixed = mixed + feature_table[centers].astype(jnp.float32) + feature_table[others].astype(jnp.float32)
    return (jax.nn.silu(mixed).astype(jnp.bfloat16), directions, envelope)

def tensor_terms(latent, directions, centers, live_mask, w_chan, atom_count):
    channel = jnp.dot(latent, w_chan, preferred_element_type=jnp.float32) * live_mask[:, None]
    harmonic = harmonics(directions)
    products = jnp.concatenate([channel * term[:, None] for term in harmonic], axis=1)
    return jax.ops.segment_sum(products, centers, num_segments=atom_count)

def energy_terms(latent, directions, envelope, tensor, centers, live_mask, w_lat, w_ten, w_out):
    harmonic = harmonics(directions)
    gathered = tensor[centers]
    width = gathered.shape[1] // 9
    bands = []
    for lower, upper in ((0, 1), (1, 4), (4, 9)):
        band = gathered[:, lower * width:(lower + 1) * width] * harmonic[lower][:, None]
        for index in range(lower + 1, upper):
            band = band + gathered[:, index * width:(index + 1) * width] * harmonic[index][:, None]
        bands.append(band)
    invariant = jnp.concatenate(bands, axis=1).astype(jnp.bfloat16)
    hidden = jax.nn.silu(jnp.dot(latent, w_lat, preferred_element_type=jnp.float32) + jnp.dot(invariant, w_ten, preferred_element_type=jnp.float32))
    return lax.optimization_barrier(jnp.sum(hidden * w_out[None, :], axis=1)) * envelope * live_mask

def reference(positions, attributes, edge_center, edge_other, edge_count, rim_rows, z_rows, w_emb, w_rbf, w_chan, w_lat, w_ten, w_out):
    grid_shape = (N_GX, N_GY, N_GZ)
    devices = N_GX * N_GY * N_GZ
    embedded = embed_atoms(attributes.reshape(-1, ADIM), w_emb).reshape(grid_shape + (ATOMS, F))
    rim_flat = rim_rows.reshape(devices, 8 * RIM)
    rim_features = jax.vmap(lambda atom_table, row_index: atom_table[row_index])(embedded.reshape(devices, ATOMS, F), rim_flat).reshape(grid_shape + (8, RIM, F))
    rim_positions = split_join(jax.vmap(lambda atom_table, row_index: atom_table[:, row_index])(positions.reshape(devices, 3, ATOMS), rim_flat)).reshape(grid_shape + (3, 8, RIM))
    cycle_features = []
    cycle_positions = []
    for cycle_row, cycle_column in cycle_cells:
        shift_x, cell_row = source_of(cycle_row)
        shift_y, cell_column = source_of(cycle_column)
        rim_index = rim_cells.index((cell_row, cell_column))
        cycle_features.append(jnp.roll(rim_features[:, :, :, rim_index], (-shift_x, -shift_y), axis=(0, 1)))
        shifted = jnp.roll(rim_positions[:, :, :, :, rim_index], (-shift_x, -shift_y), axis=(0, 1))
        cycle_positions.append(shifted + jnp.array([shift_x, shift_y, 0], jnp.float32)[:, None])
    inner_features = jnp.concatenate([embedded] + cycle_features, axis=3)
    inner_positions = jnp.concatenate([positions] + cycle_positions, axis=4)
    inner_len = ATOMS + 16 * RIM
    slab_flat = z_rows.reshape(devices, ZROWS)
    slab_features = jax.vmap(lambda atom_table, row_index: atom_table[row_index])(inner_features.reshape(devices, inner_len, F), slab_flat).reshape(grid_shape + (ZROWS, F))
    slab_positions = split_join(jax.vmap(lambda atom_table, row_index: atom_table[:, row_index])(inner_positions.reshape(devices, 3, inner_len), slab_flat)).reshape(grid_shape + (3, ZROWS))
    slab_features = jnp.roll(slab_features, 1, axis=2)
    slab_positions = jnp.roll(slab_positions, 1, axis=2)
    slab_lift = (1 - 2 * jnp.arange(N_GZ)).astype(jnp.float32)
    slab_positions = slab_positions.at[:, :, :, 2].add(slab_lift[None, None, :, None])
    feature_table = jnp.concatenate([inner_features, slab_features], axis=3).reshape(devices, TBL, F)
    position_table = jnp.concatenate([inner_positions, slab_positions], axis=4).reshape(devices, 3, TBL)

    def device_pass(items):
        place_table, embed_table, centers, others, live_count = items
        live_mask = (jnp.arange(centers.shape[0]) < live_count).astype(jnp.float32)

        def total_energy(place_values):
            latent, directions, envelope = latent_of(place_values, embed_table, centers, others, w_rbf)
            tensor = 0.125 * tensor_terms(latent, directions, centers, live_mask, w_chan, ATOMS)
            edge_energy = energy_terms(latent, directions, envelope, tensor, centers, live_mask, w_lat, w_ten, w_out)
            return (jnp.sum(edge_energy), jax.ops.segment_sum(edge_energy, centers, num_segments=ATOMS))
        total, pullback, atom_values = jax.vjp(total_energy, place_table, has_aux=True)
        gradient = pullback(jnp.ones_like(total))[0]
        return (atom_values, gradient)
    atom_energy, gradient = lax.map(device_pass, (position_table, feature_table, edge_center.reshape(devices, EDGES), edge_other.reshape(devices, EDGES), edge_count.reshape(devices)))
    gradient = gradient.reshape(grid_shape + (3, TBL))
    slab_grad = jnp.roll(gradient[..., inner_len:], 1, axis=2).reshape(devices, 3, ZROWS)
    inner_grad = jax.vmap(lambda grads, row_index, values: grads.at[:, row_index].add(values))(gradient[..., :inner_len].reshape(devices, 3, inner_len), slab_flat, slab_grad).reshape(grid_shape + (3, inner_len))
    own_grad = inner_grad[..., :ATOMS]
    cycle_grad = inner_grad[..., ATOMS:].reshape(grid_shape + (3, 16, RIM))
    rim_grad = jnp.zeros(grid_shape + (3, 8, RIM), jnp.float32)
    for cycle_index, (cycle_row, cycle_column) in enumerate(cycle_cells):
        shift_x, cell_row = source_of(cycle_row)
        shift_y, cell_column = source_of(cycle_column)
        rim_index = rim_cells.index((cell_row, cell_column))
        rim_grad = rim_grad.at[:, :, :, :, rim_index].add(jnp.roll(cycle_grad[:, :, :, :, cycle_index], (shift_x, shift_y), axis=(0, 1)))
    own_grad = jax.vmap(lambda grads, row_index, values: grads.at[:, row_index].add(values))(own_grad.reshape(devices, 3, ATOMS), rim_flat, rim_grad.reshape(devices, 3, 8 * RIM))
    return (atom_energy.reshape(grid_shape + (ATOMS,)), (-own_grad).reshape(grid_shape + (3, ATOMS)))
```

```python
import jax
import jax.numpy as jnp
from jax import lax
from jax.experimental import pallas as pl
from jax.experimental.pallas import tpu as pltpu
from jax.sharding import PartitionSpec as P

f32 = jnp.float32
bf16 = jnp.bfloat16
LANES = 128
PARTS = 16
ROOT3 = 3.0**0.5
BANDS = (0, 1, 1, 1, 2, 2, 2, 2, 2)

rim_cells = [(0, 0), (0, 1), (0, 2), (1, 0), (1, 2), (2, 0), (2, 1), (2, 2)]
cycle_cells = [(p, q) for p in range(5) for q in range(5) if p in (0, 4) or q in (0, 4)]


def source_of(position):
    if position == 0:
        return (-1, 2)
    if position == 4:
        return (1, 0)
    return (0, position - 1)


routes = {}
for _cycle, (_p, _q) in enumerate(cycle_cells):
    (_sx, _a), (_sy, _b) = source_of(_p), source_of(_q)
    routes.setdefault((_sx, _sy), []).append((_cycle, rim_cells.index((_a, _b))))
directions = sorted(routes, key=lambda way: (-len(routes[way]), way))


def dot(a, b):
    return lax.dot_general(a, b, (((1,), (0,)), ((), ())), preferred_element_type=f32)


def dot_t(a, b):
    return lax.dot_general(a, b, (((1,), (1,)), ((), ())), preferred_element_type=f32)


def rows_of(shape):
    return lax.broadcasted_iota(jnp.int32, shape, 0)


def one_hot(index, size):
    return jnp.where(rows_of((size, index.shape[1])) == index, 1.0, 0.0)


def halves(values):
    upper = values.astype(bf16).astype(f32)
    return upper, values - upper


def masked(hot_low, high16, value):
    mask = jnp.where(high16 == value, 1.0, 0.0).astype(bf16)
    size, lanes = hot_low.shape
    return (hot_low.reshape(size // 16, 16, lanes) * mask[None]).reshape(size, lanes)


def sigmoid(x):
    return 0.5 * jnp.tanh(0.5 * x) + 0.5


def pack_kernel(pos_ref, attr_ref, rim_ref, own_ref, *rest):
    sends, parts = rest[:-1], rest[-1]
    atoms, width = attr_ref.shape
    eye = jnp.where(
        rows_of((width, width)) == lax.broadcasted_iota(jnp.int32, (width, width), 1), 1.0, 0.0
    ).astype(bf16)
    own_ref[0:width, :] = dot_t(eye, attr_ref[...]).astype(bf16)
    upper, lower = halves(pos_ref[...])
    parts[...] = jnp.zeros_like(parts)
    parts[0:3, :] = upper
    parts[3:6, :] = lower
    own_ref[width : width + PARTS, :] = parts[...].astype(bf16)
    packed = own_ref[...]
    for rim in range(8):
        hot = one_hot(rim_ref[rim : rim + 1, :], atoms).astype(bf16)
        cell = dot(packed, hot).astype(bf16)
        for way, send in zip(directions, sends):
            for slot, (_, source) in enumerate(routes[way]):
                if source == rim:
                    send[:, slot * LANES : (slot + 1) * LANES] = cell


def slab_kernel(pos_ref, own_ref, zrows_ref, *rest):
    got, (inner_ref, send_ref, parts) = rest[:8], rest[8:]
    atoms = own_ref.shape[1]
    height = own_ref.shape[0]
    width = height - PARTS
    inner_len = inner_ref.shape[1]
    inner_ref[:, 0:atoms] = own_ref[...]
    parts[...] = jnp.zeros_like(parts)
    upper, lower = halves(pos_ref[...])
    parts[0:3, 0:atoms] = upper
    parts[3:6, 0:atoms] = lower
    for way, ref in zip(directions, got):
        for slot, (cycle, _) in enumerate(routes[way]):
            lanes = slice(slot * LANES, (slot + 1) * LANES)
            into = slice(atoms + cycle * LANES, atoms + (cycle + 1) * LANES)
            inner_ref[0:width, into] = ref[0:width, lanes]
            arrived = ref[width:height, lanes].astype(f32)
            joined = arrived[0:3] + arrived[3:6]
            axis = rows_of((3, LANES))
            shift = jnp.where(axis == 0, float(way[0]), jnp.where(axis == 1, float(way[1]), 0.0))
            upper, lower = halves(joined + shift)
            parts[0:3, into] = upper
            parts[3:6, into] = lower
    inner_ref[width:height, :] = parts[...].astype(bf16)
    hot = one_hot(zrows_ref[...], inner_len).astype(bf16)
    send_ref[...] = dot(inner_ref[...], hot).astype(bf16)


def embed_kernel(inner_ref, w_emb_ref, feat_ref, place_ref):
    width = w_emb_ref.shape[1]
    inner_len = inner_ref.shape[1]
    for first in range(0, inner_len, 512):
        raw = dot(w_emb_ref[...], inner_ref[0:width, first : first + 512])
        feat_ref[:, first : first + 512] = (raw * sigmoid(raw)).astype(bf16)
    parts = inner_ref[width:, :].astype(f32)
    place_ref[...] = jnp.zeros_like(place_ref)
    for high in range(inner_len // LANES):
        place_ref[0:6, high, :] = parts[0:6, high * LANES : (high + 1) * LANES]


def harmonic_rows(x, y, z):
    return [
        None,
        x,
        y,
        z,
        ROOT3 * x * y,
        ROOT3 * y * z,
        ROOT3 * z * x,
        0.5 * ROOT3 * (x * x - y * y),
        0.5 * (3.0 * z * z - 1.0),
    ]


def fold8(values):
    return jnp.sum(values.reshape(values.shape[0] // 8, 8, values.shape[1]), axis=0)


def edge_kernel(
    count_ref,
    lift_ref,
    centers_ref,
    others_ref,
    feat_in_ref,
    place_in_ref,
    slab_ref,
    w_emb_ref,
    w_rad_ref,
    w_chan_t_ref,
    w_chan_ref,
    w_lat_t_ref,
    w_ten_t_ref,
    w_back_ref,
    w_out_ref,
    w_rbf_ref,
    grad_ref,
    energy_ref,
    feat,
    place,
    hot,
    center_hot,
    low_o,
    low_c,
    latent_s,
    slope_s,
    chan_s,
    geo_s,
    dlat_s,
    dharm_s,
    tensor,
    tensor_b,
    dtensor,
    acc_o,
    acc_c,
):
    blocks, _, eb = centers_ref.shape
    width = w_emb_ref.shape[1]
    features = feat_in_ref.shape[0]
    inner_len = feat_in_ref.shape[1]
    table = inner_len + LANES
    highs = table // LANES
    atoms = tensor.shape[1]
    c_highs = atoms // LANES
    chans = w_chan_t_ref.shape[0]
    hpad = place_in_ref.shape[1]
    count = count_ref[0]

    feat[:, 0:inner_len] = feat_in_ref[...]
    raw = dot(w_emb_ref[...], slab_ref[0:width, :])
    feat[:, inner_len:table] = (raw * sigmoid(raw)).astype(bf16)
    feat[:, table : table + LANES] = w_rad_ref[...]
    place[...] = place_in_ref[...]
    arrived = slab_ref[width:, :].astype(f32)
    joined = arrived[0:3] + arrived[3:6]
    joined = joined + jnp.where(rows_of((3, LANES)) == 2, lift_ref[0], 0.0)
    upper, lower = halves(joined)
    place[0:3, highs - 1, :] = upper
    place[3:6, highs - 1, :] = lower
    hot[table:, :] = jnp.zeros((hot.shape[0] - table, eb), bf16)
    tensor[...] = jnp.zeros_like(tensor)
    dtensor[...] = jnp.zeros_like(dtensor)
    acc_o[...] = jnp.zeros_like(acc_o)
    acc_c[...] = jnp.zeros_like(acc_c)

    def first_pass(b, carry):
        c = centers_ref[b]
        o = others_ref[b]
        live = jnp.where(
            lax.broadcasted_iota(jnp.int32, (1, eb), 1) + b * eb < count, 1.0, 0.0
        )
        c_high = lax.shift_right_logical(c, 7)
        o_high = lax.shift_right_logical(o, 7)
        hot_c = one_hot(lax.bitwise_and(c, LANES - 1), LANES).astype(bf16)
        hot_o = one_hot(lax.bitwise_and(o, LANES - 1), LANES).astype(bf16)
        low_c[b] = hot_c
        low_o[b] = hot_o
        c_high16 = jnp.broadcast_to(c_high, (16, eb))
        o_high16 = jnp.broadcast_to(o_high, (16, eb))

        place_rows = place[...].reshape(6 * hpad, LANES).astype(bf16)
        picked = dot(place_rows, hot_o)
        picked = (picked[0 : 3 * hpad] + picked[3 * hpad :]).reshape(3, hpad, eb)
        po = jnp.sum(picked * one_hot(o_high, hpad)[None], axis=1)
        own_rows = place[:, 0:8, :].reshape(48, LANES).astype(bf16)
        picked = dot(own_rows, hot_c)
        picked = (picked[0:24] + picked[24:48]).reshape(3, 8, eb)
        pc = jnp.sum(picked * one_hot(c_high, 8)[None], axis=1)
        sep = po - pc
        rx, ry, rz = sep[0:1], sep[1:2], sep[2:3]
        squared = rx * rx + ry * ry + rz * rz
        inv_d = lax.rsqrt(squared + 0.25)
        dist = (squared + 0.25) * inv_d
        env = 1.0 / (1.0 + squared * squared * (1.0 / 16.0))
        x, y, z = rx * inv_d, ry * inv_d, rz * inv_d
        for row, value in enumerate((x, y, z, inv_d, dist, env, squared, live)):
            geo_s[b, row : row + 1, :] = value
        mu = 0.5 + 0.4 * rows_of((8, eb)).astype(f32)
        u = (dist - mu) * 2.0
        upper, lower = halves(jnp.exp(-(u * u)) * env)
        radial = jnp.concatenate([upper, lower], axis=0).astype(bf16)
        hot[table : table + 16, :] = radial
        hot[table + 16 : table + 32, :] = radial

        for high in range(highs):
            chunk = masked(hot_o, o_high16, high)
            if high < c_highs:
                own = masked(hot_c, c_high16, high)
                center_hot[b, high * LANES : (high + 1) * LANES, :] = own
                chunk = chunk + own
            hot[high * LANES : (high + 1) * LANES, :] = chunk

        mixed = dot(feat[...], hot[...])
        s = sigmoid(mixed)
        value = mixed * s
        latent = value.astype(bf16)
        latent_s[b] = latent
        slope_s[b] = (s + value * (1.0 - s)).astype(bf16)
        chan = dot(w_chan_t_ref[...], latent) * live
        chan_s[b] = chan
        harm = harmonic_rows(x, y, z)
        products = jnp.concatenate(
            [(chan if h is None else chan * h).astype(bf16) for h in harm], axis=0
        )
        tensor[...] += dot_t(products, center_hot[b])
        return carry

    lax.fori_loop(0, blocks, first_pass, 0)
    tensor_b[...] = (0.125 * tensor[...]).astype(bf16)

    def second_pass(b, carry):
        geo = geo_s[b]
        x, y, z = geo[0:1], geo[1:2], geo[2:3]
        env, live = geo[5:6], geo[7:8]
        harm = harmonic_rows(x, y, z)
        gathered = dot(tensor_b[...], center_hot[b])
        parts = [gathered[m * chans : (m + 1) * chans] for m in range(9)]
        bands = [parts[0], None, None]
        for m in range(1, 9):
            term = parts[m] * harm[m]
            band = BANDS[m]
            bands[band] = term if bands[band] is None else bands[band] + term
        invariant = jnp.concatenate([band.astype(bf16) for band in bands], axis=0)
        pre = dot(w_lat_t_ref[...], latent_s[b]) + dot(w_ten_t_ref[...], invariant)
        s = sigmoid(pre)
        value = pre * s
        weight = w_out_ref[...]
        summed = jnp.sum(value * weight, axis=0, keepdims=True)
        geo_s[b, 8:9, :] = summed
        dpre = (weight * (env * live) * (s + value * (1.0 - s))).astype(bf16)
        back = dot(w_back_ref[...], dpre)
        dlat_s[b] = back[0:features].astype(bf16)
        dbands = [
            back[features + band * chans : features + (band + 1) * chans] for band in range(3)
        ]
        products = jnp.concatenate(
            [
                (dbands[BANDS[m]] if harm[m] is None else dbands[BANDS[m]] * harm[m]).astype(bf16)
                for m in range(9)
            ],
            axis=0,
        )
        dtensor[...] += dot_t(products, center_hot[b])
        for m in range(1, 9):
            dharm_s[b, (m - 1) * 8 : m * 8, :] = fold8(dbands[BANDS[m]] * parts[m])
        return carry

    lax.fori_loop(0, blocks, second_pass, 0)
    tensor_b[...] = (0.125 * dtensor[...]).astype(bf16)

    def third_pass(b, carry):
        geo = geo_s[b]
        x, y, z = geo[0:1], geo[1:2], geo[2:3]
        inv_d, dist, env, squared = geo[3:4], geo[4:5], geo[5:6], geo[6:7]
        live, summed = geo[7:8], geo[8:9]
        harm = harmonic_rows(x, y, z)
        gathered = dot(tensor_b[...], center_hot[b])
        chan = chan_s[b]
        dchan = gathered[0:chans]
        dh = [None]
        for m in range(1, 9):
            part = gathered[m * chans : (m + 1) * chans]
            dchan = dchan + part * harm[m]
            total = dharm_s[b, (m - 1) * 8 : m * 8, :] + fold8(part * chan)
            dh.append(jnp.sum(total, axis=0, keepdims=True))
        dchan = (dchan * live).astype(bf16)
        dlat = dlat_s[b].astype(f32) + dot(w_chan_ref[...], dchan)
        dmixed = (dlat * slope_s[b].astype(f32)).astype(bf16)
        drad = dot(w_rbf_ref[...], dmixed)
        drad = drad[0:8] + drad[8:16]
        mu = 0.5 + 0.4 * rows_of((8, eb)).astype(f32)
        u = (dist - mu) * 2.0
        weighted = drad * jnp.exp(-(u * u))
        denv = jnp.sum(weighted, axis=0, keepdims=True) + live * summed
        ddist = -4.0 * env * jnp.sum(weighted * u, axis=0, keepdims=True)
        dx = dh[1] + ROOT3 * (y * dh[4] + z * dh[6] + x * dh[7])
        dy = dh[2] + ROOT3 * (x * dh[4] + z * dh[5] - y * dh[7])
        dz = dh[3] + ROOT3 * (y * dh[5] + x * dh[6]) + 3.0 * z * dh[8]
        ddist = ddist - (dx * x + dy * y + dz * z) * inv_d
        dsq = denv * (env * env * squared * -0.125) + ddist * (0.5 * inv_d)
        both = 2.0 * dsq * dist
        gs = [dx * inv_d + both * x, dy * inv_d + both * y, dz * inv_d + both * z]
        energy = summed * env * live

        c_high = lax.shift_right_logical(centers_ref[b], 7)
        o_high = lax.shift_right_logical(others_ref[b], 7)
        mask_o = one_hot(o_high, hpad)
        mask_c = one_hot(c_high, 8)
        split = [halves(g) for g in gs]
        rows_o = jnp.concatenate(
            [mask_o * split[d][part] for part in range(2) for d in range(3)], axis=0
        ).astype(bf16)
        split.append(halves(energy))
        rows_c = jnp.concatenate(
            [mask_c * split[d][part] for part in range(2) for d in range(4)], axis=0
        ).astype(bf16)
        acc_o[...] += dot_t(rows_o, low_o[b])
        acc_c[...] += dot_t(rows_c, low_c[b])
        return carry

    lax.fori_loop(0, blocks, third_pass, 0)
    sum_o = acc_o[0 : 3 * hpad, :] + acc_o[3 * hpad :, :]
    sum_c = acc_c[0:32, :] + acc_c[32:64, :]
    for d in range(3):
        grad_ref[d] = sum_o[d * hpad : (d + 1) * hpad]
        grad_ref[d, 0:8, :] = sum_o[d * hpad : d * hpad + 8] - sum_c[d * 8 : (d + 1) * 8]
    energy_ref[...] = sum_c[24:32]


def return_kernel(grad_ref, back_ref, zrows_ref, own_ref, *sends):
    hpad = grad_ref.shape[1]
    z_rows = zrows_ref[...]
    mask = one_hot(lax.shift_right_logical(z_rows, 7), hpad)
    low = one_hot(lax.bitwise_and(z_rows, LANES - 1), LANES).astype(bf16)
    pieces = [halves(back_ref[d : d + 1, :]) for d in range(3)]
    rows = jnp.concatenate(
        [mask * pieces[d][part] for part in range(2) for d in range(3)], axis=0
    ).astype(bf16)
    landed = dot_t(rows, low)
    landed = landed[0 : 3 * hpad] + landed[3 * hpad :]
    base = own_ref.shape[1] // 2
    for d in range(3):
        total = grad_ref[d] + landed[d * hpad : (d + 1) * hpad]
        own_ref[d] = total[0:8]
        for way, send in zip(directions, sends):
            for slot, (cycle, _) in enumerate(routes[way]):
                row = base + cycle
                send[slot * 3 + d : slot * 3 + d + 1, :] = total[row : row + 1]


def force_kernel(own_ref, rim_ref, *rest):
    got, (out_ref, rim_sum) = rest[:8], rest[8:]
    rim_sum[...] = jnp.zeros_like(rim_sum)
    for way, ref in zip(directions, got):
        for slot, (_, rim) in enumerate(routes[way]):
            rim_sum[rim, 0:3, :] += ref[slot * 3 : slot * 3 + 3, :]
    total = jnp.zeros((48, LANES), f32)
    for rim in range(8):
        index = rim_ref[rim : rim + 1, :]
        mask = one_hot(lax.shift_right_logical(index, 7), 8)
        low = one_hot(lax.bitwise_and(index, LANES - 1), LANES).astype(bf16)
        values = rim_sum[rim]
        pieces = [halves(values[d : d + 1, :]) for d in range(3)]
        rows = jnp.concatenate(
            [mask * pieces[d][part] for part in range(2) for d in range(3)], axis=0
        ).astype(bf16)
        total = total + dot_t(rows, low)
    total = total[0:24] + total[24:48]
    for d in range(3):
        for high in range(out_ref.shape[1] // LANES):
            value = own_ref[d, high : high + 1, :] + total[d * 8 + high : d * 8 + high + 1, :]
            out_ref[d : d + 1, high * LANES : (high + 1) * LANES] = -value


def call(kernel, out_shape, args, scratch=(), smem=0, limit=None):
    vmem = pl.BlockSpec(memory_space=pltpu.VMEM)
    scalar = pl.BlockSpec(memory_space=pltpu.SMEM)
    return pl.pallas_call(
        kernel,
        out_shape=out_shape,
        in_specs=[scalar] * smem + [vmem] * (len(args) - smem),
        out_specs=jax.tree.map(lambda _: vmem, out_shape),
        scratch_shapes=list(scratch),
        compiler_params=pltpu.CompilerParams(vmem_limit_bytes=limit),
    )(*args)


def shifted(x, way):
    nx, ny = lax.axis_size("gx"), lax.axis_size("gy")
    pairs = [
        (((i + way[0]) % nx) * ny + (j + way[1]) % ny, i * ny + j)
        for i in range(nx)
        for j in range(ny)
    ]
    return lax.ppermute(x, ("gx", "gy"), pairs)


def swapped(x):
    count = lax.axis_size("gz")
    return lax.ppermute(x, "gz", [(i, i ^ 1) for i in range(count)])


def per_device(
    positions,
    attributes,
    edge_center,
    edge_other,
    edge_count,
    rim_rows,
    z_rows,
    w_emb,
    w_rbf,
    w_chan,
    w_lat,
    w_ten,
    w_out,
):
    pos = positions[0, 0, 0]
    attr = attributes[0, 0, 0]
    rim = rim_rows[0, 0, 0]
    zr = z_rows[0, 0]
    count = edge_count[0, 0]
    atoms, width = attr.shape
    edges = edge_center.shape[-1]
    features = w_emb.shape[1]
    chans = w_chan.shape[1]
    height = width + PARTS
    inner_len = atoms + 16 * LANES
    table = inner_len + LANES
    hpad = -(-(table // LANES) // 8) * 8
    eb = 512 if edges % 512 == 0 else LANES
    blocks = edges // eb
    centers = edge_center.reshape(blocks, 1, eb)
    others = edge_other.reshape(blocks, 1, eb)
    lift = (1 - 2 * lax.axis_index("gz")).astype(f32).reshape(1)
    big = 60 * 1024 * 1024

    w_emb_t = w_emb.T
    rbf_hi = w_rbf.astype(bf16)
    rbf_lo = (w_rbf - rbf_hi.astype(f32)).astype(bf16)
    w_rad = jnp.concatenate(
        [rbf_hi, rbf_hi, rbf_lo, rbf_lo, jnp.zeros((LANES - 32, features), bf16)], axis=0
    ).T
    w_rbf2 = jnp.concatenate([rbf_hi, rbf_lo], axis=0)
    w_back = jnp.concatenate([w_lat, w_ten], axis=0)
    w_out_col = w_out[:, None]

    shape = jax.ShapeDtypeStruct
    sends = tuple(shape((height, len(routes[way]) * LANES), bf16) for way in directions)
    own, *sent = call(
        pack_kernel,
        (shape((height, atoms), bf16),) + sends,
        (pos, attr, rim),
        [pltpu.VMEM((PARTS, atoms), f32)],
    )
    got = [shifted(x, way) for x, way in zip(sent, directions)]
    inner, slab_send = call(
        slab_kernel,
        (shape((height, inner_len), bf16), shape((height, LANES), bf16)),
        (pos, own, zr, *got),
        [pltpu.VMEM((PARTS, inner_len), f32)],
    )
    slab_got = swapped(slab_send)
    feat, place = call(
        embed_kernel,
        (shape((features, inner_len), bf16), shape((6, hpad, LANES), f32)),
        (inner, w_emb_t),
    )
    grads, energy = call(
        edge_kernel,
        (shape((3, hpad, LANES), f32), shape((8, LANES), f32)),
        (
            count,
            lift,
            centers,
            others,
            feat,
            place,
            slab_got,
            w_emb_t,
            w_rad,
            w_chan.T,
            w_chan,
            w_lat.T,
            w_ten.T,
            w_back,
            w_out_col,
            w_rbf2,
        ),
        [
            pltpu.VMEM((features, table + LANES), bf16),
            pltpu.VMEM((6, hpad, LANES), f32),
            pltpu.VMEM((table + LANES, eb), bf16),
            pltpu.VMEM((blocks, atoms, eb), bf16),
            pltpu.VMEM((blocks, LANES, eb), bf16),
            pltpu.VMEM((blocks, LANES, eb), bf16),
            pltpu.VMEM((blocks, features, eb), bf16),
            pltpu.VMEM((blocks, features, eb), bf16),
            pltpu.VMEM((blocks, chans, eb), f32),
            pltpu.VMEM((blocks, 16, eb), f32),
            pltpu.VMEM((blocks, features, eb), bf16),
            pltpu.VMEM((blocks, 64, eb), f32),
            pltpu.VMEM((9 * chans, atoms), f32),
            pltpu.VMEM((9 * chans, atoms), bf16),
            pltpu.VMEM((9 * chans, atoms), f32),
            pltpu.VMEM((6 * hpad, LANES), f32),
            pltpu.VMEM((64, LANES), f32),
        ],
        smem=2,
        limit=big,
    )
    slab_back = swapped(grads[:, table // LANES - 1])
    messages = tuple(shape((3 * len(routes[way]), LANES), f32) for way in directions)
    own_grad, *sent = call(
        return_kernel,
        (shape((3, 8, LANES), f32),) + messages,
        (grads, slab_back, zr),
    )
    got = [shifted(x, (-way[0], -way[1])) for x, way in zip(sent, directions)]
    forces = call(
        force_kernel,
        shape((3, atoms), f32),
        (own_grad, rim, *got),
        [pltpu.VMEM((8, 8, LANES), f32)],
    )
    atom_energy = energy[0 : atoms // LANES].reshape(1, 1, 1, atoms)
    return (atom_energy, forces[None, None, None])


def solution(mesh):
    return jax.shard_map(
        per_device,
        mesh=mesh,
        in_specs=(
            P("gx", "gy", "gz", None, None),
            P("gx", "gy", "gz", None, None),
            P("gx", "gy", "gz", None),
            P("gx", "gy", "gz", None),
            P("gx", "gy", "gz"),
            P("gx", "gy", "gz", None, None),
            P("gx", "gy", "gz", None),
            P(),
            P(),
            P(),
            P(),
            P(),
            P(),
        ),
        out_specs=(P("gx", "gy", "gz", None), P("gx", "gy", "gz", None, None)),
        check_vma=False,
    )
```

```python
import jax
import jax.numpy as jnp
from jax import lax
from jax.experimental import pallas as pl
from jax.experimental.pallas import tpu as pltpu
from jax.sharding import PartitionSpec as P

f32 = jnp.float32
bf16 = jnp.bfloat16
LANES = 128
PARTS = 16
ROOT3 = 3.0**0.5
BANDS = (0, 1, 1, 1, 2, 2, 2, 2, 2)

rim_cells = [(0, 0), (0, 1), (0, 2), (1, 0), (1, 2), (2, 0), (2, 1), (2, 2)]
cycle_cells = [(p, q) for p in range(5) for q in range(5) if p in (0, 4) or q in (0, 4)]


def source_of(position):
    if position == 0:
        return (-1, 2)
    if position == 4:
        return (1, 0)
    return (0, position - 1)


routes = {}
for _cycle, (_p, _q) in enumerate(cycle_cells):
    (_sx, _a), (_sy, _b) = source_of(_p), source_of(_q)
    routes.setdefault((_sx, _sy), []).append((_cycle, rim_cells.index((_a, _b))))
sides = [(0, -1), (0, 1), (-1, 0), (1, 0)]


def dot(a, b):
    return lax.dot_general(a, b, (((1,), (0,)), ((), ())), preferred_element_type=f32)


def dot_t(a, b):
    return lax.dot_general(a, b, (((1,), (1,)), ((), ())), preferred_element_type=f32)


def rows_of(shape):
    return lax.broadcasted_iota(jnp.int32, shape, 0)


def one_hot(index, size):
    return jnp.where(rows_of((size, index.shape[1])) == index, 1.0, 0.0)


def halves(values):
    upper = values.astype(bf16).astype(f32)
    return upper, values - upper


def masked(hot_low, high16, value):
    mask = jnp.where(high16 == value, 1.0, 0.0).astype(bf16)
    size, lanes = hot_low.shape
    return (hot_low.reshape(size // 16, 16, lanes) * mask[None]).reshape(size, lanes)


def sigmoid(x):
    return 0.5 * jnp.tanh(0.5 * x) + 0.5


def pack_kernel(pos_ref, attr_ref, rim_ref, own_ref, *rest):
    sends, parts = rest[:-1], rest[-1]
    atoms, width = attr_ref.shape
    eye = jnp.where(
        rows_of((width, width)) == lax.broadcasted_iota(jnp.int32, (width, width), 1), 1.0, 0.0
    ).astype(bf16)
    own_ref[0:width, :] = dot_t(eye, attr_ref[...]).astype(bf16)
    parts[...] = jnp.zeros_like(parts)
    for d in range(3):
        parts[d : d + 1, :], parts[3 + d : 4 + d, :] = halves(pos_ref[d])
    own_ref[width : width + PARTS, :] = parts[...].astype(bf16)
    packed = own_ref[...]
    for rim in range(8):
        hot = one_hot(rim_ref[rim : rim + 1, :], atoms).astype(bf16)
        cell = dot(packed, hot).astype(bf16)
        for way, send in zip(sides, sends):
            for slot, (_, source) in enumerate(routes[way]):
                if source == rim:
                    send[:, slot * LANES : (slot + 1) * LANES] = cell


def corner_kernel(minus_ref, plus_ref, to_plus_ref, to_minus_ref):
    first, last = slice(0, LANES), slice(2 * LANES, 3 * LANES)
    for slot, ref in enumerate((minus_ref, plus_ref)):
        lanes = slice(slot * LANES, (slot + 1) * LANES)
        to_plus_ref[:, lanes] = ref[:, last]
        to_minus_ref[:, lanes] = ref[:, first]


def slab_kernel(pos_ref, own_ref, zrows_ref, *rest):
    got, corners, (inner_ref, send_ref, parts) = rest[:4], rest[4:6], rest[6:]
    atoms = own_ref.shape[1]
    height = own_ref.shape[0]
    width = height - PARTS
    inner_len = inner_ref.shape[1]
    inner_ref[:, 0:atoms] = own_ref[...]
    parts[...] = jnp.zeros_like(parts)
    for d in range(3):
        parts[d : d + 1, 0:atoms], parts[3 + d : 4 + d, 0:atoms] = halves(pos_ref[d])
    arrivals = []
    for way, ref in zip(sides, got):
        for slot, (cycle, _) in enumerate(routes[way]):
            arrivals.append((way, ref, slot, cycle))
    for sx, ref in zip((-1, 1), corners):
        for slot, sy in enumerate((-1, 1)):
            arrivals.append(((sx, sy), ref, slot, routes[(sx, sy)][0][0]))
    for way, ref, slot, cycle in arrivals:
        lanes = slice(slot * LANES, (slot + 1) * LANES)
        into = slice(atoms + cycle * LANES, atoms + (cycle + 1) * LANES)
        inner_ref[0:width, into] = ref[0:width, lanes]
        arrived = ref[width:height, lanes].astype(f32)
        joined = arrived[0:3] + arrived[3:6]
        axis = rows_of((3, LANES))
        shift = jnp.where(axis == 0, float(way[0]), jnp.where(axis == 1, float(way[1]), 0.0))
        upper, lower = halves(joined + shift)
        parts[0:3, into] = upper
        parts[3:6, into] = lower
    inner_ref[width:height, :] = parts[...].astype(bf16)
    hot = one_hot(zrows_ref[...], inner_len).astype(bf16)
    send_ref[...] = dot(inner_ref[...], hot).astype(bf16)


def unit(size):
    lanes = lax.broadcasted_iota(jnp.int32, (size, size), 1)
    return jnp.where(rows_of((size, size)) == lanes, 1.0, 0.0)


def weights_kernel(
    w_emb_ref,
    w_rbf_ref,
    w_chan_t_ref,
    w_lat_ref,
    w_ten_ref,
    w_out_ref,
    emb_t_ref,
    rad_ref,
    chan_ref,
    lat_t_ref,
    ten_t_ref,
    back_ref,
    out_ref,
    rbf_ref,
    scratch,
):
    features = w_lat_ref.shape[0]
    eye = unit(features)
    eye_b = eye.astype(bf16)
    emb_t_ref[...] = dot_t(eye_b, w_emb_ref[...]).astype(bf16)
    chan_ref[...] = dot_t(eye_b, w_chan_t_ref[...]).astype(bf16)
    lat_t_ref[...] = dot_t(eye_b, w_lat_ref[...]).astype(bf16)
    ten_t_ref[...] = dot_t(eye_b, w_ten_ref[...]).astype(bf16)
    back_ref[0:features, :] = w_lat_ref[...]
    back_ref[features:, :] = w_ten_ref[...]
    column = jnp.sum(eye * w_out_ref[...], axis=1, keepdims=True)
    out_ref[...] = jnp.broadcast_to(column, out_ref.shape)
    upper, lower = halves(w_rbf_ref[...])
    rbf_ref[...] = jnp.concatenate([upper, lower], axis=0).astype(bf16)
    scratch[...] = jnp.zeros_like(scratch)
    for start, value in ((0, upper), (8, upper), (16, lower), (24, lower)):
        scratch[start : start + 8, :] = value
    rad_ref[...] = dot_t(eye_b, scratch[...].astype(bf16)).astype(bf16)


def embed_kernel(inner_ref, w_emb_ref, feat_ref, place_ref):
    width = w_emb_ref.shape[1]
    inner_len = inner_ref.shape[1]
    for first in range(0, inner_len, 512):
        raw = dot(w_emb_ref[...], inner_ref[0:width, first : first + 512])
        feat_ref[:, first : first + 512] = (raw * sigmoid(raw)).astype(bf16)
    parts = inner_ref[width:, :].astype(f32)
    place_ref[...] = jnp.zeros_like(place_ref)
    for high in range(inner_len // LANES):
        place_ref[0:6, high, :] = parts[0:6, high * LANES : (high + 1) * LANES]


def harmonic_rows(x, y, z):
    return [
        None,
        x,
        y,
        z,
        ROOT3 * x * y,
        ROOT3 * y * z,
        ROOT3 * z * x,
        0.5 * ROOT3 * (x * x - y * y),
        0.5 * (3.0 * z * z - 1.0),
    ]


def fold8(values):
    return jnp.sum(values.reshape(values.shape[0] // 8, 8, values.shape[1]), axis=0)


def edge_kernel(
    count_ref,
    lift_ref,
    centers_ref,
    others_ref,
    feat_in_ref,
    place_in_ref,
    slab_ref,
    w_emb_ref,
    w_rad_ref,
    w_chan_t_ref,
    w_chan_ref,
    w_lat_t_ref,
    w_ten_t_ref,
    w_back_ref,
    w_out_ref,
    w_rbf_ref,
    grad_ref,
    slab_grad_ref,
    energy_ref,
    feat,
    place,
    hot,
    center_hot,
    low_o,
    low_c,
    latent_s,
    slope_s,
    chan_s,
    geo_s,
    dlat_s,
    dharm_s,
    tensor,
    tensor_b,
    dtensor,
    acc_o,
    acc_c,
):
    blocks, _, eb = centers_ref.shape
    width = w_emb_ref.shape[1]
    features = feat_in_ref.shape[0]
    inner_len = feat_in_ref.shape[1]
    table = inner_len + LANES
    highs = table // LANES
    atoms = tensor.shape[1]
    c_highs = atoms // LANES
    chans = w_chan_t_ref.shape[0]
    hpad = place_in_ref.shape[1]
    count = count_ref[0]

    feat[:, 0:inner_len] = feat_in_ref[...]
    raw = dot(w_emb_ref[...], slab_ref[0:width, :])
    feat[:, inner_len:table] = (raw * sigmoid(raw)).astype(bf16)
    feat[:, table : table + LANES] = w_rad_ref[...]
    place[...] = place_in_ref[...]
    arrived = slab_ref[width:, :].astype(f32)
    joined = arrived[0:3] + arrived[3:6]
    joined = joined + jnp.where(rows_of((3, LANES)) == 2, lift_ref[0], 0.0)
    upper, lower = halves(joined)
    place[0:3, highs - 1, :] = upper
    place[3:6, highs - 1, :] = lower
    hot[table:, :] = jnp.zeros((hot.shape[0] - table, eb), bf16)
    tensor[...] = jnp.zeros_like(tensor)
    dtensor[...] = jnp.zeros_like(dtensor)
    acc_o[...] = jnp.zeros_like(acc_o)
    acc_c[...] = jnp.zeros_like(acc_c)

    def first_pass(b, carry):
        c = centers_ref[b]
        o = others_ref[b]
        live = jnp.where(
            lax.broadcasted_iota(jnp.int32, (1, eb), 1) + b * eb < count, 1.0, 0.0
        )
        c_high = lax.shift_right_logical(c, 7)
        o_high = lax.shift_right_logical(o, 7)
        hot_c = one_hot(lax.bitwise_and(c, LANES - 1), LANES).astype(bf16)
        hot_o = one_hot(lax.bitwise_and(o, LANES - 1), LANES).astype(bf16)
        low_c[b] = hot_c
        low_o[b] = hot_o
        c_high16 = jnp.broadcast_to(c_high, (16, eb))
        o_high16 = jnp.broadcast_to(o_high, (16, eb))

        place_rows = place[...].reshape(6 * hpad, LANES).astype(bf16)
        picked = dot(place_rows, hot_o)
        picked = (picked[0 : 3 * hpad] + picked[3 * hpad :]).reshape(3, hpad, eb)
        po = jnp.sum(picked * one_hot(o_high, hpad)[None], axis=1)
        own_rows = place[:, 0:8, :].reshape(48, LANES).astype(bf16)
        picked = dot(own_rows, hot_c)
        picked = (picked[0:24] + picked[24:48]).reshape(3, 8, eb)
        pc = jnp.sum(picked * one_hot(c_high, 8)[None], axis=1)
        sep = po - pc
        rx, ry, rz = sep[0:1], sep[1:2], sep[2:3]
        squared = rx * rx + ry * ry + rz * rz
        inv_d = lax.rsqrt(squared + 0.25)
        dist = (squared + 0.25) * inv_d
        env = 1.0 / (1.0 + squared * squared * (1.0 / 16.0))
        x, y, z = rx * inv_d, ry * inv_d, rz * inv_d
        for row, value in enumerate((x, y, z, inv_d, dist, env, squared, live)):
            geo_s[b, row : row + 1, :] = value
        mu = 0.5 + 0.4 * rows_of((8, eb)).astype(f32)
        u = (dist - mu) * 2.0
        upper, lower = halves(jnp.exp(-(u * u)) * env)
        radial = jnp.concatenate([upper, lower], axis=0).astype(bf16)
        hot[table : table + 16, :] = radial
        hot[table + 16 : table + 32, :] = radial

        for high in range(highs):
            chunk = masked(hot_o, o_high16, high)
            if high < c_highs:
                own = masked(hot_c, c_high16, high)
                center_hot[b, high * LANES : (high + 1) * LANES, :] = own
                chunk = chunk + own
            hot[high * LANES : (high + 1) * LANES, :] = chunk

        mixed = dot(feat[...], hot[...])
        s = sigmoid(mixed)
        value = mixed * s
        latent = value.astype(bf16)
        latent_s[b] = latent
        slope_s[b] = (s + value * (1.0 - s)).astype(bf16)
        chan = dot(w_chan_t_ref[...], latent) * live
        chan_s[b] = chan
        harm = harmonic_rows(x, y, z)
        products = jnp.concatenate(
            [(chan if h is None else chan * h).astype(bf16) for h in harm], axis=0
        )
        tensor[...] += dot_t(products, center_hot[b])
        return carry

    lax.fori_loop(0, blocks, first_pass, 0)
    tensor_b[...] = (0.125 * tensor[...]).astype(bf16)

    def second_pass(b, carry):
        geo = geo_s[b]
        x, y, z = geo[0:1], geo[1:2], geo[2:3]
        env, live = geo[5:6], geo[7:8]
        harm = harmonic_rows(x, y, z)
        gathered = dot(tensor_b[...], center_hot[b])
        parts = [gathered[m * chans : (m + 1) * chans] for m in range(9)]
        bands = [parts[0], None, None]
        for m in range(1, 9):
            term = parts[m] * harm[m]
            band = BANDS[m]
            bands[band] = term if bands[band] is None else bands[band] + term
        invariant = jnp.concatenate([band.astype(bf16) for band in bands], axis=0)
        pre = dot(w_lat_t_ref[...], latent_s[b]) + dot(w_ten_t_ref[...], invariant)
        s = sigmoid(pre)
        value = pre * s
        weight = jnp.concatenate([w_out_ref[...]] * (eb // LANES), axis=1)
        summed = jnp.sum(value * weight, axis=0, keepdims=True)
        geo_s[b, 8:9, :] = summed
        dpre = (weight * (env * live) * (s + value * (1.0 - s))).astype(bf16)
        back = dot(w_back_ref[...], dpre)
        dlat_s[b] = back[0:features].astype(bf16)
        dbands = [
            back[features + band * chans : features + (band + 1) * chans] for band in range(3)
        ]
        products = jnp.concatenate(
            [
                (dbands[BANDS[m]] if harm[m] is None else dbands[BANDS[m]] * harm[m]).astype(bf16)
                for m in range(9)
            ],
            axis=0,
        )
        dtensor[...] += dot_t(products, center_hot[b])
        for m in range(1, 9):
            dharm_s[b, (m - 1) * 8 : m * 8, :] = fold8(dbands[BANDS[m]] * parts[m])
        return carry

    lax.fori_loop(0, blocks, second_pass, 0)
    tensor_b[...] = (0.125 * dtensor[...]).astype(bf16)

    def third_pass(b, carry):
        geo = geo_s[b]
        x, y, z = geo[0:1], geo[1:2], geo[2:3]
        inv_d, dist, env, squared = geo[3:4], geo[4:5], geo[5:6], geo[6:7]
        live, summed = geo[7:8], geo[8:9]
        harm = harmonic_rows(x, y, z)
        gathered = dot(tensor_b[...], center_hot[b])
        chan = chan_s[b]
        dchan = gathered[0:chans]
        dh = [None]
        for m in range(1, 9):
            part = gathered[m * chans : (m + 1) * chans]
            dchan = dchan + part * harm[m]
            total = dharm_s[b, (m - 1) * 8 : m * 8, :] + fold8(part * chan)
            dh.append(jnp.sum(total, axis=0, keepdims=True))
        dchan = (dchan * live).astype(bf16)
        dlat = dlat_s[b].astype(f32) + dot(w_chan_ref[...], dchan)
        dmixed = (dlat * slope_s[b].astype(f32)).astype(bf16)
        drad = dot(w_rbf_ref[...], dmixed)
        drad = drad[0:8] + drad[8:16]
        mu = 0.5 + 0.4 * rows_of((8, eb)).astype(f32)
        u = (dist - mu) * 2.0
        weighted = drad * jnp.exp(-(u * u))
        denv = jnp.sum(weighted, axis=0, keepdims=True) + live * summed
        ddist = -4.0 * env * jnp.sum(weighted * u, axis=0, keepdims=True)
        dx = dh[1] + ROOT3 * (y * dh[4] + z * dh[6] + x * dh[7])
        dy = dh[2] + ROOT3 * (x * dh[4] + z * dh[5] - y * dh[7])
        dz = dh[3] + ROOT3 * (y * dh[5] + x * dh[6]) + 3.0 * z * dh[8]
        ddist = ddist - (dx * x + dy * y + dz * z) * inv_d
        dsq = denv * (env * env * squared * -0.125) + ddist * (0.5 * inv_d)
        both = 2.0 * dsq * dist
        gs = [dx * inv_d + both * x, dy * inv_d + both * y, dz * inv_d + both * z]
        energy = summed * env * live

        c_high = lax.shift_right_logical(centers_ref[b], 7)
        o_high = lax.shift_right_logical(others_ref[b], 7)
        mask_o = one_hot(o_high, hpad)
        mask_c = one_hot(c_high, 8)
        split = [halves(g) for g in gs]
        rows_o = jnp.concatenate(
            [mask_o * split[d][part] for part in range(2) for d in range(3)], axis=0
        ).astype(bf16)
        split.append(halves(energy))
        rows_c = jnp.concatenate(
            [mask_c * split[d][part] for part in range(2) for d in range(4)], axis=0
        ).astype(bf16)
        acc_o[...] += dot_t(rows_o, low_o[b])
        acc_c[...] += dot_t(rows_c, low_c[b])
        return carry

    lax.fori_loop(0, blocks, third_pass, 0)
    sum_o = acc_o[0 : 3 * hpad, :] + acc_o[3 * hpad :, :]
    sum_c = acc_c[0:32, :] + acc_c[32:64, :]
    for d in range(3):
        grad_ref[d] = sum_o[d * hpad : (d + 1) * hpad]
        grad_ref[d, 0:8, :] = sum_o[d * hpad : d * hpad + 8] - sum_c[d * 8 : (d + 1) * 8]
        slab_grad_ref[d : d + 1, :] = sum_o[d * hpad + highs - 1 : d * hpad + highs]
    for high in range(c_highs):
        lanes = slice(high * LANES, (high + 1) * LANES)
        energy_ref[:, lanes] = sum_c[24 + high : 25 + high]


def return_kernel(grad_ref, back_ref, zrows_ref, own_ref, to_xm_ref, to_xp_ref, to_ym_ref, to_yp_ref):
    hpad = grad_ref.shape[1]
    z_rows = zrows_ref[...]
    mask = one_hot(lax.shift_right_logical(z_rows, 7), hpad)
    low = one_hot(lax.bitwise_and(z_rows, LANES - 1), LANES).astype(bf16)
    pieces = [halves(back_ref[d : d + 1, :]) for d in range(3)]
    rows = jnp.concatenate(
        [mask * pieces[d][part] for part in range(2) for d in range(3)], axis=0
    ).astype(bf16)
    landed = dot_t(rows, low)
    landed = landed[0 : 3 * hpad] + landed[3 * hpad :]
    base = own_ref.shape[1] // 2
    for d in range(3):
        total = grad_ref[d] + landed[d * hpad : (d + 1) * hpad]
        own_ref[d] = total[0:8]
        for cycle, (p, q) in enumerate(cycle_cells):
            value = total[base + cycle : base + cycle + 1]
            if p in (0, 4):
                ref = to_xm_ref if p == 0 else to_xp_ref
                ref[q * 3 + d : q * 3 + d + 1, :] = value
            else:
                ref = to_ym_ref if q == 0 else to_yp_ref
                ref[(p - 1) * 3 + d : (p - 1) * 3 + d + 1, :] = value


def turn_kernel(from_xp_ref, from_xm_ref, to_ym_ref, to_yp_ref, send_ym_ref, send_yp_ref):
    for q, old, new in ((0, to_ym_ref, send_ym_ref), (4, to_yp_ref, send_yp_ref)):
        new[0:3, :] = old[0:3, :] + from_xm_ref[q * 3 : q * 3 + 3, :]
        new[3:6, :] = old[3:6, :]
        new[6:9, :] = old[6:9, :] + from_xp_ref[q * 3 : q * 3 + 3, :]


def force_kernel(
    own_ref, rim_ref, from_xp_ref, from_xm_ref, from_yp_ref, from_ym_ref, out_ref, rim_sum
):
    rim_sum[...] = jnp.zeros_like(rim_sum)
    for a, ref in ((2, from_xp_ref), (0, from_xm_ref)):
        for b in range(3):
            rim_sum[rim_cells.index((a, b)), 0:3, :] += ref[(b + 1) * 3 : (b + 2) * 3, :]
    for b, ref in ((2, from_yp_ref), (0, from_ym_ref)):
        for a in range(3):
            rim_sum[rim_cells.index((a, b)), 0:3, :] += ref[a * 3 : (a + 1) * 3, :]
    total = jnp.zeros((48, LANES), f32)
    for rim in range(8):
        index = rim_ref[rim : rim + 1, :]
        mask = one_hot(lax.shift_right_logical(index, 7), 8)
        low = one_hot(lax.bitwise_and(index, LANES - 1), LANES).astype(bf16)
        values = rim_sum[rim]
        pieces = [halves(values[d : d + 1, :]) for d in range(3)]
        rows = jnp.concatenate(
            [mask * pieces[d][part] for part in range(2) for d in range(3)], axis=0
        ).astype(bf16)
        total = total + dot_t(rows, low)
    total = total[0:24] + total[24:48]
    for d in range(3):
        for high in range(out_ref.shape[2] // LANES):
            value = own_ref[d, high : high + 1, :] + total[d * 8 + high : d * 8 + high + 1, :]
            out_ref[d, :, high * LANES : (high + 1) * LANES] = -value


def call(kernel, out_shape, args, scratch=(), smem=0, limit=None):
    vmem = pl.BlockSpec(memory_space=pltpu.VMEM)
    scalar = pl.BlockSpec(memory_space=pltpu.SMEM)
    return pl.pallas_call(
        kernel,
        out_shape=out_shape,
        in_specs=[scalar] * smem + [vmem] * (len(args) - smem),
        out_specs=jax.tree.map(lambda _: vmem, out_shape),
        scratch_shapes=list(scratch),
        compiler_params=pltpu.CompilerParams(vmem_limit_bytes=limit),
    )(*args)


def shifted(x, axis, step):
    count = lax.axis_size(axis)
    return lax.ppermute(x, axis, [((i + step) % count, i) for i in range(count)])


def swapped(x):
    count = lax.axis_size("gz")
    return lax.ppermute(x, "gz", [(i, i ^ 1) for i in range(count)])


def per_device(
    positions,
    attributes,
    edge_center,
    edge_other,
    edge_count,
    rim_rows,
    z_rows,
    w_emb,
    w_rbf,
    w_chan,
    w_lat,
    w_ten,
    w_out,
):
    pos = positions.reshape(3, 1, -1)
    attr = attributes[0, 0, 0]
    rim = rim_rows[0, 0, 0]
    zr = z_rows[0, 0]
    count = edge_count[0, 0]
    atoms, width = attr.shape
    edges = edge_center.shape[-1]
    features = w_emb.shape[1]
    chans = w_chan.shape[1]
    height = width + PARTS
    inner_len = atoms + 16 * LANES
    table = inner_len + LANES
    hpad = -(-(table // LANES) // 8) * 8
    eb = 512 if edges % 512 == 0 else LANES
    blocks = edges // eb
    centers = edge_center.reshape(blocks, 1, eb)
    others = edge_other.reshape(blocks, 1, eb)
    lift = (1 - 2 * lax.axis_index("gz")).astype(f32).reshape(1)
    big = 44 * 1024 * 1024

    shape = jax.ShapeDtypeStruct
    w_chan_t = w_chan.T
    prepared = call(
        weights_kernel,
        (
            shape((features, width), bf16),
            shape((features, LANES), bf16),
            shape((features, chans), bf16),
            shape((features, features), bf16),
            shape((features, 3 * chans), bf16),
            shape((features + 3 * chans, features), bf16),
            shape((features, LANES), f32),
            shape((16, features), bf16),
        ),
        (w_emb, w_rbf, w_chan_t, w_lat, w_ten, w_out[None]),
        [pltpu.VMEM((LANES, features), f32)],
    )
    own, *sent = call(
        pack_kernel,
        (shape((height, atoms), bf16),) + (shape((height, 3 * LANES), bf16),) * 4,
        (pos, attr, rim),
        [pltpu.VMEM((PARTS, atoms), f32)],
    )
    got = [
        shifted(x, "gx" if way[0] else "gy", way[0] + way[1]) for x, way in zip(sent, sides)
    ]
    to_plus, to_minus = call(
        corner_kernel,
        (shape((height, 2 * LANES), bf16),) * 2,
        (got[0], got[1]),
    )
    corners = [shifted(to_plus, "gx", -1), shifted(to_minus, "gx", 1)]
    corners, prepared = lax.optimization_barrier((corners, prepared))
    w_emb_t, w_rad, w_chan_r, w_lat_t, w_ten_t, w_back, w_out_col, w_rbf2 = prepared
    inner, slab_send = call(
        slab_kernel,
        (shape((height, inner_len), bf16), shape((height, LANES), bf16)),
        (pos, own, zr, *got, *corners),
        [pltpu.VMEM((PARTS, inner_len), f32)],
    )
    slab_got = swapped(slab_send)
    feat, place = call(
        embed_kernel,
        (shape((features, inner_len), bf16), shape((6, hpad, LANES), f32)),
        (inner, w_emb_t),
    )
    grads, slab_grad, energy = call(
        edge_kernel,
        (shape((3, hpad, LANES), f32), shape((3, LANES), f32), shape((1, atoms), f32)),
        (
            count,
            lift,
            centers,
            others,
            feat,
            place,
            slab_got,
            w_emb_t,
            w_rad,
            w_chan_t,
            w_chan_r,
            w_lat_t,
            w_ten_t,
            w_back,
            w_out_col,
            w_rbf2,
        ),
        [
            pltpu.VMEM((features, table + LANES), bf16),
            pltpu.VMEM((6, hpad, LANES), f32),
            pltpu.VMEM((table + LANES, eb), bf16),
            pltpu.VMEM((blocks, atoms, eb), bf16),
            pltpu.VMEM((blocks, LANES, eb), bf16),
            pltpu.VMEM((blocks, LANES, eb), bf16),
            pltpu.VMEM((blocks, features, eb), bf16),
            pltpu.VMEM((blocks, features, eb), bf16),
            pltpu.VMEM((blocks, chans, eb), f32),
            pltpu.VMEM((blocks, 16, eb), f32),
            pltpu.VMEM((blocks, features, eb), bf16),
            pltpu.VMEM((blocks, 64, eb), f32),
            pltpu.VMEM((9 * chans, atoms), f32),
            pltpu.VMEM((9 * chans, atoms), bf16),
            pltpu.VMEM((9 * chans, atoms), f32),
            pltpu.VMEM((6 * hpad, LANES), f32),
            pltpu.VMEM((64, LANES), f32),
        ],
        smem=2,
        limit=big,
    )
    slab_back = swapped(slab_grad)
    along_x, along_y = shape((15, LANES), f32), shape((9, LANES), f32)
    own_grad, to_xm, to_xp, to_ym, to_yp = call(
        return_kernel,
        (shape((3, 8, LANES), f32), along_x, along_x, along_y, along_y),
        (grads, slab_back, zr),
    )
    from_xp, from_xm = shifted(to_xm, "gx", 1), shifted(to_xp, "gx", -1)
    to_ym, to_yp = call(turn_kernel, (along_y, along_y), (from_xp, from_xm, to_ym, to_yp))
    from_yp, from_ym = shifted(to_ym, "gy", 1), shifted(to_yp, "gy", -1)
    forces = call(
        force_kernel,
        shape((3, 1, atoms), f32),
        (own_grad, rim, from_xp, from_xm, from_yp, from_ym),
        [pltpu.VMEM((8, 8, LANES), f32)],
    )
    return (energy.reshape(1, 1, 1, atoms), forces.reshape(1, 1, 1, 3, atoms))


def solution(mesh):
    return jax.shard_map(
        per_device,
        mesh=mesh,
        in_specs=(
            P("gx", "gy", "gz", None, None),
            P("gx", "gy", "gz", None, None),
            P("gx", "gy", "gz", None),
            P("gx", "gy", "gz", None),
            P("gx", "gy", "gz"),
            P("gx", "gy", "gz", None, None),
            P("gx", "gy", "gz", None),
            P(),
            P(),
            P(),
            P(),
            P(),
            P(),
        ),
        out_specs=(P("gx", "gy", "gz", None), P("gx", "gy", "gz", None, None)),
        check_vma=False,
    )
```

```python
import jax
import jax.numpy as jnp
from jax import lax
from jax.experimental import pallas as pl
from jax.experimental.pallas import tpu as pltpu
from jax.sharding import PartitionSpec as P

f32 = jnp.float32
bf16 = jnp.bfloat16
LANES = 128
PARTS = 16
BLOCK = 256
ROOT3 = 3.0**0.5
BANDS = (0, 1, 1, 1, 2, 2, 2, 2, 2)

rim_cells = [(0, 0), (0, 1), (0, 2), (1, 0), (1, 2), (2, 0), (2, 1), (2, 2)]
cycle_cells = [(p, q) for p in range(5) for q in range(5) if p in (0, 4) or q in (0, 4)]


def source_of(position):
    if position == 0:
        return (-1, 2)
    if position == 4:
        return (1, 0)
    return (0, position - 1)


routes = {}
for _cycle, (_p, _q) in enumerate(cycle_cells):
    (_sx, _a), (_sy, _b) = source_of(_p), source_of(_q)
    routes.setdefault((_sx, _sy), []).append((_cycle, rim_cells.index((_a, _b))))
sides = [(0, -1), (0, 1), (-1, 0), (1, 0)]


def dot(a, b):
    return lax.dot_general(a, b, (((1,), (0,)), ((), ())), preferred_element_type=f32)


def dot_t(a, b):
    return lax.dot_general(a, b, (((1,), (1,)), ((), ())), preferred_element_type=f32)


def rows_of(shape):
    return lax.broadcasted_iota(jnp.int32, shape, 0)


def one_hot(index, size):
    return jnp.where(rows_of((size, index.shape[1])) == index, 1.0, 0.0)


def halves(values):
    upper = values.astype(bf16).astype(f32)
    return upper, values - upper


def masked(hot_low, high16, value):
    mask = jnp.where(high16 == value, 1.0, 0.0).astype(bf16)
    size, lanes = hot_low.shape
    return (hot_low.reshape(size // 16, 16, lanes) * mask[None]).reshape(size, lanes)


def half_silu(x):
    half = 0.5 * x
    return (0.5 * (half * (1.0 + jnp.tanh(half)))).astype(bf16)


def pack_kernel(pos_ref, attr_ref, rim_ref, own_ref, *rest):
    sends, parts = rest[:-1], rest[-1]
    atoms, width = attr_ref.shape
    eye = jnp.where(
        rows_of((width, width)) == lax.broadcasted_iota(jnp.int32, (width, width), 1), 1.0, 0.0
    ).astype(bf16)
    own_ref[0:width, :] = dot_t(eye, attr_ref[...]).astype(bf16)
    parts[...] = jnp.zeros_like(parts)
    for d in range(3):
        parts[d : d + 1, :], parts[3 + d : 4 + d, :] = halves(pos_ref[d])
    own_ref[width : width + PARTS, :] = parts[...].astype(bf16)
    packed = own_ref[...]
    for rim in range(8):
        hot = one_hot(rim_ref[rim : rim + 1, :], atoms).astype(bf16)
        cell = dot(packed, hot).astype(bf16)
        for way, send in zip(sides, sends):
            for slot, (_, source) in enumerate(routes[way]):
                if source == rim:
                    send[:, slot * LANES : (slot + 1) * LANES] = cell


def corner_kernel(minus_ref, plus_ref, to_plus_ref, to_minus_ref):
    first, last = slice(0, LANES), slice(2 * LANES, 3 * LANES)
    for slot, ref in enumerate((minus_ref, plus_ref)):
        lanes = slice(slot * LANES, (slot + 1) * LANES)
        to_plus_ref[:, lanes] = ref[:, last]
        to_minus_ref[:, lanes] = ref[:, first]


def slab_kernel(pos_ref, own_ref, zrows_ref, *rest):
    got, corners, (inner_ref, send_ref, parts) = rest[:4], rest[4:6], rest[6:]
    atoms = own_ref.shape[1]
    height = own_ref.shape[0]
    width = height - PARTS
    inner_len = inner_ref.shape[1]
    inner_ref[:, 0:atoms] = own_ref[...]
    parts[...] = jnp.zeros_like(parts)
    for d in range(3):
        parts[d : d + 1, 0:atoms], parts[3 + d : 4 + d, 0:atoms] = halves(pos_ref[d])
    arrivals = []
    for way, ref in zip(sides, got):
        for slot, (cycle, _) in enumerate(routes[way]):
            arrivals.append((way, ref, slot, cycle))
    for sx, ref in zip((-1, 1), corners):
        for slot, sy in enumerate((-1, 1)):
            arrivals.append(((sx, sy), ref, slot, routes[(sx, sy)][0][0]))
    for way, ref, slot, cycle in arrivals:
        lanes = slice(slot * LANES, (slot + 1) * LANES)
        into = slice(atoms + cycle * LANES, atoms + (cycle + 1) * LANES)
        inner_ref[0:width, into] = ref[0:width, lanes]
        arrived = ref[width:height, lanes].astype(f32)
        joined = arrived[0:3] + arrived[3:6]
        axis = rows_of((3, LANES))
        shift = jnp.where(axis == 0, float(way[0]), jnp.where(axis == 1, float(way[1]), 0.0))
        upper, lower = halves(joined + shift)
        parts[0:3, into] = upper
        parts[3:6, into] = lower
    inner_ref[width:height, :] = parts[...].astype(bf16)
    hot = one_hot(zrows_ref[...], inner_len).astype(bf16)
    send_ref[...] = dot(inner_ref[...], hot).astype(bf16)


def unit(size):
    lanes = lax.broadcasted_iota(jnp.int32, (size, size), 1)
    return jnp.where(rows_of((size, size)) == lanes, 1.0, 0.0)


def weights_kernel(
    w_emb_ref,
    w_rbf_ref,
    w_chan_t_ref,
    w_lat_ref,
    w_ten_ref,
    w_out_ref,
    emb_t_ref,
    rad_ref,
    chan_ref,
    lat_t_ref,
    ten_t_ref,
    back_ref,
    out_ref,
    rbf_ref,
    scratch,
):
    features = w_lat_ref.shape[0]
    eye = unit(features)
    eye_b = eye.astype(bf16)
    emb_t_ref[...] = dot_t(eye_b, w_emb_ref[...]).astype(bf16)
    chan_ref[...] = dot_t(eye_b, w_chan_t_ref[...]).astype(bf16)
    lat_t_ref[...] = (0.5 * dot_t(eye_b, w_lat_ref[...])).astype(bf16)
    ten_t_ref[...] = (0.5 * dot_t(eye_b, w_ten_ref[...])).astype(bf16)
    back_ref[0:features, :] = w_lat_ref[...]
    back_ref[features:, :] = w_ten_ref[...]
    column = jnp.sum(eye * w_out_ref[...], axis=1, keepdims=True)
    out_ref[...] = jnp.broadcast_to(column, out_ref.shape)
    upper, lower = halves(0.5 * w_rbf_ref[...])
    rbf_ref[...] = jnp.concatenate([upper, lower], axis=0).astype(bf16)
    scratch[...] = jnp.zeros_like(scratch)
    for start, value in ((0, upper), (8, upper), (16, lower), (24, lower)):
        scratch[start : start + 8, :] = value
    rad_ref[...] = dot_t(eye_b, scratch[...].astype(bf16)).astype(bf16)


def embed_kernel(inner_ref, w_emb_ref, feat_ref, place_ref):
    width = w_emb_ref.shape[1]
    inner_len = inner_ref.shape[1]
    for first in range(0, inner_len, 512):
        raw = dot(w_emb_ref[...], inner_ref[0:width, first : first + 512])
        feat_ref[:, first : first + 512] = half_silu(raw)
    parts = inner_ref[width:, :].astype(f32)
    place_ref[...] = jnp.zeros_like(place_ref)
    for high in range(inner_len // LANES):
        place_ref[0:6, high, :] = parts[0:6, high * LANES : (high + 1) * LANES]


def bucket_kernel(count_ref, centers_ref, others_ref, center_ref, other_ref, meta_ref, rows_s, low_s):
    lines = centers_ref.shape[0]
    count = count_ref[0]
    c, o = centers_ref[...], others_ref[...]
    shape = (lines, LANES)
    order = rows_of(shape) * LANES + lax.broadcasted_iota(jnp.int32, shape, 1)
    half = lax.shift_right_logical(c, 8)
    marks = [
        jnp.where(order < count, jnp.where(half == h, 1.0, 0.0), 0.0) for h in range(2)
    ]
    square = (LANES, LANES)
    tri = jnp.where(rows_of(square) < lax.broadcasted_iota(jnp.int32, square, 1), 1.0, 0.0)
    tall = (lines, lines)
    below = jnp.where(lax.broadcasted_iota(jnp.int32, tall, 1) < rows_of(tall), 1.0, 0.0)
    starts = [0.0, None]
    slot = jnp.full(shape, -1.0, f32)
    for h in range(2):
        mark = marks[h].astype(bf16)
        inside = dot(mark, tri.astype(bf16))
        totals = dot(mark, jnp.ones(square, bf16))
        before = dot(below.astype(bf16), totals.astype(bf16))
        everything = jnp.sum(totals, axis=0, keepdims=True)
        if h == 0:
            blocks = jnp.floor((everything + (BLOCK - 1)) * (1.0 / BLOCK))
            starts[1] = blocks * BLOCK
            first_blocks = blocks
        else:
            blocks = first_blocks + jnp.floor((everything + (BLOCK - 1)) * (1.0 / BLOCK))
        slot = jnp.where(marks[h] > 0.0, starts[h] + before + inside, slot)
    meta_ref[0:1, :] = first_blocks.astype(jnp.int32)
    meta_ref[1:2, :] = blocks.astype(jnp.int32)
    slot = slot.astype(jnp.int32)
    slot_high = lax.shift_right_arithmetic(slot, 7)
    slot_low = lax.bitwise_and(slot, LANES - 1)
    highs = center_ref.shape[0]
    values = [
        jnp.ones(shape, f32),
        lax.bitwise_and(c, 255).astype(f32),
        lax.shift_right_logical(o, 7).astype(f32),
        lax.bitwise_and(o, LANES - 1).astype(f32),
    ]
    for line in range(lines):
        lanes = slice(line * LANES, (line + 1) * LANES)
        high = one_hot(slot_high[line : line + 1], highs)
        rows_s[:, lanes] = jnp.concatenate(
            [high * value[line : line + 1] for value in values], axis=0
        ).astype(bf16)
        low_s[:, lanes] = one_hot(slot_low[line : line + 1], LANES).astype(bf16)
    placed = dot_t(rows_s[...], low_s[...])
    center = placed[highs : 2 * highs] + placed[0:highs] - 1.0
    other = placed[2 * highs : 3 * highs] * float(LANES) + placed[3 * highs :]
    center_ref[...] = center.astype(jnp.int32)
    other_ref[...] = other.astype(jnp.int32)


def harmonic_rows(x, y, z):
    return [
        None,
        x,
        y,
        z,
        ROOT3 * x * y,
        ROOT3 * y * z,
        ROOT3 * z * x,
        0.5 * ROOT3 * (x * x - y * y),
        0.5 * (3.0 * z * z - 1.0),
    ]


def fold8(values):
    return jnp.sum(values.reshape(values.shape[0] // 8, 8, values.shape[1]), axis=0)


def edge_kernel(
    meta_ref,
    lift_ref,
    centers_ref,
    others_ref,
    feat_in_ref,
    place_in_ref,
    slab_ref,
    w_emb_ref,
    w_rad_ref,
    w_chan_t_ref,
    w_chan_ref,
    w_lat_t_ref,
    w_ten_t_ref,
    w_back_ref,
    w_out_ref,
    w_rbf_ref,
    grad_ref,
    slab_grad_ref,
    energy_ref,
    feat,
    place,
    place_b,
    own_b,
    hot_a,
    hot_b,
    center_hot,
    low_o,
    latent_s,
    slope_s,
    chan_s,
    geo_s,
    dlat_s,
    dharm_s,
    tensor,
    tensor_b,
    acc_o,
    acc_c,
):
    eb = centers_ref.shape[2]
    width = w_emb_ref.shape[1]
    features = feat_in_ref.shape[0]
    inner_len = feat_in_ref.shape[1]
    table = inner_len + LANES
    highs = table // LANES
    span = tensor.shape[2]
    halves_n = tensor.shape[0]
    chans = w_chan_t_ref.shape[0]
    hpad = place_in_ref.shape[1]
    first_blocks = meta_ref[0, 0]
    pairs = (meta_ref[1, 0] + 1) // 2

    feat[:, 0:inner_len] = feat_in_ref[...]
    raw = dot(w_emb_ref[...], slab_ref[0:width, :])
    feat[:, inner_len:table] = half_silu(raw)
    feat[:, table : table + LANES] = w_rad_ref[...]
    place[...] = place_in_ref[...]
    arrived = slab_ref[width:, :].astype(f32)
    joined = arrived[0:3] + arrived[3:6]
    joined = joined + jnp.where(rows_of((3, LANES)) == 2, lift_ref[0], 0.0)
    upper, lower = halves(joined)
    place[0:3, highs - 1, :] = upper
    place[3:6, highs - 1, :] = lower
    place_b[...] = place[...].reshape(6 * hpad, LANES).astype(bf16)
    own_b[...] = place[:, 0:8, :].reshape(48, LANES).astype(bf16)
    for hot in (hot_a, hot_b):
        hot[table:, :] = jnp.zeros((hot.shape[0] - table, eb), bf16)
    tensor[...] = jnp.zeros_like(tensor)
    acc_o[...] = jnp.zeros_like(acc_o)
    acc_c[...] = jnp.zeros_like(acc_c)

    def half_of(b):
        return jnp.where(b >= first_blocks, 1, 0)

    def prepare(b, hot):
        slot_c = centers_ref[b]
        o = others_ref[b]
        live = jnp.where(slot_c >= 0, 1.0, 0.0)
        c = jnp.maximum(slot_c, 0)
        half = half_of(b)
        c_high = lax.shift_right_logical(c, 7)
        o_high = lax.shift_right_logical(o, 7)
        hot_c = one_hot(lax.bitwise_and(c, LANES - 1), LANES).astype(bf16)
        hot_o = one_hot(lax.bitwise_and(o, LANES - 1), LANES).astype(bf16)
        low_o[b] = hot_o
        c_high16 = jnp.broadcast_to(c_high, (16, eb))
        o_high16 = jnp.broadcast_to(o_high, (16, eb))
        for high in range(highs):
            hot[high * LANES : (high + 1) * LANES, :] = masked(hot_o, o_high16, high)
        own = jnp.concatenate(
            [masked(hot_c, c_high16, high) for high in range(span // LANES)], axis=0
        )
        center_hot[b] = own
        rows = pl.ds(pl.multiple_of(half * span, span), span)
        hot[rows, :] += own

        picked = dot(place_b[...], hot_o)
        picked = (picked[0 : 3 * hpad] + picked[3 * hpad :]).reshape(3, hpad, eb)
        po = jnp.sum(picked * one_hot(o_high, hpad)[None], axis=1)
        picked = dot(own_b[...], hot_c)
        picked = (picked[0:24] + picked[24:48]).reshape(3, 8, eb)
        c_whole = c_high + half * (span // LANES)
        pc = jnp.sum(picked * one_hot(c_whole, 8)[None], axis=1)
        sep = po - pc
        rx, ry, rz = sep[0:1], sep[1:2], sep[2:3]
        squared = rx * rx + ry * ry + rz * rz
        inv_d = lax.rsqrt(squared + 0.25)
        dist = (squared + 0.25) * inv_d
        env = 1.0 / (1.0 + squared * squared * (1.0 / 16.0))
        x, y, z = rx * inv_d, ry * inv_d, rz * inv_d
        for row, value in enumerate((x, y, z, inv_d, dist, env, squared, live)):
            geo_s[b, row : row + 1, :] = value
        mu = 0.5 + 0.4 * rows_of((8, eb)).astype(f32)
        u = (dist - mu) * 2.0
        upper, lower = halves(jnp.exp(-(u * u)) * env)
        radial = jnp.concatenate([upper, lower], axis=0).astype(bf16)
        hot[table : table + 16, :] = radial
        hot[table + 16 : table + 32, :] = radial
        return x, y, z, live

    def activate(b, mixed):
        up = 1.0 + jnp.tanh(mixed)
        value = mixed * up
        latent = value.astype(bf16)
        latent_s[b] = latent
        slope_s[b] = (up + value * (2.0 - up)).astype(bf16)
        return latent

    def spread(b, latent, geo):
        x, y, z, live = geo
        chan = dot(w_chan_t_ref[...], latent) * live
        chan_s[b] = chan
        return jnp.concatenate(
            [
                (chan if h is None else chan * h).astype(bf16)
                for h in harmonic_rows(x, y, z)
            ],
            axis=0,
        )

    def first_pass(pair, carry):
        a, b = 2 * pair, 2 * pair + 1
        geo_a = prepare(a, hot_a)
        mixed_a = dot(feat[...], hot_a[...])
        geo_b = prepare(b, hot_b)
        mixed_b = dot(feat[...], hot_b[...])
        latent_a = activate(a, mixed_a)
        products_a = spread(a, latent_a, geo_a)
        latent_b = activate(b, mixed_b)
        tensor[half_of(a)] += dot_t(products_a, center_hot[a])
        products_b = spread(b, latent_b, geo_b)
        tensor[half_of(b)] += dot_t(products_b, center_hot[b])
        return carry

    lax.fori_loop(0, pairs, first_pass, 0)
    tensor_b[...] = (0.125 * tensor[...]).astype(bf16)
    tensor[...] = jnp.zeros_like(tensor)

    def invariants(b, gathered):
        geo = geo_s[b]
        harm = harmonic_rows(geo[0:1], geo[1:2], geo[2:3])
        parts = [gathered[m * chans : (m + 1) * chans] for m in range(9)]
        bands = [parts[0], None, None]
        for m in range(1, 9):
            term = parts[m] * harm[m]
            band = BANDS[m]
            bands[band] = term if bands[band] is None else bands[band] + term
        return jnp.concatenate([band.astype(bf16) for band in bands], axis=0)

    def hidden(b, invariant):
        return dot(w_lat_t_ref[...], latent_s[b]) + dot(w_ten_t_ref[...], invariant)

    def readout(b, pre):
        geo = geo_s[b]
        up = 1.0 + jnp.tanh(pre)
        value = pre * up
        weight = jnp.concatenate([w_out_ref[...]] * (eb // LANES), axis=1)
        geo_s[b, 8:9, :] = jnp.sum(value * weight, axis=0, keepdims=True)
        scale = 0.5 * geo[5:6] * geo[7:8]
        return ((up + value * (2.0 - up)) * (weight * scale)).astype(bf16)

    def unfold(b, back, gathered):
        geo = geo_s[b]
        harm = harmonic_rows(geo[0:1], geo[1:2], geo[2:3])
        dlat_s[b] = back[0:features].astype(bf16)
        dbands = [
            back[features + band * chans : features + (band + 1) * chans] for band in range(3)
        ]
        for m in range(1, 9):
            part = gathered[m * chans : (m + 1) * chans]
            dharm_s[b, (m - 1) * 8 : m * 8, :] = fold8(dbands[BANDS[m]] * part)
        return jnp.concatenate(
            [
                (dbands[BANDS[m]] if harm[m] is None else dbands[BANDS[m]] * harm[m]).astype(bf16)
                for m in range(9)
            ],
            axis=0,
        )

    def second_pass(pair, carry):
        a, b = 2 * pair, 2 * pair + 1
        gathered_a = dot(tensor_b[half_of(a)], center_hot[a])
        gathered_b = dot(tensor_b[half_of(b)], center_hot[b])
        pre_a = hidden(a, invariants(a, gathered_a))
        pre_b = hidden(b, invariants(b, gathered_b))
        back_a = dot(w_back_ref[...], readout(a, pre_a))
        back_b = dot(w_back_ref[...], readout(b, pre_b))
        products_a = unfold(a, back_a, gathered_a)
        tensor[half_of(a)] += dot_t(products_a, center_hot[a])
        products_b = unfold(b, back_b, gathered_b)
        tensor[half_of(b)] += dot_t(products_b, center_hot[b])
        return carry

    lax.fori_loop(0, pairs, second_pass, 0)
    tensor_b[...] = (0.125 * tensor[...]).astype(bf16)

    def channels_back(b, gathered):
        geo = geo_s[b]
        harm = harmonic_rows(geo[0:1], geo[1:2], geo[2:3])
        chan = chan_s[b]
        dchan = gathered[0:chans]
        dh = [None]
        for m in range(1, 9):
            part = gathered[m * chans : (m + 1) * chans]
            dchan = dchan + part * harm[m]
            total = dharm_s[b, (m - 1) * 8 : m * 8, :] + fold8(part * chan)
            dh.append(jnp.sum(total, axis=0, keepdims=True))
        return (dchan * geo[7:8]).astype(bf16), dh

    def radial_back(b, dchan):
        dlat = dlat_s[b] + dot(w_chan_ref[...], dchan).astype(bf16)
        drad = dot(w_rbf_ref[...], dlat * slope_s[b])
        return drad[0:8] + drad[8:16]

    def finish(b, drad, dh):
        geo = geo_s[b]
        x, y, z = geo[0:1], geo[1:2], geo[2:3]
        inv_d, dist, env, squared = geo[3:4], geo[4:5], geo[5:6], geo[6:7]
        live, summed = geo[7:8], geo[8:9]
        mu = 0.5 + 0.4 * rows_of((8, eb)).astype(f32)
        u = (dist - mu) * 2.0
        weighted = drad * jnp.exp(-(u * u))
        denv = jnp.sum(weighted, axis=0, keepdims=True) + live * summed
        ddist = -4.0 * env * jnp.sum(weighted * u, axis=0, keepdims=True)
        dx = dh[1] + ROOT3 * (y * dh[4] + z * dh[6] + x * dh[7])
        dy = dh[2] + ROOT3 * (x * dh[4] + z * dh[5] - y * dh[7])
        dz = dh[3] + ROOT3 * (y * dh[5] + x * dh[6]) + 3.0 * z * dh[8]
        ddist = ddist - (dx * x + dy * y + dz * z) * inv_d
        dsq = denv * (env * env * squared * -0.125) + ddist * (0.5 * inv_d)
        both = 2.0 * dsq * dist
        gs = [dx * inv_d + both * x, dy * inv_d + both * y, dz * inv_d + both * z]
        energy = summed * env * live

        o_high = lax.shift_right_logical(others_ref[b], 7)
        mask_o = one_hot(o_high, hpad)
        split = [halves(g) for g in gs]
        rows_o = jnp.concatenate(
            [mask_o * split[d][part] for part in range(2) for d in range(3)], axis=0
        ).astype(bf16)
        split.append(halves(energy))
        rows_c = jnp.concatenate(
            [split[d][part] for part in range(2) for d in range(4)]
            + [jnp.zeros((8, eb), f32)],
            axis=0,
        ).astype(bf16)
        acc_o[...] += dot_t(rows_o, low_o[b])
        acc_c[half_of(b)] += dot_t(rows_c, center_hot[b])

    def third_pass(pair, carry):
        a, b = 2 * pair, 2 * pair + 1
        gathered_a = dot(tensor_b[half_of(a)], center_hot[a])
        gathered_b = dot(tensor_b[half_of(b)], center_hot[b])
        dchan_a, dh_a = channels_back(a, gathered_a)
        drad_a = radial_back(a, dchan_a)
        dchan_b, dh_b = channels_back(b, gathered_b)
        drad_b = radial_back(b, dchan_b)
        finish(a, drad_a, dh_a)
        finish(b, drad_b, dh_b)
        return carry

    lax.fori_loop(0, pairs, third_pass, 0)
    sum_o = acc_o[0 : 3 * hpad, :] + acc_o[3 * hpad :, :]
    for d in range(3):
        grad_ref[d] = sum_o[d * hpad : (d + 1) * hpad]
        slab_grad_ref[d : d + 1, :] = sum_o[d * hpad + highs - 1 : d * hpad + highs]
    for half in range(halves_n):
        sum_c = acc_c[half, 0:4, :] + acc_c[half, 4:8, :]
        for part in range(span // LANES):
            high = half * (span // LANES) + part
            lanes = slice(part * LANES, (part + 1) * LANES)
            for d in range(3):
                grad_ref[d, high : high + 1, :] = (
                    sum_o[d * hpad + high : d * hpad + high + 1] - sum_c[d : d + 1, lanes]
                )
            energy_ref[:, high * LANES : (high + 1) * LANES] = sum_c[3:4, lanes]


def return_kernel(grad_ref, back_ref, zrows_ref, own_ref, to_xm_ref, to_xp_ref, to_ym_ref, to_yp_ref):
    hpad = grad_ref.shape[1]
    z_rows = zrows_ref[...]
    mask = one_hot(lax.shift_right_logical(z_rows, 7), hpad)
    low = one_hot(lax.bitwise_and(z_rows, LANES - 1), LANES).astype(bf16)
    pieces = [halves(back_ref[d : d + 1, :]) for d in range(3)]
    rows = jnp.concatenate(
        [mask * pieces[d][part] for part in range(2) for d in range(3)], axis=0
    ).astype(bf16)
    landed = dot_t(rows, low)
    landed = landed[0 : 3 * hpad] + landed[3 * hpad :]
    base = own_ref.shape[1] // 2
    for d in range(3):
        total = grad_ref[d] + landed[d * hpad : (d + 1) * hpad]
        own_ref[d] = total[0:8]
        for cycle, (p, q) in enumerate(cycle_cells):
            value = total[base + cycle : base + cycle + 1]
            if p in (0, 4):
                ref = to_xm_ref if p == 0 else to_xp_ref
                ref[q * 3 + d : q * 3 + d + 1, :] = value
            else:
                ref = to_ym_ref if q == 0 else to_yp_ref
                ref[(p - 1) * 3 + d : (p - 1) * 3 + d + 1, :] = value


def turn_kernel(from_xp_ref, from_xm_ref, to_ym_ref, to_yp_ref, send_ym_ref, send_yp_ref):
    for q, old, new in ((0, to_ym_ref, send_ym_ref), (4, to_yp_ref, send_yp_ref)):
        new[0:3, :] = old[0:3, :] + from_xm_ref[q * 3 : q * 3 + 3, :]
        new[3:6, :] = old[3:6, :]
        new[6:9, :] = old[6:9, :] + from_xp_ref[q * 3 : q * 3 + 3, :]


def force_kernel(
    own_ref, rim_ref, from_xp_ref, from_xm_ref, from_yp_ref, from_ym_ref, out_ref, rim_sum
):
    rim_sum[...] = jnp.zeros_like(rim_sum)
    for a, ref in ((2, from_xp_ref), (0, from_xm_ref)):
        for b in range(3):
            rim_sum[rim_cells.index((a, b)), 0:3, :] += ref[(b + 1) * 3 : (b + 2) * 3, :]
    for b, ref in ((2, from_yp_ref), (0, from_ym_ref)):
        for a in range(3):
            rim_sum[rim_cells.index((a, b)), 0:3, :] += ref[a * 3 : (a + 1) * 3, :]
    total = jnp.zeros((48, LANES), f32)
    for rim in range(8):
        index = rim_ref[rim : rim + 1, :]
        mask = one_hot(lax.shift_right_logical(index, 7), 8)
        low = one_hot(lax.bitwise_and(index, LANES - 1), LANES).astype(bf16)
        values = rim_sum[rim]
        pieces = [halves(values[d : d + 1, :]) for d in range(3)]
        rows = jnp.concatenate(
            [mask * pieces[d][part] for part in range(2) for d in range(3)], axis=0
        ).astype(bf16)
        total = total + dot_t(rows, low)
    total = total[0:24] + total[24:48]
    for d in range(3):
        for high in range(out_ref.shape[2] // LANES):
            value = own_ref[d, high : high + 1, :] + total[d * 8 + high : d * 8 + high + 1, :]
            out_ref[d, :, high * LANES : (high + 1) * LANES] = -value


def call(kernel, out_shape, args, scratch=(), smem=0, limit=None):
    vmem = pl.BlockSpec(memory_space=pltpu.VMEM)
    scalar = pl.BlockSpec(memory_space=pltpu.SMEM)
    return pl.pallas_call(
        kernel,
        out_shape=out_shape,
        in_specs=[scalar] * smem + [vmem] * (len(args) - smem),
        out_specs=jax.tree.map(lambda _: vmem, out_shape),
        scratch_shapes=list(scratch),
        compiler_params=pltpu.CompilerParams(vmem_limit_bytes=limit),
    )(*args)


def shifted(x, axis, step):
    count = lax.axis_size(axis)
    return lax.ppermute(x, axis, [((i + step) % count, i) for i in range(count)])


def swapped(x):
    count = lax.axis_size("gz")
    return lax.ppermute(x, "gz", [(i, i ^ 1) for i in range(count)])


def per_device(
    positions,
    attributes,
    edge_center,
    edge_other,
    edge_count,
    rim_rows,
    z_rows,
    w_emb,
    w_rbf,
    w_chan,
    w_lat,
    w_ten,
    w_out,
):
    pos = positions.reshape(3, 1, -1)
    attr = attributes[0, 0, 0]
    rim = rim_rows[0, 0, 0]
    zr = z_rows[0, 0]
    count = edge_count[0, 0]
    atoms, width = attr.shape
    edges = edge_center.shape[-1]
    features = w_emb.shape[1]
    chans = w_chan.shape[1]
    height = width + PARTS
    inner_len = atoms + 16 * LANES
    table = inner_len + LANES
    hpad = -(-(table // LANES) // 8) * 8
    eb = BLOCK
    span = 2 * LANES
    blocks = -(-(edges // eb + atoms // span - 1) // 2) * 2
    slot_rows = -(-(blocks * eb // LANES) // 8) * 8
    lift = (1 - 2 * lax.axis_index("gz")).astype(f32).reshape(1)
    big = 36 * 1024 * 1024

    shape = jax.ShapeDtypeStruct
    w_chan_t = w_chan.T
    prepared = call(
        weights_kernel,
        (
            shape((features, width), bf16),
            shape((features, LANES), bf16),
            shape((features, chans), bf16),
            shape((features, features), bf16),
            shape((features, 3 * chans), bf16),
            shape((features + 3 * chans, features), bf16),
            shape((features, LANES), f32),
            shape((16, features), bf16),
        ),
        (w_emb, w_rbf, w_chan_t, w_lat, w_ten, w_out[None]),
        [pltpu.VMEM((LANES, features), f32)],
    )
    own, *sent = call(
        pack_kernel,
        (shape((height, atoms), bf16),) + (shape((height, 3 * LANES), bf16),) * 4,
        (pos, attr, rim),
        [pltpu.VMEM((PARTS, atoms), f32)],
    )
    got = [
        shifted(x, "gx" if way[0] else "gy", way[0] + way[1]) for x, way in zip(sent, sides)
    ]
    lines = edges // LANES
    bucketed = call(
        bucket_kernel,
        (
            shape((slot_rows, LANES), jnp.int32),
            shape((slot_rows, LANES), jnp.int32),
            shape((2, LANES), jnp.int32),
        ),
        (count, edge_center.reshape(lines, LANES), edge_other.reshape(lines, LANES)),
        [pltpu.VMEM((4 * slot_rows, edges), bf16), pltpu.VMEM((LANES, edges), bf16)],
        smem=1,
        limit=24 * 1024 * 1024,
    )
    first, bucketed = lax.optimization_barrier((got[:2], bucketed))
    got = [*first, *got[2:]]
    centers, others, meta = bucketed
    centers = centers.reshape(-1, 1, eb)
    others = others.reshape(-1, 1, eb)
    to_plus, to_minus = call(
        corner_kernel,
        (shape((height, 2 * LANES), bf16),) * 2,
        (got[0], got[1]),
    )
    corners = [shifted(to_plus, "gx", -1), shifted(to_minus, "gx", 1)]
    corners, prepared = lax.optimization_barrier((corners, prepared))
    w_emb_t, w_rad, w_chan_r, w_lat_t, w_ten_t, w_back, w_out_col, w_rbf2 = prepared
    inner, slab_send = call(
        slab_kernel,
        (shape((height, inner_len), bf16), shape((height, LANES), bf16)),
        (pos, own, zr, *got, *corners),
        [pltpu.VMEM((PARTS, inner_len), f32)],
    )
    slab_got = swapped(slab_send)
    feat, place = call(
        embed_kernel,
        (shape((features, inner_len), bf16), shape((6, hpad, LANES), f32)),
        (inner, w_emb_t),
    )
    grads, slab_grad, energy = call(
        edge_kernel,
        (shape((3, hpad, LANES), f32), shape((3, LANES), f32), shape((1, atoms), f32)),
        (
            meta,
            lift,
            centers,
            others,
            feat,
            place,
            slab_got,
            w_emb_t,
            w_rad,
            w_chan_t,
            w_chan_r,
            w_lat_t,
            w_ten_t,
            w_back,
            w_out_col,
            w_rbf2,
        ),
        [
            pltpu.VMEM((features, table + LANES), bf16),
            pltpu.VMEM((6, hpad, LANES), f32),
            pltpu.VMEM((6 * hpad, LANES), bf16),
            pltpu.VMEM((48, LANES), bf16),
            pltpu.VMEM((table + LANES, eb), bf16),
            pltpu.VMEM((table + LANES, eb), bf16),
            pltpu.VMEM((blocks, span, eb), bf16),
            pltpu.VMEM((blocks, LANES, eb), bf16),
            pltpu.VMEM((blocks, features, eb), bf16),
            pltpu.VMEM((blocks, features, eb), bf16),
            pltpu.VMEM((blocks, chans, eb), f32),
            pltpu.VMEM((blocks, 16, eb), f32),
            pltpu.VMEM((blocks, features, eb), bf16),
            pltpu.VMEM((blocks, 64, eb), f32),
            pltpu.VMEM((atoms // span, 9 * chans, span), f32),
            pltpu.VMEM((atoms // span, 9 * chans, span), bf16),
            pltpu.VMEM((6 * hpad, LANES), f32),
            pltpu.VMEM((atoms // span, 16, span), f32),
        ],
        smem=2,
        limit=big,
    )
    slab_back = swapped(slab_grad)
    along_x, along_y = shape((15, LANES), f32), shape((9, LANES), f32)
    own_grad, to_xm, to_xp, to_ym, to_yp = call(
        return_kernel,
        (shape((3, 8, LANES), f32), along_x, along_x, along_y, along_y),
        (grads, slab_back, zr),
    )
    from_xp, from_xm = shifted(to_xm, "gx", 1), shifted(to_xp, "gx", -1)
    to_ym, to_yp = call(turn_kernel, (along_y, along_y), (from_xp, from_xm, to_ym, to_yp))
    from_yp, from_ym = shifted(to_ym, "gy", 1), shifted(to_yp, "gy", -1)
    forces = call(
        force_kernel,
        shape((3, 1, atoms), f32),
        (own_grad, rim, from_xp, from_xm, from_yp, from_ym),
        [pltpu.VMEM((8, 8, LANES), f32)],
    )
    return (energy.reshape(1, 1, 1, atoms), forces.reshape(1, 1, 1, 3, atoms))


def solution(mesh):
    return jax.shard_map(
        per_device,
        mesh=mesh,
        in_specs=(
            P("gx", "gy", "gz", None, None),
            P("gx", "gy", "gz", None, None),
            P("gx", "gy", "gz", None),
            P("gx", "gy", "gz", None),
            P("gx", "gy", "gz"),
            P("gx", "gy", "gz", None, None),
            P("gx", "gy", "gz", None),
            P(),
            P(),
            P(),
            P(),
            P(),
            P(),
        ),
        out_specs=(P("gx", "gy", "gz", None), P("gx", "gy", "gz", None, None)),
        check_vma=False,
    )
```

```python
import collections

import jax
import jax.numpy as jnp
from jax import lax
from jax.experimental import pallas as pl
from jax.experimental.pallas import tpu as pltpu
from jax.sharding import PartitionSpec as P

f32 = jnp.float32
bf16 = jnp.bfloat16
LANES = 128
PARTS = 16
BLOCK = 512
ROOT3 = 3.0**0.5
BANDS = (0, 1, 1, 1, 2, 2, 2, 2, 2)

rim_cells = [(0, 0), (0, 1), (0, 2), (1, 0), (1, 2), (2, 0), (2, 1), (2, 2)]
cycle_cells = [(p, q) for p in range(5) for q in range(5) if p in (0, 4) or q in (0, 4)]


def source_of(position):
    if position == 0:
        return (-1, 2)
    if position == 4:
        return (1, 0)
    return (0, position - 1)


routes = {}
for _cycle, (_p, _q) in enumerate(cycle_cells):
    (_sx, _a), (_sy, _b) = source_of(_p), source_of(_q)
    routes.setdefault((_sx, _sy), []).append((_cycle, rim_cells.index((_a, _b))))
sides = [(0, -1), (0, 1), (-1, 0), (1, 0)]


def dot(a, b):
    return lax.dot_general(a, b, (((1,), (0,)), ((), ())), preferred_element_type=f32)


def dot_t(a, b):
    return lax.dot_general(a, b, (((1,), (1,)), ((), ())), preferred_element_type=f32)


def rows_of(shape):
    return lax.broadcasted_iota(jnp.int32, shape, 0)


def one_hot(index, size):
    return jnp.where(rows_of((size, index.shape[1])) == index, 1.0, 0.0)


def halves(values):
    upper = values.astype(bf16).astype(f32)
    return upper, values - upper


def masked(hot_low, high16, value):
    mask = jnp.where(high16 == value, 1.0, 0.0).astype(bf16)
    size, lanes = hot_low.shape
    return (hot_low.reshape(size // 16, 16, lanes) * mask[None]).reshape(size, lanes)


def half_silu(x):
    half = 0.5 * x
    return (0.5 * (half * (1.0 + jnp.tanh(half)))).astype(bf16)


def fetch(sources, targets, sems):
    copies = [
        pltpu.make_async_copy(source, target, sems.at[index])
        for index, (source, target) in enumerate(zip(sources, targets))
    ]
    for copy in copies:
        copy.start()
    for copy in copies:
        copy.wait()


def pack_kernel(pos_hbm, attr_hbm, rim_hbm, zrows_hbm, own_ref, rim_ref, zrows_ref, *rest):
    sends, (parts, pos_ref, attr_ref, sems) = rest[:4], rest[4:]
    fetch(
        (pos_hbm, attr_hbm, rim_hbm, zrows_hbm), (pos_ref, attr_ref, rim_ref, zrows_ref), sems
    )
    atoms, width = attr_ref.shape
    eye = jnp.where(
        rows_of((width, width)) == lax.broadcasted_iota(jnp.int32, (width, width), 1), 1.0, 0.0
    ).astype(bf16)
    own_ref[0:width, :] = dot_t(eye, attr_ref[...]).astype(bf16)
    parts[...] = jnp.zeros_like(parts)
    for d in range(3):
        parts[d : d + 1, :], parts[3 + d : 4 + d, :] = halves(pos_ref[d])
    own_ref[width : width + PARTS, :] = parts[...].astype(bf16)
    packed = own_ref[...]
    for rim in range(8):
        hot = one_hot(rim_ref[rim : rim + 1, :], atoms).astype(bf16)
        cell = dot(packed, hot).astype(bf16)
        for way, send in zip(sides, sends):
            for slot, (_, source) in enumerate(routes[way]):
                if source == rim:
                    send[:, slot * LANES : (slot + 1) * LANES] = cell


def corner_kernel(minus_ref, plus_ref, to_plus_ref, to_minus_ref):
    first, last = slice(0, LANES), slice(2 * LANES, 3 * LANES)
    for slot, ref in enumerate((minus_ref, plus_ref)):
        lanes = slice(slot * LANES, (slot + 1) * LANES)
        to_plus_ref[:, lanes] = ref[:, last]
        to_minus_ref[:, lanes] = ref[:, first]


def slab_kernel(own_ref, zrows_ref, *rest):
    got, corners, (inner_ref, send_ref, parts) = rest[:4], rest[4:6], rest[6:]
    atoms = own_ref.shape[1]
    height = own_ref.shape[0]
    width = height - PARTS
    inner_len = inner_ref.shape[1]
    inner_ref[:, 0:atoms] = own_ref[...]
    parts[...] = jnp.zeros_like(parts)
    parts[0:6, 0:atoms] = own_ref[width:height, :].astype(f32)[0:6]
    arrivals = []
    for way, ref in zip(sides, got):
        for slot, (cycle, _) in enumerate(routes[way]):
            arrivals.append((way, ref, slot, cycle))
    for sx, ref in zip((-1, 1), corners):
        for slot, sy in enumerate((-1, 1)):
            arrivals.append(((sx, sy), ref, slot, routes[(sx, sy)][0][0]))
    for way, ref, slot, cycle in arrivals:
        lanes = slice(slot * LANES, (slot + 1) * LANES)
        into = slice(atoms + cycle * LANES, atoms + (cycle + 1) * LANES)
        inner_ref[0:width, into] = ref[0:width, lanes]
        arrived = ref[width:height, lanes].astype(f32)
        joined = arrived[0:3] + arrived[3:6]
        axis = rows_of((3, LANES))
        shift = jnp.where(axis == 0, float(way[0]), jnp.where(axis == 1, float(way[1]), 0.0))
        upper, lower = halves(joined + shift)
        parts[0:3, into] = upper
        parts[3:6, into] = lower
    inner_ref[width:height, :] = parts[...].astype(bf16)
    hot = one_hot(zrows_ref[...], inner_len).astype(bf16)
    send_ref[...] = dot(inner_ref[...], hot).astype(bf16)


def unit(size):
    lanes = lax.broadcasted_iota(jnp.int32, (size, size), 1)
    return jnp.where(rows_of((size, size)) == lanes, 1.0, 0.0)


def weights_kernel(
    w_emb_hbm,
    w_rbf_hbm,
    w_chan_t_hbm,
    w_lat_hbm,
    w_ten_hbm,
    w_out_hbm,
    emb_t_ref,
    rad_ref,
    chan_ref,
    w_chan_t_ref,
    lat_t_ref,
    ten_t_ref,
    back_ref,
    out_ref,
    rbf_ref,
    scratch,
    w_emb_ref,
    w_rbf_ref,
    w_lat_ref,
    w_ten_ref,
    w_out_ref,
    sems,
):
    fetch(
        (w_emb_hbm, w_rbf_hbm, w_chan_t_hbm, w_lat_hbm, w_ten_hbm, w_out_hbm),
        (w_emb_ref, w_rbf_ref, w_chan_t_ref, w_lat_ref, w_ten_ref, w_out_ref),
        sems,
    )
    features = w_lat_ref.shape[0]
    eye = unit(features)
    eye_b = eye.astype(bf16)
    emb_t_ref[...] = dot_t(eye_b, w_emb_ref[...]).astype(bf16)
    chan_ref[...] = dot_t(eye_b, w_chan_t_ref[...]).astype(bf16)
    lat_t_ref[...] = (0.5 * dot_t(eye_b, w_lat_ref[...])).astype(bf16)
    ten_t_ref[...] = (0.5 * dot_t(eye_b, w_ten_ref[...])).astype(bf16)
    back_ref[0:features, :] = w_lat_ref[...]
    back_ref[features:, :] = w_ten_ref[...]
    column = jnp.sum(eye * w_out_ref[...], axis=1, keepdims=True)
    out_ref[...] = jnp.broadcast_to(column, out_ref.shape)
    upper, lower = halves(0.5 * w_rbf_ref[...])
    rbf_ref[...] = jnp.concatenate([upper, lower], axis=0).astype(bf16)
    scratch[...] = jnp.zeros_like(scratch)
    for start, value in ((0, upper), (8, upper), (16, lower), (24, lower)):
        scratch[start : start + 8, :] = value
    rad_ref[...] = dot_t(eye_b, scratch[...].astype(bf16)).astype(bf16)


def embed_kernel(inner_ref, w_emb_ref, feat_ref, place_ref):
    width = w_emb_ref.shape[1]
    inner_len = inner_ref.shape[1]
    for first in range(0, inner_len, 512):
        raw = dot(w_emb_ref[...], inner_ref[0:width, first : first + 512])
        feat_ref[:, first : first + 512] = half_silu(raw)
    parts = inner_ref[width:, :].astype(f32)
    place_ref[...] = jnp.zeros_like(place_ref)
    for high in range(inner_len // LANES):
        place_ref[0:6, high, :] = parts[0:6, high * LANES : (high + 1) * LANES]


def bucket_kernel(
    count_ref,
    centers_hbm,
    others_hbm,
    center_ref,
    other_ref,
    meta_ref,
    rows_s,
    low_s,
    centers_ref,
    others_ref,
    sems,
):
    fetch((centers_hbm, others_hbm), (centers_ref, others_ref), sems)
    lines = centers_ref.shape[0]
    count = count_ref[0]
    c, o = centers_ref[...], others_ref[...]
    shape = (lines, LANES)
    order = rows_of(shape) * LANES + lax.broadcasted_iota(jnp.int32, shape, 1)
    half = lax.shift_right_logical(c, 8)
    marks = [
        jnp.where(order < count, jnp.where(half == h, 1.0, 0.0), 0.0) for h in range(2)
    ]
    square = (LANES, LANES)
    tri = jnp.where(rows_of(square) < lax.broadcasted_iota(jnp.int32, square, 1), 1.0, 0.0)
    tall = (lines, lines)
    below = jnp.where(lax.broadcasted_iota(jnp.int32, tall, 1) < rows_of(tall), 1.0, 0.0)
    starts = [0.0, None]
    slot = jnp.full(shape, -1.0, f32)
    for h in range(2):
        mark = marks[h].astype(bf16)
        inside = dot(mark, tri.astype(bf16))
        totals = dot(mark, jnp.ones(square, bf16))
        before = dot(below.astype(bf16), totals.astype(bf16))
        everything = jnp.sum(totals, axis=0, keepdims=True)
        if h == 0:
            blocks = jnp.floor((everything + (BLOCK - 1)) * (1.0 / BLOCK))
            starts[1] = blocks * BLOCK
            first_blocks = blocks
        else:
            blocks = first_blocks + jnp.floor((everything + (BLOCK - 1)) * (1.0 / BLOCK))
        slot = jnp.where(marks[h] > 0.0, starts[h] + before + inside, slot)
    meta_ref[0:1, :] = first_blocks.astype(jnp.int32)
    meta_ref[1:2, :] = blocks.astype(jnp.int32)
    slot = slot.astype(jnp.int32)
    slot_high = lax.shift_right_arithmetic(slot, 7)
    slot_low = lax.bitwise_and(slot, LANES - 1)
    highs = center_ref.shape[0]
    values = [
        jnp.ones(shape, f32),
        lax.bitwise_and(c, 255).astype(f32),
        lax.shift_right_logical(o, 7).astype(f32),
        lax.bitwise_and(o, LANES - 1).astype(f32),
    ]
    for line in range(lines):
        lanes = slice(line * LANES, (line + 1) * LANES)
        high = one_hot(slot_high[line : line + 1], highs)
        rows_s[:, lanes] = jnp.concatenate(
            [high * value[line : line + 1] for value in values], axis=0
        ).astype(bf16)
        low_s[:, lanes] = one_hot(slot_low[line : line + 1], LANES).astype(bf16)
    placed = dot_t(rows_s[...], low_s[...])
    center = placed[highs : 2 * highs] + placed[0:highs] - 1.0
    other = placed[2 * highs : 3 * highs] * float(LANES) + placed[3 * highs :]
    center_ref[...] = center.astype(jnp.int32)
    other_ref[...] = other.astype(jnp.int32)


def harmonic_rows(x, y, z):
    return [
        None,
        x,
        y,
        z,
        ROOT3 * x * y,
        ROOT3 * y * z,
        ROOT3 * z * x,
        0.5 * ROOT3 * (x * x - y * y),
        0.5 * (3.0 * z * z - 1.0),
    ]


def fold8(values):
    return jnp.sum(values.reshape(values.shape[0] // 8, 8, values.shape[1]), axis=0)


FIELDS = (
    ["hot", "center_hot", "low_o", "latent", "slope", "chan"]
    + ["geo", "dlat", "dharm", "tensor", "acc_o", "acc_c"]
)
Scratch = collections.namedtuple("Scratch", FIELDS)


def edge_kernel(
    meta_ref,
    lift_ref,
    centers_ref,
    others_ref,
    feat_in_ref,
    place_in_ref,
    slab_ref,
    w_emb_ref,
    w_rad_ref,
    w_chan_t_ref,
    w_chan_ref,
    w_lat_t_ref,
    w_ten_t_ref,
    w_back_ref,
    w_out_ref,
    w_rbf_ref,
    grad_ref,
    slab_grad_ref,
    energy_ref,
    feat,
    place,
    place_b,
    own_b,
    tensor_b,
    *scratch,
):
    names = len(scratch) // 2
    even, odd = (Scratch(*scratch[side * names : (side + 1) * names]) for side in range(2))
    eb = centers_ref.shape[2]
    width = w_emb_ref.shape[1]
    features = feat_in_ref.shape[0]
    inner_len = feat_in_ref.shape[1]
    table = inner_len + LANES
    highs = table // LANES
    span = tensor_b.shape[2]
    halves_n = tensor_b.shape[0]
    chans = w_chan_t_ref.shape[0]
    hpad = place_in_ref.shape[1]
    first_blocks = meta_ref[0, 0]
    total_blocks = meta_ref[1, 0]
    pairs = total_blocks // 2

    feat[:, 0:inner_len] = feat_in_ref[...]
    raw = dot(w_emb_ref[...], slab_ref[0:width, :])
    feat[:, inner_len:table] = half_silu(raw)
    feat[:, table : table + LANES] = w_rad_ref[...]
    place[...] = place_in_ref[...]
    arrived = slab_ref[width:, :].astype(f32)
    joined = arrived[0:3] + arrived[3:6]
    joined = joined + jnp.where(rows_of((3, LANES)) == 2, lift_ref[0], 0.0)
    upper, lower = halves(joined)
    place[0:3, highs - 1, :] = upper
    place[3:6, highs - 1, :] = lower
    place_b[...] = place[...].reshape(6 * hpad, LANES).astype(bf16)
    own_b[...] = place[:, 0:8, :].reshape(48, LANES).astype(bf16)
    for own in (even, odd):
        own.hot[table:, :] = jnp.zeros((own.hot.shape[0] - table, eb), bf16)
        for ref in (own.tensor, own.acc_o, own.acc_c):
            ref[...] = jnp.zeros_like(ref)

    def half_of(b):
        return jnp.where(b >= first_blocks, 1, 0)

    def each_block(run):
        def step(pair, carry):
            run([(even, 2 * pair, pair), (odd, 2 * pair + 1, pair)])
            return carry

        lax.fori_loop(0, pairs, step, 0)

        @pl.when(total_blocks > 2 * pairs)
        def _():
            run([(even, 2 * pairs, pairs)])

    def prepare(side):
        own_s, b, at = side
        hot = own_s.hot
        slot_c = centers_ref[b]
        o = others_ref[b]
        live = jnp.where(slot_c >= 0, 1.0, 0.0)
        c = jnp.maximum(slot_c, 0)
        half = half_of(b)
        c_high = lax.shift_right_logical(c, 7)
        o_high = lax.shift_right_logical(o, 7)
        hot_c = one_hot(lax.bitwise_and(c, LANES - 1), LANES).astype(bf16)
        hot_o = one_hot(lax.bitwise_and(o, LANES - 1), LANES).astype(bf16)
        own_s.low_o[at] = hot_o
        c_high16 = jnp.broadcast_to(c_high, (16, eb))
        o_high16 = jnp.broadcast_to(o_high, (16, eb))
        for high in range(highs):
            hot[high * LANES : (high + 1) * LANES, :] = masked(hot_o, o_high16, high)
        own = jnp.concatenate(
            [masked(hot_c, c_high16, high) for high in range(span // LANES)], axis=0
        )
        own_s.center_hot[at] = own
        rows = pl.ds(pl.multiple_of(half * span, span), span)
        hot[rows, :] += own

        picked = dot(place_b[...], hot_o)
        picked = (picked[0 : 3 * hpad] + picked[3 * hpad :]).reshape(3, hpad, eb)
        po = jnp.sum(picked * one_hot(o_high, hpad)[None], axis=1)
        picked = dot(own_b[...], hot_c)
        picked = (picked[0:24] + picked[24:48]).reshape(3, 8, eb)
        c_whole = c_high + half * (span // LANES)
        pc = jnp.sum(picked * one_hot(c_whole, 8)[None], axis=1)
        sep = po - pc
        rx, ry, rz = sep[0:1], sep[1:2], sep[2:3]
        squared = rx * rx + ry * ry + rz * rz
        inv_d = lax.rsqrt(squared + 0.25)
        dist = (squared + 0.25) * inv_d
        env = 1.0 / (1.0 + squared * squared * (1.0 / 16.0))
        x, y, z = rx * inv_d, ry * inv_d, rz * inv_d
        for row, value in enumerate((x, y, z, inv_d, dist, env, squared, live)):
            own_s.geo[at, row : row + 1, :] = value
        mu = 0.5 + 0.4 * rows_of((8, eb)).astype(f32)
        u = (dist - mu) * 2.0
        upper, lower = halves(jnp.exp(-(u * u)) * env)
        radial = jnp.concatenate([upper, lower], axis=0).astype(bf16)
        hot[table : table + 16, :] = radial
        hot[table + 16 : table + 32, :] = radial
        return x, y, z, live, own

    def activate(side, mixed):
        own_s, _, at = side
        up = 1.0 + jnp.tanh(mixed)
        value = mixed * up
        latent = value.astype(bf16)
        own_s.latent[at] = latent
        own_s.slope[at] = (up + value * (2.0 - up)).astype(bf16)
        return latent

    def spread(side, latent, geo):
        own_s, _, at = side
        x, y, z, live, _ = geo
        chan = dot(w_chan_t_ref[...], latent) * live
        own_s.chan[at] = chan
        return jnp.concatenate(
            [
                (chan if h is None else chan * h).astype(bf16)
                for h in harmonic_rows(x, y, z)
            ],
            axis=0,
        )

    def gather_tensor(side):
        own_s, b, at = side
        return dot(tensor_b[half_of(b)], own_s.center_hot[at])

    def add_tensor(side, products, hot):
        own_s, b, _ = side
        own_s.tensor[half_of(b)] += dot_t(products, hot)

    def first_pass(sides):
        geos, mixed = [], []
        for side in sides:
            geos.append(prepare(side))
            mixed.append(dot(feat[...], side[0].hot[...]))
        products = []
        for side, geo, values in zip(sides, geos, mixed):
            products.append(spread(side, activate(side, values), geo))
        for side, geo, values in zip(sides, geos, products):
            add_tensor(side, values, geo[4])

    each_block(first_pass)
    tensor_b[...] = (0.125 * (even.tensor[...] + odd.tensor[...])).astype(bf16)
    for own in (even, odd):
        own.tensor[...] = jnp.zeros_like(own.tensor)

    def invariants(side, gathered):
        geo = side[0].geo[side[2]]
        harm = harmonic_rows(geo[0:1], geo[1:2], geo[2:3])
        parts = [gathered[m * chans : (m + 1) * chans] for m in range(9)]
        bands = [parts[0], None, None]
        for m in range(1, 9):
            term = parts[m] * harm[m]
            band = BANDS[m]
            bands[band] = term if bands[band] is None else bands[band] + term
        return jnp.concatenate([band.astype(bf16) for band in bands], axis=0)

    def hidden(side, invariant):
        return dot(w_lat_t_ref[...], side[0].latent[side[2]]) + dot(w_ten_t_ref[...], invariant)

    def readout(side, pre):
        own_s, _, at = side
        geo = own_s.geo[at]
        up = 1.0 + jnp.tanh(pre)
        value = pre * up
        weight = jnp.concatenate([w_out_ref[...]] * (eb // LANES), axis=1)
        own_s.geo[at, 8:9, :] = jnp.sum(value * weight, axis=0, keepdims=True)
        scale = 0.5 * geo[5:6] * geo[7:8]
        return ((up + value * (2.0 - up)) * (weight * scale)).astype(bf16)

    def unfold(side, back, gathered):
        own_s, _, at = side
        geo = own_s.geo[at]
        harm = harmonic_rows(geo[0:1], geo[1:2], geo[2:3])
        own_s.dlat[at] = back[0:features].astype(bf16)
        dbands = [
            back[features + band * chans : features + (band + 1) * chans] for band in range(3)
        ]
        for m in range(1, 9):
            part = gathered[m * chans : (m + 1) * chans]
            own_s.dharm[at, (m - 1) * 8 : m * 8, :] = fold8(dbands[BANDS[m]] * part)
        return jnp.concatenate(
            [
                (dbands[BANDS[m]] if harm[m] is None else dbands[BANDS[m]] * harm[m]).astype(bf16)
                for m in range(9)
            ],
            axis=0,
        )

    def second_pass(sides):
        gathered = [gather_tensor(side) for side in sides]
        pre = [hidden(side, invariants(side, g)) for side, g in zip(sides, gathered)]
        back = [dot(w_back_ref[...], readout(side, values)) for side, values in zip(sides, pre)]
        for side, values, g in zip(sides, back, gathered):
            add_tensor(side, unfold(side, values, g), side[0].center_hot[side[2]])

    each_block(second_pass)
    tensor_b[...] = (0.125 * (even.tensor[...] + odd.tensor[...])).astype(bf16)

    def channels_back(side, gathered):
        own_s, _, at = side
        geo = own_s.geo[at]
        harm = harmonic_rows(geo[0:1], geo[1:2], geo[2:3])
        chan = own_s.chan[at]
        dchan = gathered[0:chans]
        dh = [None]
        for m in range(1, 9):
            part = gathered[m * chans : (m + 1) * chans]
            dchan = dchan + part * harm[m]
            total = own_s.dharm[at, (m - 1) * 8 : m * 8, :] + fold8(part * chan)
            dh.append(jnp.sum(total, axis=0, keepdims=True))
        return (dchan * geo[7:8]).astype(bf16), dh

    def radial_back(side, dchan):
        own_s, _, at = side
        dlat = own_s.dlat[at] + dot(w_chan_ref[...], dchan).astype(bf16)
        drad = dot(w_rbf_ref[...], dlat * own_s.slope[at])
        return drad[0:8] + drad[8:16]

    def finish(side, drad, dh):
        own_s, b, at = side
        geo = own_s.geo[at]
        x, y, z = geo[0:1], geo[1:2], geo[2:3]
        inv_d, dist, env, squared = geo[3:4], geo[4:5], geo[5:6], geo[6:7]
        live, summed = geo[7:8], geo[8:9]
        mu = 0.5 + 0.4 * rows_of((8, eb)).astype(f32)
        u = (dist - mu) * 2.0
        weighted = drad * jnp.exp(-(u * u))
        denv = jnp.sum(weighted, axis=0, keepdims=True) + live * summed
        ddist = -4.0 * env * jnp.sum(weighted * u, axis=0, keepdims=True)
        dx = dh[1] + ROOT3 * (y * dh[4] + z * dh[6] + x * dh[7])
        dy = dh[2] + ROOT3 * (x * dh[4] + z * dh[5] - y * dh[7])
        dz = dh[3] + ROOT3 * (y * dh[5] + x * dh[6]) + 3.0 * z * dh[8]
        ddist = ddist - (dx * x + dy * y + dz * z) * inv_d
        dsq = denv * (env * env * squared * -0.125) + ddist * (0.5 * inv_d)
        both = 2.0 * dsq * dist
        gs = [dx * inv_d + both * x, dy * inv_d + both * y, dz * inv_d + both * z]
        energy = summed * env * live

        o_high = lax.shift_right_logical(others_ref[b], 7)
        mask_o = one_hot(o_high, hpad)
        split = [halves(g) for g in gs]
        rows_o = jnp.concatenate(
            [mask_o * split[d][part] for part in range(2) for d in range(3)], axis=0
        ).astype(bf16)
        split.append(halves(energy))
        rows_c = jnp.concatenate(
            [split[d][part] for part in range(2) for d in range(4)]
            + [jnp.zeros((8, eb), f32)],
            axis=0,
        ).astype(bf16)
        own_s.acc_o[...] += dot_t(rows_o, own_s.low_o[at])
        own_s.acc_c[half_of(b)] += dot_t(rows_c, own_s.center_hot[at])

    def third_pass(sides):
        gathered = [gather_tensor(side) for side in sides]
        back = []
        for side, g in zip(sides, gathered):
            dchan, dh = channels_back(side, g)
            back.append((radial_back(side, dchan), dh))
        for side, (drad, dh) in zip(sides, back):
            finish(side, drad, dh)

    each_block(third_pass)
    sum_o = even.acc_o[...] + odd.acc_o[...]
    sum_o = sum_o[0 : 3 * hpad] + sum_o[3 * hpad :]
    for d in range(3):
        grad_ref[d] = sum_o[d * hpad : (d + 1) * hpad]
        slab_grad_ref[d : d + 1, :] = sum_o[d * hpad + highs - 1 : d * hpad + highs]
    for half in range(halves_n):
        sum_c = even.acc_c[half] + odd.acc_c[half]
        sum_c = sum_c[0:4] + sum_c[4:8]
        for part in range(span // LANES):
            high = half * (span // LANES) + part
            lanes = slice(part * LANES, (part + 1) * LANES)
            for d in range(3):
                grad_ref[d, high : high + 1, :] = (
                    sum_o[d * hpad + high : d * hpad + high + 1] - sum_c[d : d + 1, lanes]
                )
            energy_ref[:, high * LANES : (high + 1) * LANES] = sum_c[3:4, lanes]


def return_kernel(grad_ref, back_ref, zrows_ref, own_ref, to_xm_ref, to_xp_ref, to_ym_ref, to_yp_ref):
    hpad = grad_ref.shape[1]
    z_rows = zrows_ref[...]
    mask = one_hot(lax.shift_right_logical(z_rows, 7), hpad)
    low = one_hot(lax.bitwise_and(z_rows, LANES - 1), LANES).astype(bf16)
    pieces = [halves(back_ref[d : d + 1, :]) for d in range(3)]
    rows = jnp.concatenate(
        [mask * pieces[d][part] for part in range(2) for d in range(3)], axis=0
    ).astype(bf16)
    landed = dot_t(rows, low)
    landed = landed[0 : 3 * hpad] + landed[3 * hpad :]
    base = own_ref.shape[1] // 2
    for d in range(3):
        total = grad_ref[d] + landed[d * hpad : (d + 1) * hpad]
        own_ref[d] = total[0:8]
        for cycle, (p, q) in enumerate(cycle_cells):
            value = total[base + cycle : base + cycle + 1]
            if p in (0, 4):
                ref = to_xm_ref if p == 0 else to_xp_ref
                ref[q * 3 + d : q * 3 + d + 1, :] = value
            else:
                ref = to_ym_ref if q == 0 else to_yp_ref
                ref[(p - 1) * 3 + d : (p - 1) * 3 + d + 1, :] = value


def turn_kernel(from_xp_ref, from_xm_ref, to_ym_ref, to_yp_ref, send_ym_ref, send_yp_ref):
    for q, old, new in ((0, to_ym_ref, send_ym_ref), (4, to_yp_ref, send_yp_ref)):
        new[0:3, :] = old[0:3, :] + from_xm_ref[q * 3 : q * 3 + 3, :]
        new[3:6, :] = old[3:6, :]
        new[6:9, :] = old[6:9, :] + from_xp_ref[q * 3 : q * 3 + 3, :]


def force_kernel(
    own_ref, rim_ref, from_xp_ref, from_xm_ref, from_yp_ref, from_ym_ref, out_ref, rim_sum
):
    rim_sum[...] = jnp.zeros_like(rim_sum)
    for a, ref in ((2, from_xp_ref), (0, from_xm_ref)):
        for b in range(3):
            rim_sum[rim_cells.index((a, b)), 0:3, :] += ref[(b + 1) * 3 : (b + 2) * 3, :]
    for b, ref in ((2, from_yp_ref), (0, from_ym_ref)):
        for a in range(3):
            rim_sum[rim_cells.index((a, b)), 0:3, :] += ref[a * 3 : (a + 1) * 3, :]
    total = jnp.zeros((48, LANES), f32)
    for rim in range(8):
        index = rim_ref[rim : rim + 1, :]
        mask = one_hot(lax.shift_right_logical(index, 7), 8)
        low = one_hot(lax.bitwise_and(index, LANES - 1), LANES).astype(bf16)
        values = rim_sum[rim]
        pieces = [halves(values[d : d + 1, :]) for d in range(3)]
        rows = jnp.concatenate(
            [mask * pieces[d][part] for part in range(2) for d in range(3)], axis=0
        ).astype(bf16)
        total = total + dot_t(rows, low)
    total = total[0:24] + total[24:48]
    for d in range(3):
        for high in range(out_ref.shape[2] // LANES):
            value = own_ref[d, high : high + 1, :] + total[d * 8 + high : d * 8 + high + 1, :]
            out_ref[d, :, high * LANES : (high + 1) * LANES] = -value


def call(kernel, out_shape, args, scratch=(), smem=0, far=0, limit=12 * 1024 * 1024):
    vmem = pl.BlockSpec(memory_space=pltpu.VMEM)
    scalar = pl.BlockSpec(memory_space=pltpu.SMEM)
    distant = pl.BlockSpec(memory_space=pltpu.HBM)
    return pl.pallas_call(
        kernel,
        out_shape=out_shape,
        in_specs=[scalar] * smem + [distant] * far + [vmem] * (len(args) - smem - far),
        out_specs=jax.tree.map(lambda _: vmem, out_shape),
        scratch_shapes=list(scratch),
        compiler_params=pltpu.CompilerParams(vmem_limit_bytes=limit),
    )(*args)


def shifted(x, axis, step):
    count = lax.axis_size(axis)
    return lax.ppermute(x, axis, [((i + step) % count, i) for i in range(count)])


def swapped(x):
    count = lax.axis_size("gz")
    return lax.ppermute(x, "gz", [(i, i ^ 1) for i in range(count)])


def per_device(
    positions,
    attributes,
    edge_center,
    edge_other,
    edge_count,
    rim_rows,
    z_rows,
    w_emb,
    w_rbf,
    w_chan,
    w_lat,
    w_ten,
    w_out,
):
    pos = positions.reshape(3, 1, -1)
    attr = attributes[0, 0, 0]
    rim = rim_rows[0, 0, 0]
    zr = z_rows[0, 0]
    count = edge_count[0, 0]
    atoms, width = attr.shape
    edges = edge_center.shape[-1]
    features = w_emb.shape[1]
    chans = w_chan.shape[1]
    height = width + PARTS
    inner_len = atoms + 16 * LANES
    table = inner_len + LANES
    hpad = -(-(table // LANES) // 8) * 8
    eb = BLOCK
    span = 2 * LANES
    pairs = -(-(edges // eb + atoms // span - 1) // 2)
    slot_rows = -(-(2 * pairs * eb // LANES) // 8) * 8
    lift = (1 - 2 * lax.axis_index("gz")).astype(f32).reshape(1)
    big = 42 * 1024 * 1024

    shape = jax.ShapeDtypeStruct
    prepared = call(
        weights_kernel,
        (
            shape((features, width), bf16),
            shape((features, LANES), bf16),
            shape((features, chans), bf16),
            shape((chans, features), bf16),
            shape((features, features), bf16),
            shape((features, 3 * chans), bf16),
            shape((features + 3 * chans, features), bf16),
            shape((features, LANES), f32),
            shape((16, features), bf16),
        ),
        (w_emb, w_rbf, w_chan.T, w_lat, w_ten, w_out[None]),
        [
            pltpu.VMEM((LANES, features), f32),
            pltpu.VMEM((width, features), bf16),
            pltpu.VMEM(w_rbf.shape, f32),
            pltpu.VMEM((features, features), bf16),
            pltpu.VMEM((3 * chans, features), bf16),
            pltpu.VMEM((1, features), f32),
            pltpu.SemaphoreType.DMA((6,)),
        ],
        far=6,
        limit=None,
    )
    own, rim, zr, *sent = call(
        pack_kernel,
        (
            shape((height, atoms), bf16),
            shape(rim.shape, jnp.int32),
            shape(zr.shape, jnp.int32),
            *[shape((height, 3 * LANES), bf16)] * 4,
        ),
        (pos, attr, rim, zr),
        [
            pltpu.VMEM((PARTS, atoms), f32),
            pltpu.VMEM(pos.shape, f32),
            pltpu.VMEM(attr.shape, bf16),
            pltpu.SemaphoreType.DMA((4,)),
        ],
        far=4,
    )
    got = [
        shifted(x, "gx" if way[0] else "gy", way[0] + way[1]) for x, way in zip(sent, sides)
    ]
    lines = edges // LANES
    bucketed = call(
        bucket_kernel,
        (
            shape((slot_rows, LANES), jnp.int32),
            shape((slot_rows, LANES), jnp.int32),
            shape((2, LANES), jnp.int32),
        ),
        (count, edge_center.reshape(lines, LANES), edge_other.reshape(lines, LANES)),
        [
            pltpu.VMEM((4 * slot_rows, edges), bf16),
            pltpu.VMEM((LANES, edges), bf16),
            pltpu.VMEM((lines, LANES), jnp.int32),
            pltpu.VMEM((lines, LANES), jnp.int32),
            pltpu.SemaphoreType.DMA((2,)),
        ],
        smem=1,
        far=2,
        limit=24 * 1024 * 1024,
    )
    first, bucketed = lax.optimization_barrier((got[:2], bucketed))
    got = [*first, *got[2:]]
    centers, others, meta = bucketed
    centers = centers.reshape(-1, 1, eb)
    others = others.reshape(-1, 1, eb)
    to_plus, to_minus = call(
        corner_kernel,
        (shape((height, 2 * LANES), bf16),) * 2,
        (got[0], got[1]),
    )
    corners = [shifted(to_plus, "gx", -1), shifted(to_minus, "gx", 1)]
    corners, prepared = lax.optimization_barrier((corners, prepared))
    w_emb_t, w_rad, w_chan_r, w_chan_t, w_lat_t, w_ten_t, w_back, w_out_col, w_rbf2 = prepared
    inner, slab_send = call(
        slab_kernel,
        (shape((height, inner_len), bf16), shape((height, LANES), bf16)),
        (own, zr, *got, *corners),
        [pltpu.VMEM((PARTS, inner_len), f32)],
    )
    slab_got = swapped(slab_send)
    feat, place = call(
        embed_kernel,
        (shape((features, inner_len), bf16), shape((6, hpad, LANES), f32)),
        (inner, w_emb_t),
    )
    grads, slab_grad, energy = call(
        edge_kernel,
        (shape((3, hpad, LANES), f32), shape((3, LANES), f32), shape((1, atoms), f32)),
        (
            meta,
            lift,
            centers,
            others,
            feat,
            place,
            slab_got,
            w_emb_t,
            w_rad,
            w_chan_t,
            w_chan_r,
            w_lat_t,
            w_ten_t,
            w_back,
            w_out_col,
            w_rbf2,
        ),
        [
            pltpu.VMEM((features, table + LANES), bf16),
            pltpu.VMEM((6, hpad, LANES), f32),
            pltpu.VMEM((6 * hpad, LANES), bf16),
            pltpu.VMEM((48, LANES), bf16),
            pltpu.VMEM((atoms // span, 9 * chans, span), bf16),
        ]
        + [
            pltpu.VMEM((table + LANES, eb), bf16),
            pltpu.VMEM((pairs, span, eb), bf16),
            pltpu.VMEM((pairs, LANES, eb), bf16),
            pltpu.VMEM((pairs, features, eb), bf16),
            pltpu.VMEM((pairs, features, eb), bf16),
            pltpu.VMEM((pairs, chans, eb), f32),
            pltpu.VMEM((pairs, 16, eb), f32),
            pltpu.VMEM((pairs, features, eb), bf16),
            pltpu.VMEM((pairs, 64, eb), f32),
            pltpu.VMEM((atoms // span, 9 * chans, span), f32),
            pltpu.VMEM((6 * hpad, LANES), f32),
            pltpu.VMEM((atoms // span, 16, span), f32),
        ]
        * 2,
        smem=2,
        limit=big,
    )
    slab_back = swapped(slab_grad)
    along_x, along_y = shape((15, LANES), f32), shape((9, LANES), f32)
    own_grad, to_xm, to_xp, to_ym, to_yp = call(
        return_kernel,
        (shape((3, 8, LANES), f32), along_x, along_x, along_y, along_y),
        (grads, slab_back, zr),
    )
    from_xp, from_xm = shifted(to_xm, "gx", 1), shifted(to_xp, "gx", -1)
    to_ym, to_yp = call(turn_kernel, (along_y, along_y), (from_xp, from_xm, to_ym, to_yp))
    from_yp, from_ym = shifted(to_ym, "gy", 1), shifted(to_yp, "gy", -1)
    forces = call(
        force_kernel,
        shape((3, 1, atoms), f32),
        (own_grad, rim, from_xp, from_xm, from_yp, from_ym),
        [pltpu.VMEM((8, 8, LANES), f32)],
    )
    return (energy.reshape(1, 1, 1, atoms), forces.reshape(1, 1, 1, 3, atoms))


def solution(mesh):
    return jax.shard_map(
        per_device,
        mesh=mesh,
        in_specs=(
            P("gx", "gy", "gz", None, None),
            P("gx", "gy", "gz", None, None),
            P("gx", "gy", "gz", None),
            P("gx", "gy", "gz", None),
            P("gx", "gy", "gz"),
            P("gx", "gy", "gz", None, None),
            P("gx", "gy", "gz", None),
            P(),
            P(),
            P(),
            P(),
            P(),
            P(),
        ),
        out_specs=(P("gx", "gy", "gz", None), P("gx", "gy", "gz", None, None)),
        check_vma=False,
    )
```

```python
import collections

import jax
import jax.numpy as jnp
from jax import lax
from jax.experimental import pallas as pl
from jax.experimental.pallas import tpu as pltpu
from jax.sharding import PartitionSpec as P

f32 = jnp.float32
bf16 = jnp.bfloat16
LANES = 128
PARTS = 16
BLOCK = 512
WINDOW = 768
ROOT3 = 3.0**0.5
BANDS = (0, 1, 1, 1, 2, 2, 2, 2, 2)

rim_cells = [(0, 0), (0, 1), (0, 2), (1, 0), (1, 2), (2, 0), (2, 1), (2, 2)]
cycle_cells = [(p, q) for p in range(5) for q in range(5) if p in (0, 4) or q in (0, 4)]


def source_of(position):
    if position == 0:
        return (-1, 2)
    if position == 4:
        return (1, 0)
    return (0, position - 1)


routes = {}
for _cycle, (_p, _q) in enumerate(cycle_cells):
    (_sx, _a), (_sy, _b) = source_of(_p), source_of(_q)
    routes.setdefault((_sx, _sy), []).append((_cycle, rim_cells.index((_a, _b))))
sides = [(0, -1), (0, 1), (-1, 0), (1, 0)]


def dot(a, b):
    return lax.dot_general(a, b, (((1,), (0,)), ((), ())), preferred_element_type=f32)


def dot_t(a, b):
    return lax.dot_general(a, b, (((1,), (1,)), ((), ())), preferred_element_type=f32)


def rows_of(shape):
    return lax.broadcasted_iota(jnp.int32, shape, 0)


def one_hot(index, size):
    return jnp.where(rows_of((size, index.shape[1])) == index, 1.0, 0.0)


def halves(values):
    upper = values.astype(bf16).astype(f32)
    return upper, values - upper


def masked(hot_low, high16, value):
    mask = jnp.where(high16 == value, 1.0, 0.0).astype(bf16)
    size, lanes = hot_low.shape
    return (hot_low.reshape(size // 16, 16, lanes) * mask[None]).reshape(size, lanes)


def half_silu(x):
    half = 0.5 * x
    return (0.5 * (half * (1.0 + jnp.tanh(half)))).astype(bf16)


def pack_kernel(pos_ref, attr_ref, picks_ref, own_ref, *rest):
    sends, parts = rest[:4], rest[4]
    atoms, width = attr_ref.shape
    eye = jnp.where(
        rows_of((width, width)) == lax.broadcasted_iota(jnp.int32, (width, width), 1), 1.0, 0.0
    ).astype(bf16)
    own_ref[0:width, :] = dot_t(eye, attr_ref[...]).astype(bf16)
    parts[...] = jnp.zeros_like(parts)
    for d in range(3):
        parts[d : d + 1, :], parts[3 + d : 4 + d, :] = halves(pos_ref[d])
    own_ref[width : width + PARTS, :] = parts[...].astype(bf16)
    packed = own_ref[...]
    for rim in range(8):
        hot = one_hot(picks_ref[rim : rim + 1, :], atoms).astype(bf16)
        cell = dot(packed, hot).astype(bf16)
        for way, send in zip(sides, sends):
            for slot, (_, source) in enumerate(routes[way]):
                if source == rim:
                    send[:, slot * LANES : (slot + 1) * LANES] = cell


def corner_kernel(minus_ref, plus_ref, to_plus_ref, to_minus_ref):
    first, last = slice(0, LANES), slice(2 * LANES, 3 * LANES)
    for slot, ref in enumerate((minus_ref, plus_ref)):
        lanes = slice(slot * LANES, (slot + 1) * LANES)
        to_plus_ref[:, lanes] = ref[:, last]
        to_minus_ref[:, lanes] = ref[:, first]


def slab_kernel(own_ref, picks_ref, *rest):
    got, corners, (inner_ref, send_ref, parts) = rest[:4], rest[4:6], rest[6:]
    atoms = own_ref.shape[1]
    height = own_ref.shape[0]
    width = height - PARTS
    inner_len = inner_ref.shape[1]
    inner_ref[:, 0:atoms] = own_ref[...]
    parts[...] = jnp.zeros_like(parts)
    parts[0:6, 0:atoms] = own_ref[width:height, :].astype(f32)[0:6]
    arrivals = []
    for way, ref in zip(sides, got):
        for slot, (cycle, _) in enumerate(routes[way]):
            arrivals.append((way, ref, slot, cycle))
    for sx, ref in zip((-1, 1), corners):
        for slot, sy in enumerate((-1, 1)):
            arrivals.append(((sx, sy), ref, slot, routes[(sx, sy)][0][0]))
    for way, ref, slot, cycle in arrivals:
        lanes = slice(slot * LANES, (slot + 1) * LANES)
        into = slice(atoms + cycle * LANES, atoms + (cycle + 1) * LANES)
        inner_ref[0:width, into] = ref[0:width, lanes]
        arrived = ref[width:height, lanes].astype(f32)
        joined = arrived[0:3] + arrived[3:6]
        axis = rows_of((3, LANES))
        shift = jnp.where(axis == 0, float(way[0]), jnp.where(axis == 1, float(way[1]), 0.0))
        upper, lower = halves(joined + shift)
        parts[0:3, into] = upper
        parts[3:6, into] = lower
    inner_ref[width:height, :] = parts[...].astype(bf16)
    hot = one_hot(picks_ref[8:9, :], inner_len).astype(bf16)
    send_ref[...] = dot(inner_ref[...], hot).astype(bf16)


def unit(size):
    lanes = lax.broadcasted_iota(jnp.int32, (size, size), 1)
    return jnp.where(rows_of((size, size)) == lanes, 1.0, 0.0)


def weights_kernel(
    stacked_ref,
    small_ref,
    emb_t_ref,
    rad_ref,
    chan_ref,
    w_chan_t_ref,
    lat_t_ref,
    ten_t_ref,
    back_ref,
    out_ref,
    rbf_ref,
    scratch,
):
    features = stacked_ref.shape[1]
    width = emb_t_ref.shape[1]
    inner = back_ref.shape[0]
    w_emb = stacked_ref[0:width]
    w_back = stacked_ref[width : width + inner]
    w_chan_t = stacked_ref[width + inner :]
    eye = unit(features)
    eye_b = eye.astype(bf16)
    emb_t_ref[...] = dot_t(eye_b, w_emb).astype(bf16)
    chan_ref[...] = dot_t(eye_b, w_chan_t).astype(bf16)
    w_chan_t_ref[...] = w_chan_t
    turned = (0.5 * dot_t(eye_b, w_back)).astype(bf16)
    lat_t_ref[...] = turned[:, 0:features]
    ten_t_ref[...] = turned[:, features:]
    back_ref[...] = w_back
    column = jnp.sum(eye * small_ref[8:9, :], axis=1, keepdims=True)
    out_ref[...] = jnp.broadcast_to(column, out_ref.shape)
    upper, lower = halves(0.5 * small_ref[0:8, :])
    rbf_ref[...] = jnp.concatenate([upper, lower], axis=0).astype(bf16)
    scratch[...] = jnp.zeros_like(scratch)
    for start, value in ((0, upper), (8, upper), (16, lower), (24, lower)):
        scratch[start : start + 8, :] = value
    rad_ref[...] = dot_t(eye_b, scratch[...].astype(bf16)).astype(bf16)


def embed_kernel(inner_ref, w_emb_ref, feat_ref, place_ref):
    width = w_emb_ref.shape[1]
    inner_len = inner_ref.shape[1]
    for first in range(0, inner_len, 512):
        raw = dot(w_emb_ref[...], inner_ref[0:width, first : first + 512])
        feat_ref[:, first : first + 512] = half_silu(raw)
    parts = inner_ref[width:, :].astype(f32)
    place_ref[...] = jnp.zeros_like(place_ref)
    for high in range(inner_len // LANES):
        place_ref[0:6, high, :] = parts[0:6, high * LANES : (high + 1) * LANES]


def bucket_kernel(count_ref, ends_ref, center_ref, other_ref, meta_ref, marks_s, rows_s, low_s):
    lines = ends_ref.shape[0] // 2
    keys = marks_s.shape[0] // lines
    groups = keys // 2
    count = count_ref[0]
    c, o = ends_ref[0:lines, :], ends_ref[lines:, :]
    shape = (lines, LANES)
    order = rows_of(shape) * LANES + lax.broadcasted_iota(jnp.int32, shape, 1)
    key = lax.shift_right_logical(c, 8) * groups + lax.shift_right_logical(o, 8)
    key = jnp.where(order < count, key, -1)
    for k in range(keys):
        marks_s[k * lines : (k + 1) * lines, :] = jnp.where(key == k, 1.0, 0.0).astype(bf16)
    square = (LANES, LANES)
    tri = jnp.where(rows_of(square) < lax.broadcasted_iota(jnp.int32, square, 1), 1.0, 0.0)
    tri = tri.astype(bf16)
    tall = (lines, lines)
    below = jnp.where(lax.broadcasted_iota(jnp.int32, tall, 1) < rows_of(tall), 1.0, 0.0)
    marks = marks_s[...]
    inside = dot(marks, tri)
    totals = dot(marks, jnp.ones(square, bf16))
    lane = lax.broadcasted_iota(jnp.int32, shape, 1)
    by_key = jnp.zeros(shape, f32)
    for k in range(keys):
        by_key = jnp.where(lane == k, totals[k * lines : (k + 1) * lines], by_key)
    before = dot(below.astype(bf16), by_key.astype(bf16))
    everything = jnp.broadcast_to(jnp.sum(by_key, axis=0, keepdims=True), (16, LANES))
    upper, lower = halves(everything)
    start = (dot(upper.astype(bf16), tri) + dot(lower.astype(bf16), tri))[0:1]
    row_lane = lane[0:1]
    first = jnp.sum(jnp.where(row_lane < groups, everything[0:1], 0.0), axis=1, keepdims=True)
    second = jnp.sum(jnp.where(row_lane >= groups, everything[0:1], 0.0), axis=1, keepdims=True)
    first_blocks = jnp.floor((first + (BLOCK - 1)) * (1.0 / BLOCK))
    blocks = first_blocks + jnp.floor((second + (BLOCK - 1)) * (1.0 / BLOCK))
    start = start + jnp.where(row_lane >= groups, first_blocks * BLOCK - first, 0.0)
    offset = before + start
    slot = jnp.full(shape, -1.0, f32)
    for k in range(keys):
        place = inside[k * lines : (k + 1) * lines] + offset[:, k : k + 1]
        slot = jnp.where(key == k, place, slot)
    slot = slot.astype(jnp.int32)
    slot_high = lax.shift_right_arithmetic(slot, 7)
    slot_low = lax.bitwise_and(slot, LANES - 1)
    highs = center_ref.shape[0]
    values = [
        jnp.ones(shape, f32),
        lax.bitwise_and(c, 255).astype(f32),
        lax.shift_right_logical(o, 7).astype(f32),
        lax.bitwise_and(o, LANES - 1).astype(f32),
    ]
    for line in range(lines):
        lanes = slice(line * LANES, (line + 1) * LANES)
        high = one_hot(slot_high[line : line + 1], highs)
        rows_s[:, lanes] = jnp.concatenate(
            [high * value[line : line + 1] for value in values], axis=0
        ).astype(bf16)
        low_s[:, lanes] = one_hot(slot_low[line : line + 1], LANES).astype(bf16)
    placed = dot_t(rows_s[...], low_s[...])
    center = placed[highs : 2 * highs] + placed[0:highs] - 1.0
    other = placed[2 * highs : 3 * highs] * float(LANES) + placed[3 * highs :]
    center_ref[...] = center.astype(jnp.int32)
    other_ref[...] = other.astype(jnp.int32)
    group = jnp.floor(other * (1.0 / 256.0))
    none = float(groups)
    low = jnp.min(jnp.where(center >= 0.0, group, none), axis=1, keepdims=True)
    high = jnp.max(jnp.where(center >= 0.0, group, -1.0), axis=1, keepdims=True)
    block = lax.broadcasted_iota(jnp.int32, (highs, LANES), 1)
    line_of = rows_of((highs, LANES)) // (BLOCK // LANES) == block
    low = jnp.min(jnp.where(line_of, low, none), axis=0, keepdims=True)
    high = jnp.max(jnp.where(line_of, high, -1.0), axis=0, keepdims=True)
    low = jnp.where(high < 0.0, 0.0, low)
    high = jnp.where(high < 0.0, 0.0, high)
    meta_ref[0:1, :] = jnp.broadcast_to(first_blocks, (1, LANES)).astype(jnp.int32)
    meta_ref[1:2, :] = jnp.broadcast_to(blocks, (1, LANES)).astype(jnp.int32)
    meta_ref[2:3, :] = low.astype(jnp.int32)
    meta_ref[3:4, :] = high.astype(jnp.int32)


def harmonic_rows(x, y, z):
    return [
        None,
        x,
        y,
        z,
        ROOT3 * x * y,
        ROOT3 * y * z,
        ROOT3 * z * x,
        0.5 * ROOT3 * (x * x - y * y),
        0.5 * (3.0 * z * z - 1.0),
    ]


def fold8(values):
    return jnp.sum(values.reshape(values.shape[0] // 8, 8, values.shape[1]), axis=0)


FIELDS = (
    ["hot", "extra", "center_hot", "low_o", "latent", "slope", "chan"]
    + ["geo", "dlat", "dharm", "tensor", "acc_o", "acc_c"]
)
Scratch = collections.namedtuple("Scratch", FIELDS)


def edge_kernel(
    meta_ref,
    lift_ref,
    centers_ref,
    others_ref,
    feat_in_ref,
    place_in_ref,
    slab_ref,
    w_emb_ref,
    w_rad_ref,
    w_chan_t_ref,
    w_chan_ref,
    w_lat_t_ref,
    w_ten_t_ref,
    w_back_ref,
    w_out_ref,
    w_rbf_ref,
    grad_ref,
    slab_grad_ref,
    energy_ref,
    feat,
    feat_c,
    place,
    place_b,
    own_b,
    tensor_b,
    *scratch,
):
    names = len(scratch) // 2
    even, odd = (Scratch(*scratch[side * names : (side + 1) * names]) for side in range(2))
    eb = centers_ref.shape[2]
    width = w_emb_ref.shape[1]
    features = feat_in_ref.shape[0]
    inner_len = feat_in_ref.shape[1]
    table = inner_len + LANES
    highs = table // LANES
    span = tensor_b.shape[2]
    halves_n = tensor_b.shape[0]
    chans = w_chan_t_ref.shape[0]
    hpad = place_in_ref.shape[1]
    first_blocks = meta_ref[0, 0]
    total_blocks = meta_ref[1, 0]
    pairs = total_blocks // 2

    feat[:, 0:inner_len] = feat_in_ref[...]
    raw = dot(w_emb_ref[...], slab_ref[0:width, :])
    feat[:, inner_len:table] = half_silu(raw)
    feat[:, table:] = jnp.zeros((features, feat.shape[1] - table), bf16)
    for half in range(halves_n):
        feat_c[half, :, 0:span] = feat_in_ref[:, half * span : (half + 1) * span]
        feat_c[half, :, span:] = w_rad_ref[...]
    place[...] = place_in_ref[...]
    arrived = slab_ref[width:, :].astype(f32)
    joined = arrived[0:3] + arrived[3:6]
    joined = joined + jnp.where(rows_of((3, LANES)) == 2, lift_ref[0], 0.0)
    upper, lower = halves(joined)
    place[0:3, highs - 1, :] = upper
    place[3:6, highs - 1, :] = lower
    place_b[...] = place[...].reshape(6 * hpad, LANES).astype(bf16)
    own_b[...] = place[:, 0:8, :].reshape(48, LANES).astype(bf16)
    for own in (even, odd):
        own.hot[WINDOW + span + 32 :, :] = jnp.zeros((LANES - 32, eb), bf16)
        for ref in (own.extra, own.tensor, own.acc_o, own.acc_c):
            ref[...] = jnp.zeros_like(ref)

    def half_of(b):
        return jnp.where(b >= first_blocks, 1, 0)

    def each_block(run):
        def step(pair, carry):
            run([(even, 2 * pair, pair), (odd, 2 * pair + 1, pair)])
            return carry

        lax.fori_loop(0, pairs, step, 0)

        @pl.when(total_blocks > 2 * pairs)
        def _():
            run([(even, 2 * pairs, pairs)])

    def prepare(side):
        own_s, b, at = side
        hot = own_s.hot
        slot_c = centers_ref[b]
        o = others_ref[b]
        live = jnp.where(slot_c >= 0, 1.0, 0.0)
        c = jnp.maximum(slot_c, 0)
        half = half_of(b)
        c_high = lax.shift_right_logical(c, 7)
        o_high = lax.shift_right_logical(o, 7)
        hot_c = one_hot(lax.bitwise_and(c, LANES - 1), LANES).astype(bf16)
        hot_o = one_hot(lax.bitwise_and(o, LANES - 1), LANES).astype(bf16)
        own_s.low_o[at] = hot_o
        c_high16 = jnp.broadcast_to(c_high, (16, eb))
        o_high16 = jnp.broadcast_to(o_high, (16, eb))
        shift = 2 * meta_ref[2, b]
        for high in range(WINDOW // LANES):
            rows = slice(high * LANES, (high + 1) * LANES)
            hot[rows, :] = masked(hot_o, o_high16 - shift, high)
        own = jnp.concatenate(
            [masked(hot_c, c_high16, high) for high in range(span // LANES)], axis=0
        )
        own_s.center_hot[at] = own
        hot[WINDOW : WINDOW + span, :] = own

        picked = dot(place_b[...], hot_o)
        picked = (picked[0 : 3 * hpad] + picked[3 * hpad :]).reshape(3, hpad, eb)
        po = jnp.sum(picked * one_hot(o_high, hpad)[None], axis=1)
        picked = dot(own_b[...], hot_c)
        picked = (picked[0:24] + picked[24:48]).reshape(3, 8, eb)
        c_whole = c_high + half * (span // LANES)
        pc = jnp.sum(picked * one_hot(c_whole, 8)[None], axis=1)
        sep = po - pc
        rx, ry, rz = sep[0:1], sep[1:2], sep[2:3]
        squared = rx * rx + ry * ry + rz * rz
        inv_d = lax.rsqrt(squared + 0.25)
        dist = (squared + 0.25) * inv_d
        env = 1.0 / (1.0 + squared * squared * (1.0 / 16.0))
        x, y, z = rx * inv_d, ry * inv_d, rz * inv_d
        for row, value in enumerate((x, y, z, inv_d, dist, env, squared, live)):
            own_s.geo[at, row : row + 1, :] = value
        mu = 0.5 + 0.4 * rows_of((8, eb)).astype(f32)
        u = (dist - mu) * 2.0
        upper, lower = halves(jnp.exp(-(u * u)) * env)
        radial = jnp.concatenate([upper, lower], axis=0).astype(bf16)
        hot[WINDOW + span : WINDOW + span + 16, :] = radial
        hot[WINDOW + span + 16 : WINDOW + span + 32, :] = radial
        return x, y, z, live, own

    def window(group):
        return feat[:, pl.ds(pl.multiple_of(group * 256, 256), WINDOW)]

    def windows_of(side):
        b = side[1]
        return (meta_ref[3, b] - meta_ref[2, b]) // (WINDOW // 256) + 1

    def further_windows(side):
        own_s, b, _ = side
        windows = windows_of(side)

        @pl.when(windows > 1)
        def _():
            o = others_ref[b]
            hot_o = one_hot(lax.bitwise_and(o, LANES - 1), LANES).astype(bf16)
            o_high16 = jnp.broadcast_to(lax.shift_right_logical(o, 7), (16, eb))

            def add(index, carry):
                group = meta_ref[2, b] + index * (WINDOW // 256)
                hot = jnp.concatenate(
                    [
                        masked(hot_o, o_high16 - 2 * group, high)
                        for high in range(WINDOW // LANES)
                    ],
                    axis=0,
                )
                own_s.extra[...] += dot(window(group), hot)
                return carry

            lax.fori_loop(1, windows, add, 0)

    def clear_windows(side):
        @pl.when(windows_of(side) > 1)
        def _():
            side[0].extra[...] = jnp.zeros_like(side[0].extra)

    def mix(side):
        own_s, b, _ = side
        mixed = dot(window(meta_ref[2, b]), own_s.hot[0:WINDOW, :])
        mixed = mixed + dot(feat_c[half_of(b)], own_s.hot[WINDOW:, :])
        return mixed + own_s.extra[...]

    def activate(side, mixed):
        own_s, _, at = side
        up = 1.0 + jnp.tanh(mixed)
        value = mixed * up
        latent = value.astype(bf16)
        own_s.latent[at] = latent
        own_s.slope[at] = (up + value * (2.0 - up)).astype(bf16)
        return latent

    def spread(side, latent, geo):
        own_s, _, at = side
        x, y, z, live, _ = geo
        chan = dot(w_chan_t_ref[...], latent) * live
        own_s.chan[at] = chan
        return jnp.concatenate(
            [
                (chan if h is None else chan * h).astype(bf16)
                for h in harmonic_rows(x, y, z)
            ],
            axis=0,
        )

    def gather_tensor(side):
        own_s, b, at = side
        return dot(tensor_b[half_of(b)], own_s.center_hot[at])

    def add_tensor(side, products, hot):
        own_s, b, _ = side
        own_s.tensor[half_of(b)] += dot_t(products, hot)

    def first_pass(sides):
        geos, mixed = [], []
        for side in sides:
            further_windows(side)
        for side in sides:
            geos.append(prepare(side))
            mixed.append(mix(side))
        products = []
        for side, geo, values in zip(sides, geos, mixed):
            products.append(spread(side, activate(side, values), geo))
        for side, geo, values in zip(sides, geos, products):
            add_tensor(side, values, geo[4])
        for side in sides:
            clear_windows(side)

    each_block(first_pass)
    tensor_b[...] = (0.125 * (even.tensor[...] + odd.tensor[...])).astype(bf16)
    for own in (even, odd):
        own.tensor[...] = jnp.zeros_like(own.tensor)

    def invariants(side, gathered):
        geo = side[0].geo[side[2]]
        harm = harmonic_rows(geo[0:1], geo[1:2], geo[2:3])
        parts = [gathered[m * chans : (m + 1) * chans] for m in range(9)]
        bands = [parts[0], None, None]
        for m in range(1, 9):
            term = parts[m] * harm[m]
            band = BANDS[m]
            bands[band] = term if bands[band] is None else bands[band] + term
        return jnp.concatenate([band.astype(bf16) for band in bands], axis=0)

    def hidden(side, invariant):
        return dot(w_lat_t_ref[...], side[0].latent[side[2]]) + dot(w_ten_t_ref[...], invariant)

    def readout(side, pre):
        own_s, _, at = side
        geo = own_s.geo[at]
        up = 1.0 + jnp.tanh(pre)
        value = pre * up
        weight = jnp.concatenate([w_out_ref[...]] * (eb // LANES), axis=1)
        own_s.geo[at, 8:9, :] = jnp.sum(value * weight, axis=0, keepdims=True)
        scale = 0.5 * geo[5:6] * geo[7:8]
        return ((up + value * (2.0 - up)) * (weight * scale)).astype(bf16)

    def unfold(side, back, gathered):
        own_s, _, at = side
        geo = own_s.geo[at]
        harm = harmonic_rows(geo[0:1], geo[1:2], geo[2:3])
        own_s.dlat[at] = back[0:features].astype(bf16)
        dbands = [
            back[features + band * chans : features + (band + 1) * chans] for band in range(3)
        ]
        for m in range(1, 9):
            part = gathered[m * chans : (m + 1) * chans]
            own_s.dharm[at, (m - 1) * 8 : m * 8, :] = fold8(dbands[BANDS[m]] * part)
        return jnp.concatenate(
            [
                (dbands[BANDS[m]] if harm[m] is None else dbands[BANDS[m]] * harm[m]).astype(bf16)
                for m in range(9)
            ],
            axis=0,
        )

    def second_pass(sides):
        gathered = [gather_tensor(side) for side in sides]
        pre = [hidden(side, invariants(side, g)) for side, g in zip(sides, gathered)]
        back = [dot(w_back_ref[...], readout(side, values)) for side, values in zip(sides, pre)]
        for side, values, g in zip(sides, back, gathered):
            add_tensor(side, unfold(side, values, g), side[0].center_hot[side[2]])

    each_block(second_pass)
    tensor_b[...] = (0.125 * (even.tensor[...] + odd.tensor[...])).astype(bf16)

    def channels_back(side, gathered):
        own_s, _, at = side
        geo = own_s.geo[at]
        harm = harmonic_rows(geo[0:1], geo[1:2], geo[2:3])
        chan = own_s.chan[at]
        dchan = gathered[0:chans]
        dh = [None]
        for m in range(1, 9):
            part = gathered[m * chans : (m + 1) * chans]
            dchan = dchan + part * harm[m]
            total = own_s.dharm[at, (m - 1) * 8 : m * 8, :] + fold8(part * chan)
            dh.append(jnp.sum(total, axis=0, keepdims=True))
        return (dchan * geo[7:8]).astype(bf16), dh

    def radial_back(side, dchan):
        own_s, _, at = side
        dlat = own_s.dlat[at] + dot(w_chan_ref[...], dchan).astype(bf16)
        drad = dot(w_rbf_ref[...], dlat * own_s.slope[at])
        return drad[0:8] + drad[8:16]

    def finish(side, drad, dh):
        own_s, b, at = side
        geo = own_s.geo[at]
        x, y, z = geo[0:1], geo[1:2], geo[2:3]
        inv_d, dist, env, squared = geo[3:4], geo[4:5], geo[5:6], geo[6:7]
        live, summed = geo[7:8], geo[8:9]
        mu = 0.5 + 0.4 * rows_of((8, eb)).astype(f32)
        u = (dist - mu) * 2.0
        weighted = drad * jnp.exp(-(u * u))
        denv = jnp.sum(weighted, axis=0, keepdims=True) + live * summed
        ddist = -4.0 * env * jnp.sum(weighted * u, axis=0, keepdims=True)
        dx = dh[1] + ROOT3 * (y * dh[4] + z * dh[6] + x * dh[7])
        dy = dh[2] + ROOT3 * (x * dh[4] + z * dh[5] - y * dh[7])
        dz = dh[3] + ROOT3 * (y * dh[5] + x * dh[6]) + 3.0 * z * dh[8]
        ddist = ddist - (dx * x + dy * y + dz * z) * inv_d
        dsq = denv * (env * env * squared * -0.125) + ddist * (0.5 * inv_d)
        both = 2.0 * dsq * dist
        gs = [dx * inv_d + both * x, dy * inv_d + both * y, dz * inv_d + both * z]
        energy = summed * env * live

        o_high = lax.shift_right_logical(others_ref[b], 7)
        mask_o = one_hot(o_high, hpad)
        split = [halves(g) for g in gs]
        rows_o = jnp.concatenate(
            [mask_o * split[d][part] for part in range(2) for d in range(3)], axis=0
        ).astype(bf16)
        split.append(halves(energy))
        rows_c = jnp.concatenate(
            [split[d][part] for part in range(2) for d in range(4)]
            + [jnp.zeros((8, eb), f32)],
            axis=0,
        ).astype(bf16)
        own_s.acc_o[...] += dot_t(rows_o, own_s.low_o[at])
        own_s.acc_c[half_of(b)] += dot_t(rows_c, own_s.center_hot[at])

    def third_pass(sides):
        gathered = [gather_tensor(side) for side in sides]
        back = []
        for side, g in zip(sides, gathered):
            dchan, dh = channels_back(side, g)
            back.append((radial_back(side, dchan), dh))
        for side, (drad, dh) in zip(sides, back):
            finish(side, drad, dh)

    each_block(third_pass)
    sum_o = even.acc_o[...] + odd.acc_o[...]
    sum_o = sum_o[0 : 3 * hpad] + sum_o[3 * hpad :]
    for d in range(3):
        grad_ref[d] = sum_o[d * hpad : (d + 1) * hpad]
        slab_grad_ref[d : d + 1, :] = sum_o[d * hpad + highs - 1 : d * hpad + highs]
    for half in range(halves_n):
        sum_c = even.acc_c[half] + odd.acc_c[half]
        sum_c = sum_c[0:4] + sum_c[4:8]
        for part in range(span // LANES):
            high = half * (span // LANES) + part
            lanes = slice(part * LANES, (part + 1) * LANES)
            for d in range(3):
                grad_ref[d, high : high + 1, :] = (
                    sum_o[d * hpad + high : d * hpad + high + 1] - sum_c[d : d + 1, lanes]
                )
            energy_ref[:, high * LANES : (high + 1) * LANES] = sum_c[3:4, lanes]


def return_kernel(grad_ref, back_ref, picks_ref, own_ref, to_xm_ref, to_xp_ref, to_ym_ref, to_yp_ref):
    hpad = grad_ref.shape[1]
    z_rows = picks_ref[8:9, :]
    mask = one_hot(lax.shift_right_logical(z_rows, 7), hpad)
    low = one_hot(lax.bitwise_and(z_rows, LANES - 1), LANES).astype(bf16)
    pieces = [halves(back_ref[d : d + 1, :]) for d in range(3)]
    rows = jnp.concatenate(
        [mask * pieces[d][part] for part in range(2) for d in range(3)], axis=0
    ).astype(bf16)
    landed = dot_t(rows, low)
    landed = landed[0 : 3 * hpad] + landed[3 * hpad :]
    base = own_ref.shape[1] // 2
    for d in range(3):
        total = grad_ref[d] + landed[d * hpad : (d + 1) * hpad]
        own_ref[d] = total[0:8]
        for cycle, (p, q) in enumerate(cycle_cells):
            value = total[base + cycle : base + cycle + 1]
            if p in (0, 4):
                ref = to_xm_ref if p == 0 else to_xp_ref
                ref[q * 3 + d : q * 3 + d + 1, :] = value
            else:
                ref = to_ym_ref if q == 0 else to_yp_ref
                ref[(p - 1) * 3 + d : (p - 1) * 3 + d + 1, :] = value


def turn_kernel(from_xp_ref, from_xm_ref, to_ym_ref, to_yp_ref, send_ym_ref, send_yp_ref):
    for q, old, new in ((0, to_ym_ref, send_ym_ref), (4, to_yp_ref, send_yp_ref)):
        new[0:3, :] = old[0:3, :] + from_xm_ref[q * 3 : q * 3 + 3, :]
        new[3:6, :] = old[3:6, :]
        new[6:9, :] = old[6:9, :] + from_xp_ref[q * 3 : q * 3 + 3, :]


def force_kernel(
    own_ref, picks_ref, from_xp_ref, from_xm_ref, from_yp_ref, from_ym_ref, out_ref, rim_sum
):
    rim_sum[...] = jnp.zeros_like(rim_sum)
    for a, ref in ((2, from_xp_ref), (0, from_xm_ref)):
        for b in range(3):
            rim_sum[rim_cells.index((a, b)), 0:3, :] += ref[(b + 1) * 3 : (b + 2) * 3, :]
    for b, ref in ((2, from_yp_ref), (0, from_ym_ref)):
        for a in range(3):
            rim_sum[rim_cells.index((a, b)), 0:3, :] += ref[a * 3 : (a + 1) * 3, :]
    total = jnp.zeros((48, LANES), f32)
    for rim in range(8):
        index = picks_ref[rim : rim + 1, :]
        mask = one_hot(lax.shift_right_logical(index, 7), 8)
        low = one_hot(lax.bitwise_and(index, LANES - 1), LANES).astype(bf16)
        values = rim_sum[rim]
        pieces = [halves(values[d : d + 1, :]) for d in range(3)]
        rows = jnp.concatenate(
            [mask * pieces[d][part] for part in range(2) for d in range(3)], axis=0
        ).astype(bf16)
        total = total + dot_t(rows, low)
    total = total[0:24] + total[24:48]
    for d in range(3):
        for high in range(out_ref.shape[2] // LANES):
            value = own_ref[d, high : high + 1, :] + total[d * 8 + high : d * 8 + high + 1, :]
            out_ref[d, :, high * LANES : (high + 1) * LANES] = -value


def call(kernel, out_shape, args, scratch=(), smem=0, limit=12 * 1024 * 1024):
    vmem = pl.BlockSpec(memory_space=pltpu.VMEM)
    scalar = pl.BlockSpec(memory_space=pltpu.SMEM)
    return pl.pallas_call(
        kernel,
        out_shape=out_shape,
        in_specs=[scalar] * smem + [vmem] * (len(args) - smem),
        out_specs=jax.tree.map(lambda _: vmem, out_shape),
        scratch_shapes=list(scratch),
        compiler_params=pltpu.CompilerParams(vmem_limit_bytes=limit),
    )(*args)


def shifted(x, axis, step):
    count = lax.axis_size(axis)
    return lax.ppermute(x, axis, [((i + step) % count, i) for i in range(count)])


def swapped(x):
    count = lax.axis_size("gz")
    return lax.ppermute(x, "gz", [(i, i ^ 1) for i in range(count)])


def per_device(
    positions,
    attributes,
    edge_center,
    edge_other,
    edge_count,
    rim_rows,
    z_rows,
    w_emb,
    w_rbf,
    w_chan,
    w_lat,
    w_ten,
    w_out,
):
    pos = positions.reshape(3, 1, -1)
    attr = attributes[0, 0, 0]
    rim = rim_rows[0, 0, 0]
    zr = z_rows[0, 0]
    count = edge_count[0, 0]
    atoms, width = attr.shape
    edges = edge_center.shape[-1]
    features = w_emb.shape[1]
    chans = w_chan.shape[1]
    height = width + PARTS
    inner_len = atoms + 16 * LANES
    table = inner_len + LANES
    hpad = -(-(table // LANES) // 8) * 8
    eb = BLOCK
    span = 2 * LANES
    pairs = -(-(edges // eb + atoms // span - 1) // 2)
    slot_rows = -(-(2 * pairs * eb // LANES) // 8) * 8
    lift = (1 - 2 * lax.axis_index("gz")).astype(f32).reshape(1)
    big = 42 * 1024 * 1024

    shape = jax.ShapeDtypeStruct
    prepared = call(
        weights_kernel,
        (
            shape((features, width), bf16),
            shape((features, LANES), bf16),
            shape((features, chans), bf16),
            shape((chans, features), bf16),
            shape((features, features), bf16),
            shape((features, 3 * chans), bf16),
            shape((features + 3 * chans, features), bf16),
            shape((features, LANES), f32),
            shape((16, features), bf16),
        ),
        (
            jnp.concatenate([w_emb, w_lat, w_ten, w_chan.T], axis=0),
            jnp.concatenate([w_rbf, w_out[None]], axis=0),
        ),
        [pltpu.VMEM((LANES, features), f32)],
    )
    picks = jnp.concatenate([rim, zr], axis=0)
    own, *sent = call(
        pack_kernel,
        (shape((height, atoms), bf16),) + (shape((height, 3 * LANES), bf16),) * 4,
        (pos, attr, picks),
        [pltpu.VMEM((PARTS, atoms), f32)],
    )
    got = [
        shifted(x, "gx" if way[0] else "gy", way[0] + way[1]) for x, way in zip(sent, sides)
    ]
    lines = edges // LANES
    groups = -(-table // 256)
    ends = jnp.concatenate(
        [edge_center.reshape(lines, LANES), edge_other.reshape(lines, LANES)], axis=0
    )
    bucketed = call(
        bucket_kernel,
        (
            shape((slot_rows, LANES), jnp.int32),
            shape((slot_rows, LANES), jnp.int32),
            shape((4, LANES), jnp.int32),
        ),
        (count, ends),
        [
            pltpu.VMEM((2 * groups * lines, LANES), bf16),
            pltpu.VMEM((4 * slot_rows, edges), bf16),
            pltpu.VMEM((LANES, edges), bf16),
        ],
        smem=1,
        limit=24 * 1024 * 1024,
    )
    first, bucketed = lax.optimization_barrier((got[:2], bucketed))
    got = [*first, *got[2:]]
    centers, others, meta = bucketed
    centers = centers.reshape(-1, 1, eb)
    others = others.reshape(-1, 1, eb)
    to_plus, to_minus = call(
        corner_kernel,
        (shape((height, 2 * LANES), bf16),) * 2,
        (got[0], got[1]),
    )
    corners = [shifted(to_plus, "gx", -1), shifted(to_minus, "gx", 1)]
    corners, prepared = lax.optimization_barrier((corners, prepared))
    w_emb_t, w_rad, w_chan_r, w_chan_t, w_lat_t, w_ten_t, w_back, w_out_col, w_rbf2 = prepared
    inner, slab_send = call(
        slab_kernel,
        (shape((height, inner_len), bf16), shape((height, LANES), bf16)),
        (own, picks, *got, *corners),
        [pltpu.VMEM((PARTS, inner_len), f32)],
    )
    slab_got = swapped(slab_send)
    feat, place = call(
        embed_kernel,
        (shape((features, inner_len), bf16), shape((6, hpad, LANES), f32)),
        (inner, w_emb_t),
    )
    grads, slab_grad, energy = call(
        edge_kernel,
        (shape((3, hpad, LANES), f32), shape((3, LANES), f32), shape((1, atoms), f32)),
        (
            meta,
            lift,
            centers,
            others,
            feat,
            place,
            slab_got,
            w_emb_t,
            w_rad,
            w_chan_t,
            w_chan_r,
            w_lat_t,
            w_ten_t,
            w_back,
            w_out_col,
            w_rbf2,
        ),
        [
            pltpu.VMEM((features, (groups - 1) * 256 + WINDOW), bf16),
            pltpu.VMEM((atoms // span, features, span + LANES), bf16),
            pltpu.VMEM((6, hpad, LANES), f32),
            pltpu.VMEM((6 * hpad, LANES), bf16),
            pltpu.VMEM((48, LANES), bf16),
            pltpu.VMEM((atoms // span, 9 * chans, span), bf16),
        ]
        + [
            pltpu.VMEM((WINDOW + span + LANES, eb), bf16),
            pltpu.VMEM((features, eb), f32),
            pltpu.VMEM((pairs, span, eb), bf16),
            pltpu.VMEM((pairs, LANES, eb), bf16),
            pltpu.VMEM((pairs, features, eb), bf16),
            pltpu.VMEM((pairs, features, eb), bf16),
            pltpu.VMEM((pairs, chans, eb), f32),
            pltpu.VMEM((pairs, 16, eb), f32),
            pltpu.VMEM((pairs, features, eb), bf16),
            pltpu.VMEM((pairs, 64, eb), f32),
            pltpu.VMEM((atoms // span, 9 * chans, span), f32),
            pltpu.VMEM((6 * hpad, LANES), f32),
            pltpu.VMEM((atoms // span, 16, span), f32),
        ]
        * 2,
        smem=2,
        limit=big,
    )
    slab_back = swapped(slab_grad)
    along_x, along_y = shape((15, LANES), f32), shape((9, LANES), f32)
    own_grad, to_xm, to_xp, to_ym, to_yp = call(
        return_kernel,
        (shape((3, 8, LANES), f32), along_x, along_x, along_y, along_y),
        (grads, slab_back, picks),
    )
    from_xp, from_xm = shifted(to_xm, "gx", 1), shifted(to_xp, "gx", -1)
    to_ym, to_yp = call(turn_kernel, (along_y, along_y), (from_xp, from_xm, to_ym, to_yp))
    from_yp, from_ym = shifted(to_ym, "gy", 1), shifted(to_yp, "gy", -1)
    forces = call(
        force_kernel,
        shape((3, 1, atoms), f32),
        (own_grad, picks, from_xp, from_xm, from_yp, from_ym),
        [pltpu.VMEM((8, 8, LANES), f32)],
    )
    return (energy.reshape(1, 1, 1, atoms), forces.reshape(1, 1, 1, 3, atoms))


def solution(mesh):
    return jax.shard_map(
        per_device,
        mesh=mesh,
        in_specs=(
            P("gx", "gy", "gz", None, None),
            P("gx", "gy", "gz", None, None),
            P("gx", "gy", "gz", None),
            P("gx", "gy", "gz", None),
            P("gx", "gy", "gz"),
            P("gx", "gy", "gz", None, None),
            P("gx", "gy", "gz", None),
            P(),
            P(),
            P(),
            P(),
            P(),
            P(),
        ),
        out_specs=(P("gx", "gy", "gz", None), P("gx", "gy", "gz", None, None)),
        check_vma=False,
    )
```

```python
import collections

import jax
import jax.numpy as jnp
from jax import lax
from jax.experimental import pallas as pl
from jax.experimental.pallas import tpu as pltpu
from jax.sharding import PartitionSpec as P

f32 = jnp.float32
bf16 = jnp.bfloat16
LANES = 128
PARTS = 16
BLOCK = 512
WINDOW = 768
ROOT3 = 3.0**0.5
BANDS = (0, 1, 1, 1, 2, 2, 2, 2, 2)

rim_cells = [(0, 0), (0, 1), (0, 2), (1, 0), (1, 2), (2, 0), (2, 1), (2, 2)]
cycle_cells = [(p, q) for p in range(5) for q in range(5) if p in (0, 4) or q in (0, 4)]


def source_of(position):
    if position == 0:
        return (-1, 2)
    if position == 4:
        return (1, 0)
    return (0, position - 1)


routes = {}
for _cycle, (_p, _q) in enumerate(cycle_cells):
    (_sx, _a), (_sy, _b) = source_of(_p), source_of(_q)
    routes.setdefault((_sx, _sy), []).append((_cycle, rim_cells.index((_a, _b))))
sides = [(0, -1), (0, 1), (-1, 0), (1, 0)]


def dot(a, b):
    return lax.dot_general(a, b, (((1,), (0,)), ((), ())), preferred_element_type=f32)


def dot_t(a, b):
    return lax.dot_general(a, b, (((1,), (1,)), ((), ())), preferred_element_type=f32)


def rows_of(shape):
    return lax.broadcasted_iota(jnp.int32, shape, 0)


def one_hot(index, size):
    return jnp.where(rows_of((size, index.shape[1])) == index, 1.0, 0.0)


def halves(values):
    upper = values.astype(bf16).astype(f32)
    return upper, values - upper


def masked(hot_low, high16, value):
    mask = jnp.where(high16 == value, 1.0, 0.0).astype(bf16)
    size, lanes = hot_low.shape
    return (hot_low.reshape(size // 16, 16, lanes) * mask[None]).reshape(size, lanes)


def half_silu(x):
    half = 0.5 * x
    return (0.5 * (half * (1.0 + jnp.tanh(half)))).astype(bf16)


def pack_kernel(pos_ref, attr_ref, picks_ref, own_ref, *rest):
    sends, parts = rest[:4], rest[4]
    atoms, width = attr_ref.shape
    eye = jnp.where(
        rows_of((width, width)) == lax.broadcasted_iota(jnp.int32, (width, width), 1), 1.0, 0.0
    ).astype(bf16)
    own_ref[0:width, :] = dot_t(eye, attr_ref[...]).astype(bf16)
    parts[...] = jnp.zeros_like(parts)
    for d in range(3):
        parts[d : d + 1, :], parts[3 + d : 4 + d, :] = halves(pos_ref[d])
    own_ref[width : width + PARTS, :] = parts[...].astype(bf16)
    packed = own_ref[...]
    for rim in range(8):
        hot = one_hot(picks_ref[rim : rim + 1, :], atoms).astype(bf16)
        cell = dot(packed, hot).astype(bf16)
        for way, send in zip(sides, sends):
            for slot, (_, source) in enumerate(routes[way]):
                if source == rim:
                    send[:, slot * LANES : (slot + 1) * LANES] = cell


def corner_kernel(minus_ref, plus_ref, to_plus_ref, to_minus_ref):
    first, last = slice(0, LANES), slice(2 * LANES, 3 * LANES)
    for slot, ref in enumerate((minus_ref, plus_ref)):
        lanes = slice(slot * LANES, (slot + 1) * LANES)
        to_plus_ref[:, lanes] = ref[:, last]
        to_minus_ref[:, lanes] = ref[:, first]


def slab_kernel(own_ref, picks_ref, *rest):
    got, corners, (inner_ref, send_ref, parts) = rest[:4], rest[4:6], rest[6:]
    atoms = own_ref.shape[1]
    height = own_ref.shape[0]
    width = height - PARTS
    inner_len = inner_ref.shape[1]
    inner_ref[:, 0:atoms] = own_ref[...]
    parts[...] = jnp.zeros_like(parts)
    parts[0:6, 0:atoms] = own_ref[width:height, :].astype(f32)[0:6]
    arrivals = []
    for way, ref in zip(sides, got):
        for slot, (cycle, _) in enumerate(routes[way]):
            arrivals.append((way, ref, slot, cycle))
    for sx, ref in zip((-1, 1), corners):
        for slot, sy in enumerate((-1, 1)):
            arrivals.append(((sx, sy), ref, slot, routes[(sx, sy)][0][0]))
    for way, ref, slot, cycle in arrivals:
        lanes = slice(slot * LANES, (slot + 1) * LANES)
        into = slice(atoms + cycle * LANES, atoms + (cycle + 1) * LANES)
        inner_ref[0:width, into] = ref[0:width, lanes]
        arrived = ref[width:height, lanes].astype(f32)
        joined = arrived[0:3] + arrived[3:6]
        axis = rows_of((3, LANES))
        shift = jnp.where(axis == 0, float(way[0]), jnp.where(axis == 1, float(way[1]), 0.0))
        upper, lower = halves(joined + shift)
        parts[0:3, into] = upper
        parts[3:6, into] = lower
    inner_ref[width:height, :] = parts[...].astype(bf16)
    hot = one_hot(picks_ref[8:9, :], inner_len).astype(bf16)
    send_ref[...] = dot(inner_ref[...], hot).astype(bf16)


def unit(size):
    lanes = lax.broadcasted_iota(jnp.int32, (size, size), 1)
    return jnp.where(rows_of((size, size)) == lanes, 1.0, 0.0)


def weights_kernel(
    stacked_ref,
    small_ref,
    emb_t_ref,
    rad_ref,
    chan_ref,
    forward_ref,
    ten_t_ref,
    back_ref,
    out_ref,
    rbf_ref,
    scratch,
):
    features = stacked_ref.shape[1]
    width = emb_t_ref.shape[1]
    inner = back_ref.shape[0]
    w_emb = stacked_ref[0:width]
    w_back = stacked_ref[width : width + inner]
    w_chan_t = stacked_ref[width + inner :]
    eye = unit(features)
    eye_b = eye.astype(bf16)
    emb_t_ref[...] = dot_t(eye_b, w_emb).astype(bf16)
    chan_ref[...] = dot_t(eye_b, w_chan_t).astype(bf16)
    chans = w_chan_t.shape[0]
    forward_ref[0:chans, :] = w_chan_t
    turned = (0.5 * dot_t(eye_b, w_back)).astype(bf16)
    forward_ref[chans:, :] = turned[:, 0:features]
    ten_t_ref[...] = turned[:, features:]
    back_ref[...] = w_back
    column = jnp.sum(eye * small_ref[8:9, :], axis=1, keepdims=True)
    out_ref[...] = jnp.broadcast_to(column, out_ref.shape)
    upper, lower = halves(0.5 * small_ref[0:8, :])
    rbf_ref[...] = jnp.concatenate([upper, lower], axis=0).astype(bf16)
    scratch[...] = jnp.zeros_like(scratch)
    for start, value in ((0, upper), (8, upper), (16, lower), (24, lower)):
        scratch[start : start + 8, :] = value
    rad_ref[...] = dot_t(eye_b, scratch[...].astype(bf16)).astype(bf16)


def embed_kernel(inner_ref, w_emb_ref, feat_ref, place_ref):
    width = w_emb_ref.shape[1]
    inner_len = inner_ref.shape[1]
    for first in range(0, inner_len, 512):
        raw = dot(w_emb_ref[...], inner_ref[0:width, first : first + 512])
        feat_ref[:, first : first + 512] = half_silu(raw)
    parts = inner_ref[width:, :].astype(f32)
    place_ref[...] = jnp.zeros_like(place_ref)
    for high in range(inner_len // LANES):
        place_ref[0:6, high, :] = parts[0:6, high * LANES : (high + 1) * LANES]


def bucket_kernel(count_ref, ends_ref, center_ref, other_ref, meta_ref, marks_s, rows_s, low_s):
    lines = ends_ref.shape[0] // 2
    keys = marks_s.shape[0] // lines
    groups = keys // 2
    count = count_ref[0]
    c, o = ends_ref[0:lines, :], ends_ref[lines:, :]
    shape = (lines, LANES)
    order = rows_of(shape) * LANES + lax.broadcasted_iota(jnp.int32, shape, 1)
    key = lax.shift_right_logical(c, 8) * groups + lax.shift_right_logical(o, 8)
    key = jnp.where(order < count, key, -1)
    for k in range(keys):
        marks_s[k * lines : (k + 1) * lines, :] = jnp.where(key == k, 1.0, 0.0).astype(bf16)
    square = (LANES, LANES)
    tri = jnp.where(rows_of(square) < lax.broadcasted_iota(jnp.int32, square, 1), 1.0, 0.0)
    tri = tri.astype(bf16)
    tall = (lines, lines)
    below = jnp.where(lax.broadcasted_iota(jnp.int32, tall, 1) < rows_of(tall), 1.0, 0.0)
    marks = marks_s[...]
    inside = dot(marks, tri)
    totals = dot(marks, jnp.ones(square, bf16))
    lane = lax.broadcasted_iota(jnp.int32, shape, 1)
    by_key = jnp.zeros(shape, f32)
    for k in range(keys):
        by_key = jnp.where(lane == k, totals[k * lines : (k + 1) * lines], by_key)
    before = dot(below.astype(bf16), by_key.astype(bf16))
    everything = jnp.broadcast_to(jnp.sum(by_key, axis=0, keepdims=True), (16, LANES))
    upper, lower = halves(everything)
    start = (dot(upper.astype(bf16), tri) + dot(lower.astype(bf16), tri))[0:1]
    row_lane = lane[0:1]
    first = jnp.sum(jnp.where(row_lane < groups, everything[0:1], 0.0), axis=1, keepdims=True)
    second = jnp.sum(jnp.where(row_lane >= groups, everything[0:1], 0.0), axis=1, keepdims=True)
    first_blocks = jnp.floor((first + (BLOCK - 1)) * (1.0 / BLOCK))
    blocks = first_blocks + jnp.floor((second + (BLOCK - 1)) * (1.0 / BLOCK))
    start = start + jnp.where(row_lane >= groups, first_blocks * BLOCK - first, 0.0)
    offset = before + start
    slot = jnp.full(shape, -1.0, f32)
    for k in range(keys):
        place = inside[k * lines : (k + 1) * lines] + offset[:, k : k + 1]
        slot = jnp.where(key == k, place, slot)
    slot = slot.astype(jnp.int32)
    slot_high = lax.shift_right_arithmetic(slot, 7)
    slot_low = lax.bitwise_and(slot, LANES - 1)
    highs = center_ref.shape[0]
    values = [
        jnp.ones(shape, f32),
        lax.bitwise_and(c, 255).astype(f32),
        lax.shift_right_logical(o, 7).astype(f32),
        lax.bitwise_and(o, LANES - 1).astype(f32),
    ]
    for line in range(lines):
        lanes = slice(line * LANES, (line + 1) * LANES)
        high = one_hot(slot_high[line : line + 1], highs)
        rows_s[:, lanes] = jnp.concatenate(
            [high * value[line : line + 1] for value in values], axis=0
        ).astype(bf16)
        low_s[:, lanes] = one_hot(slot_low[line : line + 1], LANES).astype(bf16)
    placed = dot_t(rows_s[...], low_s[...])
    center = placed[highs : 2 * highs] + placed[0:highs] - 1.0
    other = placed[2 * highs : 3 * highs] * float(LANES) + placed[3 * highs :]
    center_ref[...] = center.astype(jnp.int32)
    other_ref[...] = other.astype(jnp.int32)
    group = jnp.floor(other * (1.0 / 256.0))
    none = float(groups)
    low = jnp.min(jnp.where(center >= 0.0, group, none), axis=1, keepdims=True)
    high = jnp.max(jnp.where(center >= 0.0, group, -1.0), axis=1, keepdims=True)
    block = lax.broadcasted_iota(jnp.int32, (highs, LANES), 1)
    line_of = rows_of((highs, LANES)) // (BLOCK // LANES) == block
    low = jnp.min(jnp.where(line_of, low, none), axis=0, keepdims=True)
    high = jnp.max(jnp.where(line_of, high, -1.0), axis=0, keepdims=True)
    low = jnp.where(high < 0.0, 0.0, low)
    high = jnp.where(high < 0.0, 0.0, high)
    meta_ref[0:1, :] = jnp.broadcast_to(first_blocks, (1, LANES)).astype(jnp.int32)
    meta_ref[1:2, :] = jnp.broadcast_to(blocks, (1, LANES)).astype(jnp.int32)
    meta_ref[2:3, :] = low.astype(jnp.int32)
    meta_ref[3:4, :] = high.astype(jnp.int32)


def harmonic_rows(x, y, z):
    return [
        None,
        x,
        y,
        z,
        ROOT3 * x * y,
        ROOT3 * y * z,
        ROOT3 * z * x,
        0.5 * ROOT3 * (x * x - y * y),
        0.5 * (3.0 * z * z - 1.0),
    ]


def fold8(values):
    return jnp.sum(values.reshape(values.shape[0] // 8, 8, values.shape[1]), axis=0)


FIELDS = (
    ["hot", "extra", "center_hot", "lows", "linear", "slope", "chan"]
    + ["geo", "dlat", "dharm", "tensor", "acc"]
)
Scratch = collections.namedtuple("Scratch", FIELDS)


def edge_kernel(
    meta_ref,
    lift_ref,
    centers_ref,
    others_ref,
    feat_in_ref,
    place_in_ref,
    slab_ref,
    w_emb_ref,
    w_rad_ref,
    w_forward_ref,
    w_chan_ref,
    w_ten_t_ref,
    w_back_ref,
    w_out_ref,
    w_rbf_ref,
    grad_ref,
    slab_grad_ref,
    energy_ref,
    feat,
    feat_c,
    place,
    place_b,
    tensor_b,
    *scratch,
):
    names = len(scratch) // 2
    even, odd = (Scratch(*scratch[side * names : (side + 1) * names]) for side in range(2))
    eb = centers_ref.shape[2]
    width = w_emb_ref.shape[1]
    features = feat_in_ref.shape[0]
    inner_len = feat_in_ref.shape[1]
    table = inner_len + LANES
    highs = table // LANES
    span = tensor_b.shape[2]
    halves_n = tensor_b.shape[0]
    chans = w_chan_ref.shape[1]
    hpad = place_in_ref.shape[1]
    first_blocks = meta_ref[0, 0]
    total_blocks = meta_ref[1, 0]
    pairs = total_blocks // 2

    feat[:, 0:inner_len] = feat_in_ref[...]
    raw = dot(w_emb_ref[...], slab_ref[0:width, :])
    feat[:, inner_len:table] = half_silu(raw)
    feat[:, table:] = jnp.zeros((features, feat.shape[1] - table), bf16)
    for half in range(halves_n):
        feat_c[half, :, 0:span] = feat_in_ref[:, half * span : (half + 1) * span]
        feat_c[half, :, span:] = w_rad_ref[...]
    place[...] = place_in_ref[...]
    arrived = slab_ref[width:, :].astype(f32)
    joined = arrived[0:3] + arrived[3:6]
    joined = joined + jnp.where(rows_of((3, LANES)) == 2, lift_ref[0], 0.0)
    upper, lower = halves(joined)
    place[0:3, highs - 1, :] = upper
    place[3:6, highs - 1, :] = lower
    place_b[...] = jnp.zeros_like(place_b)
    place_b[0 : 6 * hpad, 0:LANES] = place[...].reshape(6 * hpad, LANES).astype(bf16)
    place_b[6 * hpad :, LANES:] = place[:, 0:8, :].reshape(48, LANES).astype(bf16)
    for own in (even, odd):
        own.hot[WINDOW + span + 32 :, :] = jnp.zeros((LANES - 32, eb), bf16)
        for ref in (own.extra, own.tensor, own.acc):
            ref[...] = jnp.zeros_like(ref)

    def half_of(b):
        return jnp.where(b >= first_blocks, 1, 0)

    def each_block(run):
        def step(pair, carry):
            run([(even, 2 * pair, pair), (odd, 2 * pair + 1, pair)])
            return carry

        lax.fori_loop(0, pairs, step, 0)

        @pl.when(total_blocks > 2 * pairs)
        def _():
            run([(even, 2 * pairs, pairs)])

    def prepare(side):
        own_s, b, at = side
        hot = own_s.hot
        slot_c = centers_ref[b]
        o = others_ref[b]
        live = jnp.where(slot_c >= 0, 1.0, 0.0)
        c = jnp.maximum(slot_c, 0)
        half = half_of(b)
        c_high = lax.shift_right_logical(c, 7)
        o_high = lax.shift_right_logical(o, 7)
        hot_c = one_hot(lax.bitwise_and(c, LANES - 1), LANES).astype(bf16)
        hot_o = one_hot(lax.bitwise_and(o, LANES - 1), LANES).astype(bf16)
        lows = jnp.concatenate([hot_o, hot_c], axis=0)
        own_s.lows[at] = lows
        c_high16 = jnp.broadcast_to(c_high, (16, eb))
        o_high16 = jnp.broadcast_to(o_high, (16, eb))
        shift = 2 * meta_ref[2, b]
        for high in range(WINDOW // LANES):
            rows = slice(high * LANES, (high + 1) * LANES)
            hot[rows, :] = masked(hot_o, o_high16 - shift, high)
        own = jnp.concatenate(
            [masked(hot_c, c_high16, high) for high in range(span // LANES)], axis=0
        )
        own_s.center_hot[at] = own
        hot[WINDOW : WINDOW + span, :] = own

        both = dot(place_b[...], lows)
        picked = (both[0 : 3 * hpad] + both[3 * hpad : 6 * hpad]).reshape(3, hpad, eb)
        po = jnp.sum(picked * one_hot(o_high, hpad)[None], axis=1)
        picked = both[6 * hpad :]
        picked = (picked[0:24] + picked[24:48]).reshape(3, 8, eb)
        c_whole = c_high + half * (span // LANES)
        pc = jnp.sum(picked * one_hot(c_whole, 8)[None], axis=1)
        sep = po - pc
        rx, ry, rz = sep[0:1], sep[1:2], sep[2:3]
        squared = rx * rx + ry * ry + rz * rz
        inv_d = lax.rsqrt(squared + 0.25)
        dist = (squared + 0.25) * inv_d
        env = 1.0 / (1.0 + squared * squared * (1.0 / 16.0))
        x, y, z = rx * inv_d, ry * inv_d, rz * inv_d
        for row, value in enumerate((x, y, z, inv_d, dist, env, squared, live)):
            own_s.geo[at, row : row + 1, :] = value
        mu = 0.5 + 0.4 * rows_of((8, eb)).astype(f32)
        u = (dist - mu) * 2.0
        upper, lower = halves(jnp.exp(-(u * u)) * env)
        radial = jnp.concatenate([upper, lower], axis=0).astype(bf16)
        hot[WINDOW + span : WINDOW + span + 16, :] = radial
        hot[WINDOW + span + 16 : WINDOW + span + 32, :] = radial
        return x, y, z, live, own

    def window(group):
        return feat[:, pl.ds(pl.multiple_of(group * 256, 256), WINDOW)]

    def windows_of(side):
        b = side[1]
        return (meta_ref[3, b] - meta_ref[2, b]) // (WINDOW // 256) + 1

    def further_windows(side):
        own_s, b, _ = side
        windows = windows_of(side)

        @pl.when(windows > 1)
        def _():
            o = others_ref[b]
            hot_o = one_hot(lax.bitwise_and(o, LANES - 1), LANES).astype(bf16)
            o_high16 = jnp.broadcast_to(lax.shift_right_logical(o, 7), (16, eb))

            def add(index, carry):
                group = meta_ref[2, b] + index * (WINDOW // 256)
                hot = jnp.concatenate(
                    [
                        masked(hot_o, o_high16 - 2 * group, high)
                        for high in range(WINDOW // LANES)
                    ],
                    axis=0,
                )
                own_s.extra[...] += dot(window(group), hot)
                return carry

            lax.fori_loop(1, windows, add, 0)

    def clear_windows(side):
        @pl.when(windows_of(side) > 1)
        def _():
            side[0].extra[...] = jnp.zeros_like(side[0].extra)

    def mix(side):
        own_s, b, _ = side
        mixed = dot(window(meta_ref[2, b]), own_s.hot[0:WINDOW, :])
        mixed = mixed + dot(feat_c[half_of(b)], own_s.hot[WINDOW:, :])
        return mixed + own_s.extra[...]

    def activate(side, mixed):
        own_s, _, at = side
        up = 1.0 + jnp.tanh(mixed)
        value = mixed * up
        latent = value.astype(bf16)
        own_s.slope[at] = (up + value * (2.0 - up)).astype(bf16)
        return latent

    def spread(side, latent, geo):
        own_s, _, at = side
        x, y, z, live, _ = geo
        both = dot(w_forward_ref[...], latent)
        own_s.linear[at] = both[chans:]
        chan = both[0:chans] * live
        own_s.chan[at] = chan
        return jnp.concatenate(
            [
                (chan if h is None else chan * h).astype(bf16)
                for h in harmonic_rows(x, y, z)
            ],
            axis=0,
        )

    def gather_tensor(side):
        own_s, b, at = side
        return dot(tensor_b[half_of(b)], own_s.center_hot[at])

    def add_tensor(side, products, hot):
        own_s, b, _ = side
        own_s.tensor[half_of(b)] += dot_t(products, hot)

    def first_pass(sides):
        geos, mixed = [], []
        for side in sides:
            further_windows(side)
        for side in sides:
            geos.append(prepare(side))
            mixed.append(mix(side))
        products = []
        for side, geo, values in zip(sides, geos, mixed):
            products.append(spread(side, activate(side, values), geo))
        for side, geo, values in zip(sides, geos, products):
            add_tensor(side, values, geo[4])
        for side in sides:
            clear_windows(side)

    each_block(first_pass)
    tensor_b[...] = (0.125 * (even.tensor[...] + odd.tensor[...])).astype(bf16)
    for own in (even, odd):
        own.tensor[...] = jnp.zeros_like(own.tensor)

    def invariants(side, gathered):
        geo = side[0].geo[side[2]]
        harm = harmonic_rows(geo[0:1], geo[1:2], geo[2:3])
        parts = [gathered[m * chans : (m + 1) * chans] for m in range(9)]
        bands = [parts[0], None, None]
        for m in range(1, 9):
            term = parts[m] * harm[m]
            band = BANDS[m]
            bands[band] = term if bands[band] is None else bands[band] + term
        return jnp.concatenate([band.astype(bf16) for band in bands], axis=0)

    def hidden(side, invariant):
        return side[0].linear[side[2]] + dot(w_ten_t_ref[...], invariant)

    def readout(side, pre):
        own_s, _, at = side
        geo = own_s.geo[at]
        up = 1.0 + jnp.tanh(pre)
        value = pre * up
        weight = jnp.concatenate([w_out_ref[...]] * (eb // LANES), axis=1)
        own_s.geo[at, 8:9, :] = jnp.sum(value * weight, axis=0, keepdims=True)
        scale = 0.5 * geo[5:6] * geo[7:8]
        return ((up + value * (2.0 - up)) * (weight * scale)).astype(bf16)

    def unfold(side, back, gathered):
        own_s, _, at = side
        geo = own_s.geo[at]
        harm = harmonic_rows(geo[0:1], geo[1:2], geo[2:3])
        own_s.dlat[at] = back[0:features].astype(bf16)
        dbands = [
            back[features + band * chans : features + (band + 1) * chans] for band in range(3)
        ]
        for m in range(1, 9):
            part = gathered[m * chans : (m + 1) * chans]
            own_s.dharm[at, (m - 1) * 8 : m * 8, :] = fold8(dbands[BANDS[m]] * part)
        return jnp.concatenate(
            [
                (dbands[BANDS[m]] if harm[m] is None else dbands[BANDS[m]] * harm[m]).astype(bf16)
                for m in range(9)
            ],
            axis=0,
        )

    def second_pass(sides):
        gathered = [gather_tensor(side) for side in sides]
        pre = [hidden(side, invariants(side, g)) for side, g in zip(sides, gathered)]
        back = [dot(w_back_ref[...], readout(side, values)) for side, values in zip(sides, pre)]
        for side, values, g in zip(sides, back, gathered):
            add_tensor(side, unfold(side, values, g), side[0].center_hot[side[2]])

    each_block(second_pass)
    tensor_b[...] = (0.125 * (even.tensor[...] + odd.tensor[...])).astype(bf16)

    def channels_back(side, gathered):
        own_s, _, at = side
        geo = own_s.geo[at]
        harm = harmonic_rows(geo[0:1], geo[1:2], geo[2:3])
        chan = own_s.chan[at]
        dchan = gathered[0:chans]
        dh = [None]
        for m in range(1, 9):
            part = gathered[m * chans : (m + 1) * chans]
            dchan = dchan + part * harm[m]
            total = own_s.dharm[at, (m - 1) * 8 : m * 8, :] + fold8(part * chan)
            dh.append(jnp.sum(total, axis=0, keepdims=True))
        return (dchan * geo[7:8]).astype(bf16), dh

    def radial_back(side, dchan):
        own_s, _, at = side
        dlat = own_s.dlat[at] + dot(w_chan_ref[...], dchan).astype(bf16)
        drad = dot(w_rbf_ref[...], dlat * own_s.slope[at])
        return drad[0:8] + drad[8:16]

    def finish(side, drad, dh):
        own_s, b, at = side
        geo = own_s.geo[at]
        x, y, z = geo[0:1], geo[1:2], geo[2:3]
        inv_d, dist, env, squared = geo[3:4], geo[4:5], geo[5:6], geo[6:7]
        live, summed = geo[7:8], geo[8:9]
        mu = 0.5 + 0.4 * rows_of((8, eb)).astype(f32)
        u = (dist - mu) * 2.0
        weighted = drad * jnp.exp(-(u * u))
        denv = jnp.sum(weighted, axis=0, keepdims=True) + live * summed
        ddist = -4.0 * env * jnp.sum(weighted * u, axis=0, keepdims=True)
        dx = dh[1] + ROOT3 * (y * dh[4] + z * dh[6] + x * dh[7])
        dy = dh[2] + ROOT3 * (x * dh[4] + z * dh[5] - y * dh[7])
        dz = dh[3] + ROOT3 * (y * dh[5] + x * dh[6]) + 3.0 * z * dh[8]
        ddist = ddist - (dx * x + dy * y + dz * z) * inv_d
        dsq = denv * (env * env * squared * -0.125) + ddist * (0.5 * inv_d)
        both = 2.0 * dsq * dist
        gs = [dx * inv_d + both * x, dy * inv_d + both * y, dz * inv_d + both * z]
        energy = summed * env * live

        o_high = lax.shift_right_logical(others_ref[b], 7)
        mask_o = one_hot(o_high, hpad)
        split = [halves(g) for g in gs]
        rows_o = jnp.concatenate(
            [mask_o * split[d][part] for part in range(2) for d in range(3)], axis=0
        ).astype(bf16)
        split.append(halves(energy))
        values = jnp.concatenate(
            [split[d][part] for part in range(2) for d in range(4)], axis=0
        )
        c_high = lax.shift_right_arithmetic(centers_ref[b], 7)
        rows_c = jnp.concatenate(
            [
                values * jnp.where(c_high == high, 1.0, 0.0)
                for high in range(span // LANES)
            ],
            axis=0,
        ).astype(bf16)
        rows = jnp.concatenate([rows_o, rows_c], axis=0)
        own_s.acc[half_of(b)] += dot_t(rows, own_s.lows[at])

    def third_pass(sides):
        gathered = [gather_tensor(side) for side in sides]
        back = []
        for side, g in zip(sides, gathered):
            dchan, dh = channels_back(side, g)
            back.append((radial_back(side, dchan), dh))
        for side, (drad, dh) in zip(sides, back):
            finish(side, drad, dh)

    each_block(third_pass)
    acc = [even.acc[half] + odd.acc[half] for half in range(halves_n)]
    sum_o = sum(value[0 : 6 * hpad, 0:LANES] for value in acc)
    sum_o = sum_o[0 : 3 * hpad] + sum_o[3 * hpad :]
    for d in range(3):
        grad_ref[d] = sum_o[d * hpad : (d + 1) * hpad]
        slab_grad_ref[d : d + 1, :] = sum_o[d * hpad + highs - 1 : d * hpad + highs]
    for half in range(halves_n):
        for part in range(span // LANES):
            high = half * (span // LANES) + part
            base = 6 * hpad + part * 8
            sum_c = acc[half][base : base + 4, LANES:] + acc[half][base + 4 : base + 8, LANES:]
            for d in range(3):
                grad_ref[d, high : high + 1, :] = (
                    sum_o[d * hpad + high : d * hpad + high + 1] - sum_c[d : d + 1]
                )
            energy_ref[:, high * LANES : (high + 1) * LANES] = sum_c[3:4]


def return_kernel(grad_ref, back_ref, picks_ref, own_ref, to_xm_ref, to_xp_ref, to_ym_ref, to_yp_ref):
    hpad = grad_ref.shape[1]
    z_rows = picks_ref[8:9, :]
    mask = one_hot(lax.shift_right_logical(z_rows, 7), hpad)
    low = one_hot(lax.bitwise_and(z_rows, LANES - 1), LANES).astype(bf16)
    pieces = [halves(back_ref[d : d + 1, :]) for d in range(3)]
    rows = jnp.concatenate(
        [mask * pieces[d][part] for part in range(2) for d in range(3)], axis=0
    ).astype(bf16)
    landed = dot_t(rows, low)
    landed = landed[0 : 3 * hpad] + landed[3 * hpad :]
    base = own_ref.shape[1] // 2
    for d in range(3):
        total = grad_ref[d] + landed[d * hpad : (d + 1) * hpad]
        own_ref[d] = total[0:8]
        for cycle, (p, q) in enumerate(cycle_cells):
            value = total[base + cycle : base + cycle + 1]
            if p in (0, 4):
                ref = to_xm_ref if p == 0 else to_xp_ref
                ref[q * 3 + d : q * 3 + d + 1, :] = value
            else:
                ref = to_ym_ref if q == 0 else to_yp_ref
                ref[(p - 1) * 3 + d : (p - 1) * 3 + d + 1, :] = value


def turn_kernel(from_xp_ref, from_xm_ref, to_ym_ref, to_yp_ref, send_ym_ref, send_yp_ref):
    for q, old, new in ((0, to_ym_ref, send_ym_ref), (4, to_yp_ref, send_yp_ref)):
        new[0:3, :] = old[0:3, :] + from_xm_ref[q * 3 : q * 3 + 3, :]
        new[3:6, :] = old[3:6, :]
        new[6:9, :] = old[6:9, :] + from_xp_ref[q * 3 : q * 3 + 3, :]


def force_kernel(
    own_ref, picks_ref, from_xp_ref, from_xm_ref, from_yp_ref, from_ym_ref, out_ref, rim_sum
):
    rim_sum[...] = jnp.zeros_like(rim_sum)
    for a, ref in ((2, from_xp_ref), (0, from_xm_ref)):
        for b in range(3):
            rim_sum[rim_cells.index((a, b)), 0:3, :] += ref[(b + 1) * 3 : (b + 2) * 3, :]
    for b, ref in ((2, from_yp_ref), (0, from_ym_ref)):
        for a in range(3):
            rim_sum[rim_cells.index((a, b)), 0:3, :] += ref[a * 3 : (a + 1) * 3, :]
    total = jnp.zeros((48, LANES), f32)
    for rim in range(8):
        index = picks_ref[rim : rim + 1, :]
        mask = one_hot(lax.shift_right_logical(index, 7), 8)
        low = one_hot(lax.bitwise_and(index, LANES - 1), LANES).astype(bf16)
        values = rim_sum[rim]
        pieces = [halves(values[d : d + 1, :]) for d in range(3)]
        rows = jnp.concatenate(
            [mask * pieces[d][part] for part in range(2) for d in range(3)], axis=0
        ).astype(bf16)
        total = total + dot_t(rows, low)
    total = total[0:24] + total[24:48]
    for d in range(3):
        for high in range(out_ref.shape[2] // LANES):
            value = own_ref[d, high : high + 1, :] + total[d * 8 + high : d * 8 + high + 1, :]
            out_ref[d, :, high * LANES : (high + 1) * LANES] = -value


def call(kernel, out_shape, args, scratch=(), smem=0, limit=12 * 1024 * 1024):
    vmem = pl.BlockSpec(memory_space=pltpu.VMEM)
    scalar = pl.BlockSpec(memory_space=pltpu.SMEM)
    return pl.pallas_call(
        kernel,
        out_shape=out_shape,
        in_specs=[scalar] * smem + [vmem] * (len(args) - smem),
        out_specs=jax.tree.map(lambda _: vmem, out_shape),
        scratch_shapes=list(scratch),
        compiler_params=pltpu.CompilerParams(vmem_limit_bytes=limit),
    )(*args)


def shifted(x, axis, step):
    count = lax.axis_size(axis)
    return lax.ppermute(x, axis, [((i + step) % count, i) for i in range(count)])


def swapped(x):
    count = lax.axis_size("gz")
    return lax.ppermute(x, "gz", [(i, i ^ 1) for i in range(count)])


def per_device(
    positions,
    attributes,
    edge_center,
    edge_other,
    edge_count,
    rim_rows,
    z_rows,
    w_emb,
    w_rbf,
    w_chan,
    w_lat,
    w_ten,
    w_out,
):
    pos = positions.reshape(3, 1, -1)
    attr = attributes[0, 0, 0]
    rim = rim_rows[0, 0, 0]
    zr = z_rows[0, 0]
    count = edge_count[0, 0]
    atoms, width = attr.shape
    edges = edge_center.shape[-1]
    features = w_emb.shape[1]
    chans = w_chan.shape[1]
    height = width + PARTS
    inner_len = atoms + 16 * LANES
    table = inner_len + LANES
    hpad = -(-(table // LANES) // 8) * 8
    eb = BLOCK
    span = 2 * LANES
    pairs = -(-(edges // eb + atoms // span - 1) // 2)
    slot_rows = -(-(2 * pairs * eb // LANES) // 8) * 8
    lift = (1 - 2 * lax.axis_index("gz")).astype(f32).reshape(1)
    big = 44 * 1024 * 1024

    shape = jax.ShapeDtypeStruct
    picks = jnp.concatenate([rim, zr], axis=0)
    own, *sent = call(
        pack_kernel,
        (shape((height, atoms), bf16),) + (shape((height, 3 * LANES), bf16),) * 4,
        (pos, attr, picks),
        [pltpu.VMEM((PARTS, atoms), f32)],
    )
    got = [
        shifted(x, "gx" if way[0] else "gy", way[0] + way[1]) for x, way in zip(sent, sides)
    ]
    lines = edges // LANES
    groups = -(-table // 256)
    ends = jnp.concatenate(
        [edge_center.reshape(lines, LANES), edge_other.reshape(lines, LANES)], axis=0
    )
    bucketed = call(
        bucket_kernel,
        (
            shape((slot_rows, LANES), jnp.int32),
            shape((slot_rows, LANES), jnp.int32),
            shape((4, LANES), jnp.int32),
        ),
        (count, ends),
        [
            pltpu.VMEM((2 * groups * lines, LANES), bf16),
            pltpu.VMEM((4 * slot_rows, edges), bf16),
            pltpu.VMEM((LANES, edges), bf16),
        ],
        smem=1,
        limit=24 * 1024 * 1024,
    )
    first, bucketed = lax.optimization_barrier((got[:2], bucketed))
    got = [*first, *got[2:]]
    centers, others, meta = bucketed
    centers = centers.reshape(-1, 1, eb)
    others = others.reshape(-1, 1, eb)
    to_plus, to_minus = call(
        corner_kernel,
        (shape((height, 2 * LANES), bf16),) * 2,
        (got[0], got[1]),
    )
    w_emb, w_rbf, to_plus = lax.optimization_barrier((w_emb, w_rbf, to_plus))
    prepared = call(
        weights_kernel,
        (
            shape((features, width), bf16),
            shape((features, LANES), bf16),
            shape((features, chans), bf16),
            shape((chans + features, features), bf16),
            shape((features, 3 * chans), bf16),
            shape((features + 3 * chans, features), bf16),
            shape((features, LANES), f32),
            shape((16, features), bf16),
        ),
        (
            jnp.concatenate([w_emb, w_lat, w_ten, w_chan.T], axis=0),
            jnp.concatenate([w_rbf, w_out[None]], axis=0),
        ),
        [pltpu.VMEM((LANES, features), f32)],
    )
    corners = [shifted(to_plus, "gx", -1), shifted(to_minus, "gx", 1)]
    corners, prepared = lax.optimization_barrier((corners, prepared))
    w_emb_t, w_rad, w_chan_r, w_forward, w_ten_t, w_back, w_out_col, w_rbf2 = prepared
    inner, slab_send = call(
        slab_kernel,
        (shape((height, inner_len), bf16), shape((height, LANES), bf16)),
        (own, picks, *got, *corners),
        [pltpu.VMEM((PARTS, inner_len), f32)],
    )
    slab_got = swapped(slab_send)
    feat, place = call(
        embed_kernel,
        (shape((features, inner_len), bf16), shape((6, hpad, LANES), f32)),
        (inner, w_emb_t),
    )
    grads, slab_grad, energy = call(
        edge_kernel,
        (shape((3, hpad, LANES), f32), shape((3, LANES), f32), shape((1, atoms), f32)),
        (
            meta,
            lift,
            centers,
            others,
            feat,
            place,
            slab_got,
            w_emb_t,
            w_rad,
            w_forward,
            w_chan_r,
            w_ten_t,
            w_back,
            w_out_col,
            w_rbf2,
        ),
        [
            pltpu.VMEM((features, (groups - 1) * 256 + WINDOW), bf16),
            pltpu.VMEM((atoms // span, features, span + LANES), bf16),
            pltpu.VMEM((6, hpad, LANES), f32),
            pltpu.VMEM((6 * hpad + 48, 2 * LANES), bf16),
            pltpu.VMEM((atoms // span, 9 * chans, span), bf16),
        ]
        + [
            pltpu.VMEM((WINDOW + span + LANES, eb), bf16),
            pltpu.VMEM((features, eb), f32),
            pltpu.VMEM((pairs, span, eb), bf16),
            pltpu.VMEM((pairs, 2 * LANES, eb), bf16),
            pltpu.VMEM((pairs, features, eb), f32),
            pltpu.VMEM((pairs, features, eb), bf16),
            pltpu.VMEM((pairs, chans, eb), f32),
            pltpu.VMEM((pairs, 16, eb), f32),
            pltpu.VMEM((pairs, features, eb), bf16),
            pltpu.VMEM((pairs, 64, eb), f32),
            pltpu.VMEM((atoms // span, 9 * chans, span), f32),
            pltpu.VMEM((atoms // span, 6 * hpad + 8 * (span // LANES), 2 * LANES), f32),
        ]
        * 2,
        smem=2,
        limit=big,
    )
    slab_back = swapped(slab_grad)
    along_x, along_y = shape((15, LANES), f32), shape((9, LANES), f32)
    own_grad, to_xm, to_xp, to_ym, to_yp = call(
        return_kernel,
        (shape((3, 8, LANES), f32), along_x, along_x, along_y, along_y),
        (grads, slab_back, picks),
    )
    from_xp, from_xm = shifted(to_xm, "gx", 1), shifted(to_xp, "gx", -1)
    to_ym, to_yp = call(turn_kernel, (along_y, along_y), (from_xp, from_xm, to_ym, to_yp))
    from_yp, from_ym = shifted(to_ym, "gy", 1), shifted(to_yp, "gy", -1)
    forces = call(
        force_kernel,
        shape((3, 1, atoms), f32),
        (own_grad, picks, from_xp, from_xm, from_yp, from_ym),
        [pltpu.VMEM((8, 8, LANES), f32)],
    )
    return (energy.reshape(1, 1, 1, atoms), forces.reshape(1, 1, 1, 3, atoms))


def solution(mesh):
    return jax.shard_map(
        per_device,
        mesh=mesh,
        in_specs=(
            P("gx", "gy", "gz", None, None),
            P("gx", "gy", "gz", None, None),
            P("gx", "gy", "gz", None),
            P("gx", "gy", "gz", None),
            P("gx", "gy", "gz"),
            P("gx", "gy", "gz", None, None),
            P("gx", "gy", "gz", None),
            P(),
            P(),
            P(),
            P(),
            P(),
            P(),
        ),
        out_specs=(P("gx", "gy", "gz", None), P("gx", "gy", "gz", None, None)),
        check_vma=False,
    )
```

```python
import collections

import jax
import jax.numpy as jnp
from jax import lax
from jax.experimental import pallas as pl
from jax.experimental.pallas import tpu as pltpu
from jax.sharding import PartitionSpec as P

f32 = jnp.float32
bf16 = jnp.bfloat16
LANES = 128
PARTS = 16
BLOCK = 512
WINDOW = 768
ROOT3 = 3.0**0.5
BANDS = (0, 1, 1, 1, 2, 2, 2, 2, 2)

rim_cells = [(0, 0), (0, 1), (0, 2), (1, 0), (1, 2), (2, 0), (2, 1), (2, 2)]
cycle_cells = [(p, q) for p in range(5) for q in range(5) if p in (0, 4) or q in (0, 4)]


def source_of(position):
    if position == 0:
        return (-1, 2)
    if position == 4:
        return (1, 0)
    return (0, position - 1)


routes = {}
for _cycle, (_p, _q) in enumerate(cycle_cells):
    (_sx, _a), (_sy, _b) = source_of(_p), source_of(_q)
    routes.setdefault((_sx, _sy), []).append((_cycle, rim_cells.index((_a, _b))))
sides = [(0, -1), (0, 1), (-1, 0), (1, 0)]


def dot(a, b):
    return lax.dot_general(a, b, (((1,), (0,)), ((), ())), preferred_element_type=f32)


def dot_t(a, b):
    return lax.dot_general(a, b, (((1,), (1,)), ((), ())), preferred_element_type=f32)


def rows_of(shape):
    return lax.broadcasted_iota(jnp.int32, shape, 0)


def one_hot(index, size):
    return jnp.where(rows_of((size, index.shape[1])) == index, 1.0, 0.0)


def halves(values):
    upper = values.astype(bf16).astype(f32)
    return upper, values - upper


def masked(hot_low, high16, value):
    mask = jnp.where(high16 == value, 1.0, 0.0).astype(bf16)
    size, lanes = hot_low.shape
    return (hot_low.reshape(size // 16, 16, lanes) * mask[None]).reshape(size, lanes)


def half_silu(x):
    half = 0.5 * x
    return (0.5 * (half * (1.0 + jnp.tanh(half)))).astype(bf16)


def pack_kernel(pos_ref, attr_ref, picks_ref, own_ref, *rest):
    sends, parts = rest[:4], rest[4]
    atoms, width = attr_ref.shape
    eye = jnp.where(
        rows_of((width, width)) == lax.broadcasted_iota(jnp.int32, (width, width), 1), 1.0, 0.0
    ).astype(bf16)
    own_ref[0:width, :] = dot_t(eye, attr_ref[...]).astype(bf16)
    parts[...] = jnp.zeros_like(parts)
    for d in range(3):
        parts[d : d + 1, :], parts[3 + d : 4 + d, :] = halves(pos_ref[d])
    own_ref[width : width + PARTS, :] = parts[...].astype(bf16)
    packed = own_ref[...]
    for rim in range(8):
        hot = one_hot(picks_ref[rim : rim + 1, :], atoms).astype(bf16)
        cell = dot(packed, hot).astype(bf16)
        for way, send in zip(sides, sends):
            for slot, (_, source) in enumerate(routes[way]):
                if source == rim:
                    send[:, slot * LANES : (slot + 1) * LANES] = cell


def corner_kernel(minus_ref, plus_ref, to_plus_ref, to_minus_ref):
    first, last = slice(0, LANES), slice(2 * LANES, 3 * LANES)
    for slot, ref in enumerate((minus_ref, plus_ref)):
        lanes = slice(slot * LANES, (slot + 1) * LANES)
        to_plus_ref[:, lanes] = ref[:, last]
        to_minus_ref[:, lanes] = ref[:, first]


def slab_kernel(own_ref, picks_ref, *rest):
    got, corners, (inner_ref, send_ref, parts) = rest[:4], rest[4:6], rest[6:]
    atoms = own_ref.shape[1]
    height = own_ref.shape[0]
    width = height - PARTS
    inner_len = inner_ref.shape[1]
    inner_ref[:, 0:atoms] = own_ref[...]
    parts[...] = jnp.zeros_like(parts)
    parts[0:6, 0:atoms] = own_ref[width:height, :].astype(f32)[0:6]
    arrivals = []
    for way, ref in zip(sides, got):
        for slot, (cycle, _) in enumerate(routes[way]):
            arrivals.append((way, ref, slot, cycle))
    for sx, ref in zip((-1, 1), corners):
        for slot, sy in enumerate((-1, 1)):
            arrivals.append(((sx, sy), ref, slot, routes[(sx, sy)][0][0]))
    for way, ref, slot, cycle in arrivals:
        lanes = slice(slot * LANES, (slot + 1) * LANES)
        into = slice(atoms + cycle * LANES, atoms + (cycle + 1) * LANES)
        inner_ref[0:width, into] = ref[0:width, lanes]
        arrived = ref[width:height, lanes].astype(f32)
        joined = arrived[0:3] + arrived[3:6]
        axis = rows_of((3, LANES))
        shift = jnp.where(axis == 0, float(way[0]), jnp.where(axis == 1, float(way[1]), 0.0))
        upper, lower = halves(joined + shift)
        parts[0:3, into] = upper
        parts[3:6, into] = lower
    inner_ref[width:height, :] = parts[...].astype(bf16)
    hot = one_hot(picks_ref[8:9, :], inner_len).astype(bf16)
    send_ref[...] = dot(inner_ref[...], hot).astype(bf16)


def unit(size):
    lanes = lax.broadcasted_iota(jnp.int32, (size, size), 1)
    return jnp.where(rows_of((size, size)) == lanes, 1.0, 0.0)


def weights_kernel(
    stacked_ref,
    small_ref,
    emb_t_ref,
    rad_ref,
    chan_ref,
    w_chan_t_ref,
    hidden_ref,
    back_ref,
    out_ref,
    rbf_ref,
    scratch,
):
    features = stacked_ref.shape[1]
    width = emb_t_ref.shape[1]
    inner = back_ref.shape[0]
    w_emb = stacked_ref[0:width]
    w_back = stacked_ref[width : width + inner]
    w_chan_t = stacked_ref[width + inner :]
    eye = unit(features)
    eye_b = eye.astype(bf16)
    emb_t_ref[...] = dot_t(eye_b, w_emb).astype(bf16)
    chan_ref[...] = dot_t(eye_b, w_chan_t).astype(bf16)
    w_chan_t_ref[...] = w_chan_t
    turned = (0.5 * dot_t(eye_b, w_back)).astype(bf16)
    hidden_ref[...] = turned
    back_ref[...] = w_back
    column = jnp.sum(eye * small_ref[8:9, :], axis=1, keepdims=True)
    out_ref[...] = jnp.broadcast_to(column, out_ref.shape)
    upper, lower = halves(0.5 * small_ref[0:8, :])
    rbf_ref[...] = jnp.concatenate([upper, lower], axis=0).astype(bf16)
    scratch[...] = jnp.zeros_like(scratch)
    for start, value in ((0, upper), (8, upper), (16, lower), (24, lower)):
        scratch[start : start + 8, :] = value
    rad_ref[...] = dot_t(eye_b, scratch[...].astype(bf16)).astype(bf16)


def embed_kernel(inner_ref, w_emb_ref, feat_ref, place_ref):
    width = w_emb_ref.shape[1]
    inner_len = inner_ref.shape[1]
    for first in range(0, inner_len, 512):
        raw = dot(w_emb_ref[...], inner_ref[0:width, first : first + 512])
        feat_ref[:, first : first + 512] = half_silu(raw)
    parts = inner_ref[width:, :].astype(f32)
    place_ref[...] = jnp.zeros_like(place_ref)
    for high in range(inner_len // LANES):
        place_ref[0:6, high, :] = parts[0:6, high * LANES : (high + 1) * LANES]


def bucket_kernel(count_ref, ends_ref, center_ref, other_ref, meta_ref, marks_s, rows_s, low_s):
    lines = ends_ref.shape[0] // 2
    keys = marks_s.shape[0] // lines
    groups = keys // 2
    count = count_ref[0]
    c, o = ends_ref[0:lines, :], ends_ref[lines:, :]
    shape = (lines, LANES)
    order = rows_of(shape) * LANES + lax.broadcasted_iota(jnp.int32, shape, 1)
    key = lax.shift_right_logical(c, 8) * groups + lax.shift_right_logical(o, 8)
    key = jnp.where(order < count, key, -1)
    for k in range(keys):
        marks_s[k * lines : (k + 1) * lines, :] = jnp.where(key == k, 1.0, 0.0).astype(bf16)
    square = (LANES, LANES)
    tri = jnp.where(rows_of(square) < lax.broadcasted_iota(jnp.int32, square, 1), 1.0, 0.0)
    tri = tri.astype(bf16)
    tall = (lines, lines)
    below = jnp.where(lax.broadcasted_iota(jnp.int32, tall, 1) < rows_of(tall), 1.0, 0.0)
    marks = marks_s[...]
    inside = dot(marks, tri)
    totals = dot(marks, jnp.ones(square, bf16))
    lane = lax.broadcasted_iota(jnp.int32, shape, 1)
    by_key = jnp.zeros(shape, f32)
    for k in range(keys):
        by_key = jnp.where(lane == k, totals[k * lines : (k + 1) * lines], by_key)
    before = dot(below.astype(bf16), by_key.astype(bf16))
    everything = jnp.broadcast_to(jnp.sum(by_key, axis=0, keepdims=True), (16, LANES))
    upper, lower = halves(everything)
    start = (dot(upper.astype(bf16), tri) + dot(lower.astype(bf16), tri))[0:1]
    row_lane = lane[0:1]
    first = jnp.sum(jnp.where(row_lane < groups, everything[0:1], 0.0), axis=1, keepdims=True)
    second = jnp.sum(jnp.where(row_lane >= groups, everything[0:1], 0.0), axis=1, keepdims=True)
    first_blocks = jnp.floor((first + (BLOCK - 1)) * (1.0 / BLOCK))
    blocks = first_blocks + jnp.floor((second + (BLOCK - 1)) * (1.0 / BLOCK))
    start = start + jnp.where(row_lane >= groups, first_blocks * BLOCK - first, 0.0)
    offset = before + start
    slot = jnp.full(shape, -1.0, f32)
    for k in range(keys):
        place = inside[k * lines : (k + 1) * lines] + offset[:, k : k + 1]
        slot = jnp.where(key == k, place, slot)
    slot = slot.astype(jnp.int32)
    slot_high = lax.shift_right_arithmetic(slot, 7)
    slot_low = lax.bitwise_and(slot, LANES - 1)
    highs = center_ref.shape[0]
    values = [
        jnp.ones(shape, f32),
        lax.bitwise_and(c, 255).astype(f32),
        lax.shift_right_logical(o, 7).astype(f32),
        lax.bitwise_and(o, LANES - 1).astype(f32),
    ]
    for line in range(lines):
        lanes = slice(line * LANES, (line + 1) * LANES)
        high = one_hot(slot_high[line : line + 1], highs)
        rows_s[:, lanes] = jnp.concatenate(
            [high * value[line : line + 1] for value in values], axis=0
        ).astype(bf16)
        low_s[:, lanes] = one_hot(slot_low[line : line + 1], LANES).astype(bf16)
    placed = dot_t(rows_s[...], low_s[...])
    center = placed[highs : 2 * highs] + placed[0:highs] - 1.0
    other = placed[2 * highs : 3 * highs] * float(LANES) + placed[3 * highs :]
    center_ref[...] = center.astype(jnp.int32)
    other_ref[...] = other.astype(jnp.int32)
    group = jnp.floor(other * (1.0 / 256.0))
    none = float(groups)
    low = jnp.min(jnp.where(center >= 0.0, group, none), axis=1, keepdims=True)
    high = jnp.max(jnp.where(center >= 0.0, group, -1.0), axis=1, keepdims=True)
    block = lax.broadcasted_iota(jnp.int32, (highs, LANES), 1)
    line_of = rows_of((highs, LANES)) // (BLOCK // LANES) == block
    low = jnp.min(jnp.where(line_of, low, none), axis=0, keepdims=True)
    high = jnp.max(jnp.where(line_of, high, -1.0), axis=0, keepdims=True)
    low = jnp.where(high < 0.0, 0.0, low)
    high = jnp.where(high < 0.0, 0.0, high)
    meta_ref[0:1, :] = jnp.broadcast_to(first_blocks, (1, LANES)).astype(jnp.int32)
    meta_ref[1:2, :] = jnp.broadcast_to(blocks, (1, LANES)).astype(jnp.int32)
    meta_ref[2:3, :] = low.astype(jnp.int32)
    meta_ref[3:4, :] = high.astype(jnp.int32)


def harmonic_rows(x, y, z):
    return [
        None,
        x,
        y,
        z,
        ROOT3 * x * y,
        ROOT3 * y * z,
        ROOT3 * z * x,
        0.5 * ROOT3 * (x * x - y * y),
        0.5 * (3.0 * z * z - 1.0),
    ]


def fold8(values):
    return jnp.sum(values.reshape(values.shape[0] // 8, 8, values.shape[1]), axis=0)


FIELDS = (
    ["hot", "extra", "center_hot", "lows", "latent", "slope", "chan"]
    + ["geo", "res", "dlat", "dharm", "tensor", "acc"]
)
Scratch = collections.namedtuple("Scratch", FIELDS)


def edge_kernel(
    meta_ref,
    lift_ref,
    centers_ref,
    others_ref,
    feat_in_ref,
    place_in_ref,
    slab_ref,
    w_emb_ref,
    w_rad_ref,
    w_chan_t_ref,
    w_chan_ref,
    w_hidden_ref,
    w_back_ref,
    w_out_ref,
    w_rbf_ref,
    grad_ref,
    slab_grad_ref,
    energy_ref,
    feat,
    feat_c,
    place,
    place_b,
    tensor_b,
    *scratch,
):
    names = len(scratch) // 2
    even, odd = (Scratch(*scratch[side * names : (side + 1) * names]) for side in range(2))
    eb = centers_ref.shape[2]
    width = w_emb_ref.shape[1]
    features = feat_in_ref.shape[0]
    inner_len = feat_in_ref.shape[1]
    table = inner_len + LANES
    highs = table // LANES
    span = tensor_b.shape[2]
    halves_n = tensor_b.shape[0]
    chans = w_chan_ref.shape[1]
    hpad = place_in_ref.shape[1]
    first_blocks = meta_ref[0, 0]
    total_blocks = meta_ref[1, 0]
    pairs = total_blocks // 2

    feat[:, 0:inner_len] = feat_in_ref[...]
    raw = dot(w_emb_ref[...], slab_ref[0:width, :])
    feat[:, inner_len:table] = half_silu(raw)
    feat[:, table:] = jnp.zeros((features, feat.shape[1] - table), bf16)
    for half in range(halves_n):
        feat_c[half, :, 0:span] = feat_in_ref[:, half * span : (half + 1) * span]
        feat_c[half, :, span:] = w_rad_ref[...]
    place[...] = place_in_ref[...]
    arrived = slab_ref[width:, :].astype(f32)
    joined = arrived[0:3] + arrived[3:6]
    joined = joined + jnp.where(rows_of((3, LANES)) == 2, lift_ref[0], 0.0)
    upper, lower = halves(joined)
    place[0:3, highs - 1, :] = upper
    place[3:6, highs - 1, :] = lower
    place_b[...] = jnp.zeros_like(place_b)
    place_b[0 : 6 * hpad, 0:LANES] = place[...].reshape(6 * hpad, LANES).astype(bf16)
    place_b[6 * hpad :, LANES:] = place[:, 0:8, :].reshape(48, LANES).astype(bf16)
    for own in (even, odd):
        own.hot[WINDOW + span + 32 :, :] = jnp.zeros((LANES - 32, eb), bf16)
        for ref in (own.extra, own.tensor, own.acc):
            ref[...] = jnp.zeros_like(ref)

    def half_of(b):
        return jnp.where(b >= first_blocks, 1, 0)

    def each_block(run):
        def step(pair, carry):
            run([(even, 2 * pair, pair), (odd, 2 * pair + 1, pair)])
            return carry

        lax.fori_loop(0, pairs, step, 0)

        @pl.when(total_blocks > 2 * pairs)
        def _():
            run([(even, 2 * pairs, pairs)])

    def locate(sides):
        for own_s, b, at in sides:
            slot_c = centers_ref[b]
            o = others_ref[b]
            c = jnp.maximum(slot_c, 0)
            c_high = lax.shift_right_logical(c, 7)
            o_high = lax.shift_right_logical(o, 7)
            hot_c = one_hot(lax.bitwise_and(c, LANES - 1), LANES).astype(bf16)
            hot_o = one_hot(lax.bitwise_and(o, LANES - 1), LANES).astype(bf16)
            lows = jnp.concatenate([hot_o, hot_c], axis=0)
            own_s.lows[at] = lows
            c_high16 = jnp.broadcast_to(c_high, (16, eb))
            own_s.center_hot[at] = jnp.concatenate(
                [masked(hot_c, c_high16, high) for high in range(span // LANES)], axis=0
            )
            both = dot(place_b[...], lows)
            picked = (both[0 : 3 * hpad] + both[3 * hpad : 6 * hpad]).reshape(3, hpad, eb)
            po = jnp.sum(picked * one_hot(o_high, hpad)[None], axis=1)
            picked = both[6 * hpad :]
            picked = (picked[0:24] + picked[24:48]).reshape(3, 8, eb)
            c_whole = c_high + half_of(b) * (span // LANES)
            pc = jnp.sum(picked * one_hot(c_whole, 8)[None], axis=1)
            sep = po - pc
            row = pl.ds(at, 1)
            for d in range(3):
                own_s.geo[d, row, :] = sep[d : d + 1]
            own_s.geo[6, row, :] = jnp.where(slot_c >= 0, 1.0, 0.0)

    each_block(locate)
    for own in (even, odd):
        rx, ry, rz = own.geo[0], own.geo[1], own.geo[2]
        squared = rx * rx + ry * ry + rz * rz
        inv_d = lax.rsqrt(squared + 0.25)
        x, y, z = rx * inv_d, ry * inv_d, rz * inv_d
        own.geo[3] = inv_d
        own.geo[4] = (squared + 0.25) * inv_d
        own.geo[5] = 1.0 / (1.0 + squared * squared * (1.0 / 16.0))
        own.geo[7] = squared
        for m, value in enumerate(harmonic_rows(x, y, z)[1:]):
            own.geo[8 + m] = value

    def geo_row(side, index):
        own_s, _, at = side
        return own_s.geo[index, pl.ds(at, 1), :]

    def harmonics(side):
        return [None] + [geo_row(side, 8 + m) for m in range(8)]

    def prepare(side):
        own_s, b, at = side
        hot = own_s.hot
        hot_o = own_s.lows[at, 0:LANES, :]
        o_high = lax.shift_right_logical(others_ref[b], 7) - 2 * meta_ref[2, b]
        o_high16 = jnp.broadcast_to(o_high, (16, eb))
        for high in range(WINDOW // LANES):
            rows = slice(high * LANES, (high + 1) * LANES)
            hot[rows, :] = masked(hot_o, o_high16, high)
        hot[WINDOW : WINDOW + span, :] = own_s.center_hot[at]
        mu = 0.5 + 0.4 * rows_of((8, eb)).astype(f32)
        u = (geo_row(side, 4) - mu) * 2.0
        upper, lower = halves(jnp.exp(-(u * u)) * geo_row(side, 5))
        radial = jnp.concatenate([upper, lower], axis=0).astype(bf16)
        hot[WINDOW + span : WINDOW + span + 16, :] = radial
        hot[WINDOW + span + 16 : WINDOW + span + 32, :] = radial

    def window(group):
        return feat[:, pl.ds(pl.multiple_of(group * 256, 256), WINDOW)]

    def windows_of(side):
        b = side[1]
        return (meta_ref[3, b] - meta_ref[2, b]) // (WINDOW // 256) + 1

    def further_windows(side):
        own_s, b, _ = side
        windows = windows_of(side)

        @pl.when(windows > 1)
        def _():
            o = others_ref[b]
            hot_o = one_hot(lax.bitwise_and(o, LANES - 1), LANES).astype(bf16)
            o_high16 = jnp.broadcast_to(lax.shift_right_logical(o, 7), (16, eb))

            def add(index, carry):
                group = meta_ref[2, b] + index * (WINDOW // 256)
                hot = jnp.concatenate(
                    [
                        masked(hot_o, o_high16 - 2 * group, high)
                        for high in range(WINDOW // LANES)
                    ],
                    axis=0,
                )
                own_s.extra[...] += dot(window(group), hot)
                return carry

            lax.fori_loop(1, windows, add, 0)

    def clear_windows(side):
        @pl.when(windows_of(side) > 1)
        def _():
            side[0].extra[...] = jnp.zeros_like(side[0].extra)

    def mix(side):
        own_s, b, _ = side
        tables = jnp.concatenate([window(meta_ref[2, b]), feat_c[half_of(b)]], axis=1)
        return dot(tables, own_s.hot[...]) + own_s.extra[...]

    def activate(side, mixed):
        own_s, _, at = side
        up = 1.0 + jnp.tanh(mixed)
        value = mixed * up
        latent = value.astype(bf16)
        own_s.slope[at] = (up + value * (2.0 - up)).astype(bf16)
        return latent

    def spread(side, latent):
        own_s, _, at = side
        own_s.latent[at] = latent
        chan = dot(w_chan_t_ref[...], latent) * geo_row(side, 6)
        own_s.chan[at] = chan
        return jnp.concatenate(
            [(chan if h is None else chan * h).astype(bf16) for h in harmonics(side)], axis=0
        )

    def gather_tensor(side):
        own_s, b, at = side
        return dot(tensor_b[half_of(b)], own_s.center_hot[at])

    def add_tensor(side, products, hot):
        own_s, b, _ = side
        own_s.tensor[half_of(b)] += dot_t(products, hot)

    def first_pass(sides):
        for side in sides:
            further_windows(side)
        mixed = []
        for side in sides:
            prepare(side)
            mixed.append(mix(side))
        products = []
        for side, values in zip(sides, mixed):
            products.append(spread(side, activate(side, values)))
        for side, values in zip(sides, products):
            add_tensor(side, values, side[0].center_hot[side[2]])
        for side in sides:
            clear_windows(side)

    each_block(first_pass)
    tensor_b[...] = (0.125 * (even.tensor[...] + odd.tensor[...])).astype(bf16)
    for own in (even, odd):
        own.tensor[...] = jnp.zeros_like(own.tensor)

    def invariants(side, gathered):
        harm = harmonics(side)
        parts = [gathered[m * chans : (m + 1) * chans] for m in range(9)]
        bands = [parts[0], None, None]
        for m in range(1, 9):
            term = parts[m] * harm[m]
            band = BANDS[m]
            bands[band] = term if bands[band] is None else bands[band] + term
        return jnp.concatenate([band.astype(bf16) for band in bands], axis=0)

    def hidden(side, invariant):
        inputs = jnp.concatenate([side[0].latent[side[2]], invariant], axis=0)
        return dot(w_hidden_ref[...], inputs)

    def readout(side, pre):
        own_s, _, at = side
        up = 1.0 + jnp.tanh(pre)
        value = pre * up
        weight = jnp.concatenate([w_out_ref[...]] * (eb // LANES), axis=1)
        own_s.res[10, pl.ds(at, 1), :] = jnp.sum(value * weight, axis=0, keepdims=True)
        scale = 0.5 * geo_row(side, 5) * geo_row(side, 6)
        return ((up + value * (2.0 - up)) * (weight * scale)).astype(bf16)

    def unfold(side, back, gathered):
        own_s, _, at = side
        harm = harmonics(side)
        own_s.dlat[at] = back[0:features].astype(bf16)
        dbands = [
            back[features + band * chans : features + (band + 1) * chans] for band in range(3)
        ]
        for m in range(1, 9):
            part = gathered[m * chans : (m + 1) * chans]
            own_s.dharm[at, (m - 1) * 8 : m * 8, :] = fold8(dbands[BANDS[m]] * part)
        return jnp.concatenate(
            [
                (dbands[BANDS[m]] if harm[m] is None else dbands[BANDS[m]] * harm[m]).astype(bf16)
                for m in range(9)
            ],
            axis=0,
        )

    def second_pass(sides):
        gathered = [gather_tensor(side) for side in sides]
        pre = [hidden(side, invariants(side, g)) for side, g in zip(sides, gathered)]
        back = [dot(w_back_ref[...], readout(side, values)) for side, values in zip(sides, pre)]
        for side, values, g in zip(sides, back, gathered):
            add_tensor(side, unfold(side, values, g), side[0].center_hot[side[2]])

    each_block(second_pass)
    tensor_b[...] = (0.125 * (even.tensor[...] + odd.tensor[...])).astype(bf16)

    def channels_back(side, gathered):
        own_s, _, at = side
        harm = harmonics(side)
        chan = own_s.chan[at]
        dchan = gathered[0:chans]
        for m in range(1, 9):
            part = gathered[m * chans : (m + 1) * chans]
            dchan = dchan + part * harm[m]
            total = own_s.dharm[at, (m - 1) * 8 : m * 8, :] + fold8(part * chan)
            own_s.res[m - 1, pl.ds(at, 1), :] = jnp.sum(total, axis=0, keepdims=True)
        return (dchan * geo_row(side, 6)).astype(bf16)

    def radial_back(side, dchan):
        own_s, _, at = side
        dlat = own_s.dlat[at] + dot(w_chan_ref[...], dchan).astype(bf16)
        drad = dot(w_rbf_ref[...], dlat * own_s.slope[at])
        drad = drad[0:8] + drad[8:16]
        mu = 0.5 + 0.4 * rows_of((8, eb)).astype(f32)
        u = (geo_row(side, 4) - mu) * 2.0
        weighted = drad * jnp.exp(-(u * u))
        own_s.res[8, pl.ds(at, 1), :] = jnp.sum(weighted, axis=0, keepdims=True)
        own_s.res[9, pl.ds(at, 1), :] = jnp.sum(weighted * u, axis=0, keepdims=True)

    def third_pass(sides):
        gathered = [gather_tensor(side) for side in sides]
        for side, g in zip(sides, gathered):
            radial_back(side, channels_back(side, g))

    each_block(third_pass)

    for own in (even, odd):
        x, y, z = own.geo[8], own.geo[9], own.geo[10]
        inv_d, dist, env = own.geo[3], own.geo[4], own.geo[5]
        live, squared = own.geo[6], own.geo[7]
        dh = [None] + [own.res[m] for m in range(8)]
        summed = own.res[10]
        denv = own.res[8] + live * summed
        ddist = -4.0 * env * own.res[9]
        dx = dh[1] + ROOT3 * (y * dh[4] + z * dh[6] + x * dh[7])
        dy = dh[2] + ROOT3 * (x * dh[4] + z * dh[5] - y * dh[7])
        dz = dh[3] + ROOT3 * (y * dh[5] + x * dh[6]) + 3.0 * z * dh[8]
        ddist = ddist - (dx * x + dy * y + dz * z) * inv_d
        dsq = denv * (env * env * squared * -0.125) + ddist * (0.5 * inv_d)
        both = 2.0 * dsq * dist
        results = [dx * inv_d + both * x, dy * inv_d + both * y, dz * inv_d + both * z]
        results.append(summed * env * live)
        for index, value in enumerate(results):
            own.res[index], own.res[4 + index] = halves(value)

    def collect(sides):
        for own_s, b, at in sides:
            split = [own_s.res[index, pl.ds(at, 1), :] for index in range(8)]
            mask_o = one_hot(lax.shift_right_logical(others_ref[b], 7), hpad)
            values = jnp.concatenate(split, axis=0)
            c_high = lax.shift_right_arithmetic(centers_ref[b], 7)
            rows = jnp.concatenate(
                [mask_o * split[4 * part + d] for part in range(2) for d in range(3)]
                + [
                    values * jnp.where(c_high == high, 1.0, 0.0)
                    for high in range(span // LANES)
                ],
                axis=0,
            ).astype(bf16)
            own_s.acc[half_of(b)] += dot_t(rows, own_s.lows[at])

    each_block(collect)
    acc = [even.acc[half] + odd.acc[half] for half in range(halves_n)]
    sum_o = sum(value[0 : 6 * hpad, 0:LANES] for value in acc)
    sum_o = sum_o[0 : 3 * hpad] + sum_o[3 * hpad :]
    for d in range(3):
        grad_ref[d] = sum_o[d * hpad : (d + 1) * hpad]
        slab_grad_ref[d : d + 1, :] = sum_o[d * hpad + highs - 1 : d * hpad + highs]
    for half in range(halves_n):
        for part in range(span // LANES):
            high = half * (span // LANES) + part
            base = 6 * hpad + part * 8
            sum_c = acc[half][base : base + 4, LANES:] + acc[half][base + 4 : base + 8, LANES:]
            for d in range(3):
                grad_ref[d, high : high + 1, :] = (
                    sum_o[d * hpad + high : d * hpad + high + 1] - sum_c[d : d + 1]
                )
            energy_ref[:, high * LANES : (high + 1) * LANES] = sum_c[3:4]


def return_kernel(grad_ref, back_ref, picks_ref, own_ref, to_xm_ref, to_xp_ref, to_ym_ref, to_yp_ref):
    hpad = grad_ref.shape[1]
    z_rows = picks_ref[8:9, :]
    mask = one_hot(lax.shift_right_logical(z_rows, 7), hpad)
    low = one_hot(lax.bitwise_and(z_rows, LANES - 1), LANES).astype(bf16)
    pieces = [halves(back_ref[d : d + 1, :]) for d in range(3)]
    rows = jnp.concatenate(
        [mask * pieces[d][part] for part in range(2) for d in range(3)], axis=0
    ).astype(bf16)
    landed = dot_t(rows, low)
    landed = landed[0 : 3 * hpad] + landed[3 * hpad :]
    base = own_ref.shape[1] // 2
    for d in range(3):
        total = grad_ref[d] + landed[d * hpad : (d + 1) * hpad]
        own_ref[d] = total[0:8]
        for cycle, (p, q) in enumerate(cycle_cells):
            value = total[base + cycle : base + cycle + 1]
            if p in (0, 4):
                ref = to_xm_ref if p == 0 else to_xp_ref
                ref[q * 3 + d : q * 3 + d + 1, :] = value
            else:
                ref = to_ym_ref if q == 0 else to_yp_ref
                ref[(p - 1) * 3 + d : (p - 1) * 3 + d + 1, :] = value


def turn_kernel(from_xp_ref, from_xm_ref, to_ym_ref, to_yp_ref, send_ym_ref, send_yp_ref):
    for q, old, new in ((0, to_ym_ref, send_ym_ref), (4, to_yp_ref, send_yp_ref)):
        new[0:3, :] = old[0:3, :] + from_xm_ref[q * 3 : q * 3 + 3, :]
        new[3:6, :] = old[3:6, :]
        new[6:9, :] = old[6:9, :] + from_xp_ref[q * 3 : q * 3 + 3, :]


def force_kernel(
    own_ref, picks_ref, from_xp_ref, from_xm_ref, from_yp_ref, from_ym_ref, out_ref, rim_sum
):
    rim_sum[...] = jnp.zeros_like(rim_sum)
    for a, ref in ((2, from_xp_ref), (0, from_xm_ref)):
        for b in range(3):
            rim_sum[rim_cells.index((a, b)), 0:3, :] += ref[(b + 1) * 3 : (b + 2) * 3, :]
    for b, ref in ((2, from_yp_ref), (0, from_ym_ref)):
        for a in range(3):
            rim_sum[rim_cells.index((a, b)), 0:3, :] += ref[a * 3 : (a + 1) * 3, :]
    total = jnp.zeros((48, LANES), f32)
    for rim in range(8):
        index = picks_ref[rim : rim + 1, :]
        mask = one_hot(lax.shift_right_logical(index, 7), 8)
        low = one_hot(lax.bitwise_and(index, LANES - 1), LANES).astype(bf16)
        values = rim_sum[rim]
        pieces = [halves(values[d : d + 1, :]) for d in range(3)]
        rows = jnp.concatenate(
            [mask * pieces[d][part] for part in range(2) for d in range(3)], axis=0
        ).astype(bf16)
        total = total + dot_t(rows, low)
    total = total[0:24] + total[24:48]
    for d in range(3):
        for high in range(out_ref.shape[2] // LANES):
            value = own_ref[d, high : high + 1, :] + total[d * 8 + high : d * 8 + high + 1, :]
            out_ref[d, :, high * LANES : (high + 1) * LANES] = -value


def call(kernel, out_shape, args, scratch=(), smem=0, limit=12 * 1024 * 1024):
    vmem = pl.BlockSpec(memory_space=pltpu.VMEM)
    scalar = pl.BlockSpec(memory_space=pltpu.SMEM)
    return pl.pallas_call(
        kernel,
        out_shape=out_shape,
        in_specs=[scalar] * smem + [vmem] * (len(args) - smem),
        out_specs=jax.tree.map(lambda _: vmem, out_shape),
        scratch_shapes=list(scratch),
        compiler_params=pltpu.CompilerParams(vmem_limit_bytes=limit),
    )(*args)


def shifted(x, axis, step):
    count = lax.axis_size(axis)
    return lax.ppermute(x, axis, [((i + step) % count, i) for i in range(count)])


def swapped(x):
    count = lax.axis_size("gz")
    return lax.ppermute(x, "gz", [(i, i ^ 1) for i in range(count)])


def per_device(
    positions,
    attributes,
    edge_center,
    edge_other,
    edge_count,
    rim_rows,
    z_rows,
    w_emb,
    w_rbf,
    w_chan,
    w_lat,
    w_ten,
    w_out,
):
    pos = positions.reshape(3, 1, -1)
    attr = attributes[0, 0, 0]
    rim = rim_rows[0, 0, 0]
    zr = z_rows[0, 0]
    count = edge_count[0, 0]
    atoms, width = attr.shape
    edges = edge_center.shape[-1]
    features = w_emb.shape[1]
    chans = w_chan.shape[1]
    height = width + PARTS
    inner_len = atoms + 16 * LANES
    table = inner_len + LANES
    hpad = -(-(table // LANES) // 8) * 8
    eb = BLOCK
    span = 2 * LANES
    pairs = -(-(edges // eb + atoms // span - 1) // 2)
    slot_rows = -(-(2 * pairs * eb // LANES) // 8) * 8
    lift = (1 - 2 * lax.axis_index("gz")).astype(f32).reshape(1)
    big = 42 * 1024 * 1024

    shape = jax.ShapeDtypeStruct
    picks = jnp.concatenate([rim, zr], axis=0)
    own, *sent = call(
        pack_kernel,
        (shape((height, atoms), bf16),) + (shape((height, 3 * LANES), bf16),) * 4,
        (pos, attr, picks),
        [pltpu.VMEM((PARTS, atoms), f32)],
    )
    got = [
        shifted(x, "gx" if way[0] else "gy", way[0] + way[1]) for x, way in zip(sent, sides)
    ]
    lines = edges // LANES
    groups = -(-table // 256)
    ends = jnp.concatenate(
        [edge_center.reshape(lines, LANES), edge_other.reshape(lines, LANES)], axis=0
    )
    bucketed = call(
        bucket_kernel,
        (
            shape((slot_rows, LANES), jnp.int32),
            shape((slot_rows, LANES), jnp.int32),
            shape((4, LANES), jnp.int32),
        ),
        (count, ends),
        [
            pltpu.VMEM((2 * groups * lines, LANES), bf16),
            pltpu.VMEM((4 * slot_rows, edges), bf16),
            pltpu.VMEM((LANES, edges), bf16),
        ],
        smem=1,
        limit=24 * 1024 * 1024,
    )
    first, bucketed = lax.optimization_barrier((got[:2], bucketed))
    got = [*first, *got[2:]]
    centers, others, meta = bucketed
    centers = centers.reshape(-1, 1, eb)
    others = others.reshape(-1, 1, eb)
    to_plus, to_minus = call(
        corner_kernel,
        (shape((height, 2 * LANES), bf16),) * 2,
        (got[0], got[1]),
    )
    w_emb, w_rbf, to_plus = lax.optimization_barrier((w_emb, w_rbf, to_plus))
    prepared = call(
        weights_kernel,
        (
            shape((features, width), bf16),
            shape((features, LANES), bf16),
            shape((features, chans), bf16),
            shape((chans, features), bf16),
            shape((features, features + 3 * chans), bf16),
            shape((features + 3 * chans, features), bf16),
            shape((features, LANES), f32),
            shape((16, features), bf16),
        ),
        (
            jnp.concatenate([w_emb, w_lat, w_ten, w_chan.T], axis=0),
            jnp.concatenate([w_rbf, w_out[None]], axis=0),
        ),
        [pltpu.VMEM((LANES, features), f32)],
    )
    corners = [shifted(to_plus, "gx", -1), shifted(to_minus, "gx", 1)]
    corners, prepared = lax.optimization_barrier((corners, prepared))
    w_emb_t, w_rad, w_chan_r, w_chan_t, w_hidden, w_back, w_out_col, w_rbf2 = prepared
    inner, slab_send = call(
        slab_kernel,
        (shape((height, inner_len), bf16), shape((height, LANES), bf16)),
        (own, picks, *got, *corners),
        [pltpu.VMEM((PARTS, inner_len), f32)],
    )
    slab_got = swapped(slab_send)
    feat, place = call(
        embed_kernel,
        (shape((features, inner_len), bf16), shape((6, hpad, LANES), f32)),
        (inner, w_emb_t),
    )
    grads, slab_grad, energy = call(
        edge_kernel,
        (shape((3, hpad, LANES), f32), shape((3, LANES), f32), shape((1, atoms), f32)),
        (
            meta,
            lift,
            centers,
            others,
            feat,
            place,
            slab_got,
            w_emb_t,
            w_rad,
            w_chan_t,
            w_chan_r,
            w_hidden,
            w_back,
            w_out_col,
            w_rbf2,
        ),
        [
            pltpu.VMEM((features, (groups - 1) * 256 + WINDOW), bf16),
            pltpu.VMEM((atoms // span, features, span + LANES), bf16),
            pltpu.VMEM((6, hpad, LANES), f32),
            pltpu.VMEM((6 * hpad + 48, 2 * LANES), bf16),
            pltpu.VMEM((atoms // span, 9 * chans, span), bf16),
        ]
        + [
            pltpu.VMEM((WINDOW + span + LANES, eb), bf16),
            pltpu.VMEM((features, eb), f32),
            pltpu.VMEM((pairs, span, eb), bf16),
            pltpu.VMEM((pairs, 2 * LANES, eb), bf16),
            pltpu.VMEM((pairs, features, eb), bf16),
            pltpu.VMEM((pairs, features, eb), bf16),
            pltpu.VMEM((pairs, chans, eb), f32),
            pltpu.VMEM((16, -(-pairs // 8) * 8, eb), f32),
            pltpu.VMEM((11, -(-pairs // 8) * 8, eb), f32),
            pltpu.VMEM((pairs, features, eb), bf16),
            pltpu.VMEM((pairs, 64, eb), f32),
            pltpu.VMEM((atoms // span, 9 * chans, span), f32),
            pltpu.VMEM((atoms // span, 6 * hpad + 8 * (span // LANES), 2 * LANES), f32),
        ]
        * 2,
        smem=2,
        limit=big,
    )
    slab_back = swapped(slab_grad)
    along_x, along_y = shape((15, LANES), f32), shape((9, LANES), f32)
    own_grad, to_xm, to_xp, to_ym, to_yp = call(
        return_kernel,
        (shape((3, 8, LANES), f32), along_x, along_x, along_y, along_y),
        (grads, slab_back, picks),
    )
    from_xp, from_xm = shifted(to_xm, "gx", 1), shifted(to_xp, "gx", -1)
    to_ym, to_yp = call(turn_kernel, (along_y, along_y), (from_xp, from_xm, to_ym, to_yp))
    from_yp, from_ym = shifted(to_ym, "gy", 1), shifted(to_yp, "gy", -1)
    forces = call(
        force_kernel,
        shape((3, 1, atoms), f32),
        (own_grad, picks, from_xp, from_xm, from_yp, from_ym),
        [pltpu.VMEM((8, 8, LANES), f32)],
    )
    return (energy.reshape(1, 1, 1, atoms), forces.reshape(1, 1, 1, 3, atoms))


def solution(mesh):
    return jax.shard_map(
        per_device,
        mesh=mesh,
        in_specs=(
            P("gx", "gy", "gz", None, None),
            P("gx", "gy", "gz", None, None),
            P("gx", "gy", "gz", None),
            P("gx", "gy", "gz", None),
            P("gx", "gy", "gz"),
            P("gx", "gy", "gz", None, None),
            P("gx", "gy", "gz", None),
            P(),
            P(),
            P(),
            P(),
            P(),
            P(),
        ),
        out_specs=(P("gx", "gy", "gz", None), P("gx", "gy", "gz", None, None)),
        check_vma=False,
    )
```

```python
import collections

import jax
import jax.numpy as jnp
from jax import lax
from jax.experimental import pallas as pl
from jax.experimental.pallas import tpu as pltpu
from jax.sharding import PartitionSpec as P

f32 = jnp.float32
bf16 = jnp.bfloat16
LANES = 128
PARTS = 16
BLOCK = 512
WINDOW = 768
ROOT3 = 3.0**0.5
BANDS = (0, 1, 1, 1, 2, 2, 2, 2, 2)

rim_cells = [(0, 0), (0, 1), (0, 2), (1, 0), (1, 2), (2, 0), (2, 1), (2, 2)]
cycle_cells = [(p, q) for p in range(5) for q in range(5) if p in (0, 4) or q in (0, 4)]


def source_of(position):
    if position == 0:
        return (-1, 2)
    if position == 4:
        return (1, 0)
    return (0, position - 1)


routes = {}
for _cycle, (_p, _q) in enumerate(cycle_cells):
    (_sx, _a), (_sy, _b) = source_of(_p), source_of(_q)
    routes.setdefault((_sx, _sy), []).append((_cycle, rim_cells.index((_a, _b))))
sides = [(0, -1), (0, 1), (-1, 0), (1, 0)]


def dot(a, b):
    return lax.dot_general(a, b, (((1,), (0,)), ((), ())), preferred_element_type=f32)


def dot_t(a, b):
    return lax.dot_general(a, b, (((1,), (1,)), ((), ())), preferred_element_type=f32)


def rows_of(shape):
    return lax.broadcasted_iota(jnp.int32, shape, 0)


def one_hot(index, size):
    return jnp.where(rows_of((size, index.shape[1])) == index, 1.0, 0.0)


def halves(values):
    upper = values.astype(bf16).astype(f32)
    return upper, values - upper


def masked(hot_low, high16, value):
    mask = jnp.where(high16 == value, 1.0, 0.0).astype(bf16)
    size, lanes = hot_low.shape
    return (hot_low.reshape(size // 16, 16, lanes) * mask[None]).reshape(size, lanes)


def half_silu(x):
    half = 0.5 * x
    return (0.5 * (half * (1.0 + jnp.tanh(half)))).astype(bf16)


def pack_kernel(pos_ref, attr_ref, picks_ref, own_ref, *rest):
    sends, parts = rest[:4], rest[4]
    atoms, width = attr_ref.shape
    eye = jnp.where(
        rows_of((width, width)) == lax.broadcasted_iota(jnp.int32, (width, width), 1), 1.0, 0.0
    ).astype(bf16)
    own_ref[0:width, :] = dot_t(eye, attr_ref[...]).astype(bf16)
    parts[...] = jnp.zeros_like(parts)
    for d in range(3):
        parts[d : d + 1, :], parts[3 + d : 4 + d, :] = halves(pos_ref[d])
    own_ref[width : width + PARTS, :] = parts[...].astype(bf16)
    packed = own_ref[...]
    for rim in range(8):
        hot = one_hot(picks_ref[rim : rim + 1, :], atoms).astype(bf16)
        cell = dot(packed, hot).astype(bf16)
        for way, send in zip(sides, sends):
            for slot, (_, source) in enumerate(routes[way]):
                if source == rim:
                    send[:, slot * LANES : (slot + 1) * LANES] = cell


def corner_kernel(minus_ref, plus_ref, to_plus_ref, to_minus_ref):
    first, last = slice(0, LANES), slice(2 * LANES, 3 * LANES)
    for slot, ref in enumerate((minus_ref, plus_ref)):
        lanes = slice(slot * LANES, (slot + 1) * LANES)
        to_plus_ref[:, lanes] = ref[:, last]
        to_minus_ref[:, lanes] = ref[:, first]


def slab_kernel(own_ref, picks_ref, *rest):
    got, corners, (inner_ref, send_ref, parts) = rest[:4], rest[4:6], rest[6:]
    atoms = own_ref.shape[1]
    height = own_ref.shape[0]
    width = height - PARTS
    inner_len = inner_ref.shape[1]
    inner_ref[:, 0:atoms] = own_ref[...]
    parts[...] = jnp.zeros_like(parts)
    parts[0:6, 0:atoms] = own_ref[width:height, :].astype(f32)[0:6]
    arrivals = []
    for way, ref in zip(sides, got):
        for slot, (cycle, _) in enumerate(routes[way]):
            arrivals.append((way, ref, slot, cycle))
    for sx, ref in zip((-1, 1), corners):
        for slot, sy in enumerate((-1, 1)):
            arrivals.append(((sx, sy), ref, slot, routes[(sx, sy)][0][0]))
    for way, ref, slot, cycle in arrivals:
        lanes = slice(slot * LANES, (slot + 1) * LANES)
        into = slice(atoms + cycle * LANES, atoms + (cycle + 1) * LANES)
        inner_ref[0:width, into] = ref[0:width, lanes]
        arrived = ref[width:height, lanes].astype(f32)
        joined = arrived[0:3] + arrived[3:6]
        axis = rows_of((3, LANES))
        shift = jnp.where(axis == 0, float(way[0]), jnp.where(axis == 1, float(way[1]), 0.0))
        upper, lower = halves(joined + shift)
        parts[0:3, into] = upper
        parts[3:6, into] = lower
    inner_ref[width:height, :] = parts[...].astype(bf16)
    hot = one_hot(picks_ref[8:9, :], inner_len).astype(bf16)
    send_ref[...] = dot(inner_ref[...], hot).astype(bf16)


def unit(size):
    lanes = lax.broadcasted_iota(jnp.int32, (size, size), 1)
    return jnp.where(rows_of((size, size)) == lanes, 1.0, 0.0)


def weights_kernel(
    stacked_ref,
    small_ref,
    emb_t_ref,
    rad_ref,
    chan_ref,
    w_chan_t_ref,
    hidden_ref,
    back_ref,
    out_ref,
    rbf_ref,
    scratch,
):
    features = stacked_ref.shape[1]
    width = emb_t_ref.shape[1]
    inner = back_ref.shape[0]
    w_emb = stacked_ref[0:width]
    w_back = stacked_ref[width : width + inner]
    w_chan_t = stacked_ref[width + inner :]
    eye = unit(features)
    eye_b = eye.astype(bf16)
    emb_t_ref[...] = dot_t(eye_b, w_emb).astype(bf16)
    chan_ref[...] = dot_t(eye_b, w_chan_t).astype(bf16)
    w_chan_t_ref[...] = w_chan_t
    turned = (0.5 * dot_t(eye_b, w_back)).astype(bf16)
    hidden_ref[...] = turned
    back_ref[...] = w_back
    column = jnp.sum(eye * small_ref[8:9, :], axis=1, keepdims=True)
    out_ref[...] = jnp.broadcast_to(column, out_ref.shape)
    upper, lower = halves(0.5 * small_ref[0:8, :])
    rbf_ref[...] = jnp.concatenate([upper, lower], axis=0).astype(bf16)
    scratch[...] = jnp.zeros_like(scratch)
    for start, value in ((0, upper), (8, upper), (16, lower), (24, lower)):
        scratch[start : start + 8, :] = value
    rad_ref[...] = dot_t(eye_b, scratch[...].astype(bf16)).astype(bf16)


def embed_kernel(inner_ref, w_emb_ref, feat_ref, place_ref):
    width = w_emb_ref.shape[1]
    inner_len = inner_ref.shape[1]
    for first in range(0, inner_len, 512):
        raw = dot(w_emb_ref[...], inner_ref[0:width, first : first + 512])
        feat_ref[:, first : first + 512] = half_silu(raw)
    parts = inner_ref[width:, :].astype(f32)
    place_ref[...] = jnp.zeros_like(place_ref)
    for high in range(inner_len // LANES):
        place_ref[0:6, high, :] = parts[0:6, high * LANES : (high + 1) * LANES]


def bucket_kernel(count_ref, ends_ref, center_ref, other_ref, meta_ref, marks_s, rows_s, low_s):
    lines = ends_ref.shape[0] // 2
    keys = marks_s.shape[0] // lines
    groups = keys // 2
    count = count_ref[0]
    c, o = ends_ref[0:lines, :], ends_ref[lines:, :]
    shape = (lines, LANES)
    order = rows_of(shape) * LANES + lax.broadcasted_iota(jnp.int32, shape, 1)
    key = lax.shift_right_logical(c, 8) * groups + lax.shift_right_logical(o, 8)
    key = jnp.where(order < count, key, -1)
    for k in range(keys):
        marks_s[k * lines : (k + 1) * lines, :] = jnp.where(key == k, 1.0, 0.0).astype(bf16)
    square = (LANES, LANES)
    tri = jnp.where(rows_of(square) < lax.broadcasted_iota(jnp.int32, square, 1), 1.0, 0.0)
    tri = tri.astype(bf16)
    tall = (lines, lines)
    below = jnp.where(lax.broadcasted_iota(jnp.int32, tall, 1) < rows_of(tall), 1.0, 0.0)
    marks = marks_s[...]
    inside = dot(marks, tri)
    totals = dot(marks, jnp.ones(square, bf16))
    lane = lax.broadcasted_iota(jnp.int32, shape, 1)
    by_key = jnp.zeros(shape, f32)
    for k in range(keys):
        by_key = jnp.where(lane == k, totals[k * lines : (k + 1) * lines], by_key)
    before = dot(below.astype(bf16), by_key.astype(bf16))
    everything = jnp.broadcast_to(jnp.sum(by_key, axis=0, keepdims=True), (16, LANES))
    upper, lower = halves(everything)
    start = (dot(upper.astype(bf16), tri) + dot(lower.astype(bf16), tri))[0:1]
    row_lane = lane[0:1]
    first = jnp.sum(jnp.where(row_lane < groups, everything[0:1], 0.0), axis=1, keepdims=True)
    second = jnp.sum(jnp.where(row_lane >= groups, everything[0:1], 0.0), axis=1, keepdims=True)
    first_blocks = jnp.floor((first + (BLOCK - 1)) * (1.0 / BLOCK))
    blocks = first_blocks + jnp.floor((second + (BLOCK - 1)) * (1.0 / BLOCK))
    start = start + jnp.where(row_lane >= groups, first_blocks * BLOCK - first, 0.0)
    offset = before + start
    slot = jnp.full(shape, -1.0, f32)
    for k in range(keys):
        place = inside[k * lines : (k + 1) * lines] + offset[:, k : k + 1]
        slot = jnp.where(key == k, place, slot)
    slot = slot.astype(jnp.int32)
    slot_high = lax.shift_right_arithmetic(slot, 7)
    slot_low = lax.bitwise_and(slot, LANES - 1)
    highs = center_ref.shape[0]
    values = [
        jnp.ones(shape, f32),
        lax.bitwise_and(c, 255).astype(f32),
        lax.shift_right_logical(o, 7).astype(f32),
        lax.bitwise_and(o, LANES - 1).astype(f32),
    ]
    for line in range(lines):
        lanes = slice(line * LANES, (line + 1) * LANES)
        high = one_hot(slot_high[line : line + 1], highs)
        rows_s[:, lanes] = jnp.concatenate(
            [high * value[line : line + 1] for value in values], axis=0
        ).astype(bf16)
        low_s[:, lanes] = one_hot(slot_low[line : line + 1], LANES).astype(bf16)
    placed = dot_t(rows_s[...], low_s[...])
    center = placed[highs : 2 * highs] + placed[0:highs] - 1.0
    other = placed[2 * highs : 3 * highs] * float(LANES) + placed[3 * highs :]
    center_ref[...] = center.astype(jnp.int32)
    other_ref[...] = other.astype(jnp.int32)
    group = jnp.floor(other * (1.0 / 256.0))
    none = float(groups)
    low = jnp.min(jnp.where(center >= 0.0, group, none), axis=1, keepdims=True)
    high = jnp.max(jnp.where(center >= 0.0, group, -1.0), axis=1, keepdims=True)
    block = lax.broadcasted_iota(jnp.int32, (highs, LANES), 1)
    line_of = rows_of((highs, LANES)) // (BLOCK // LANES) == block
    low = jnp.min(jnp.where(line_of, low, none), axis=0, keepdims=True)
    high = jnp.max(jnp.where(line_of, high, -1.0), axis=0, keepdims=True)
    low = jnp.where(high < 0.0, 0.0, low)
    high = jnp.where(high < 0.0, 0.0, high)
    meta_ref[0:1, :] = jnp.broadcast_to(first_blocks, (1, LANES)).astype(jnp.int32)
    meta_ref[1:2, :] = jnp.broadcast_to(blocks, (1, LANES)).astype(jnp.int32)
    meta_ref[2:3, :] = low.astype(jnp.int32)
    meta_ref[3:4, :] = high.astype(jnp.int32)


def harmonic_rows(x, y, z):
    return [
        None,
        x,
        y,
        z,
        ROOT3 * x * y,
        ROOT3 * y * z,
        ROOT3 * z * x,
        0.5 * ROOT3 * (x * x - y * y),
        0.5 * (3.0 * z * z - 1.0),
    ]


def fold8(values):
    return jnp.sum(values.reshape(values.shape[0] // 8, 8, values.shape[1]), axis=0)


FIELDS = (
    ["hot", "extra", "center_hot", "edge_hot", "lows", "latent", "slope", "chan"]
    + ["geo", "res", "dlat", "dharm", "tensor", "acc"]
)
Scratch = collections.namedtuple("Scratch", FIELDS)


def edge_kernel(
    meta_ref,
    lift_ref,
    centers_ref,
    others_ref,
    feat_in_ref,
    place_in_ref,
    slab_ref,
    w_emb_ref,
    w_rad_ref,
    w_chan_t_ref,
    w_chan_ref,
    w_hidden_ref,
    w_back_ref,
    w_out_ref,
    w_rbf_ref,
    grad_ref,
    slab_grad_ref,
    energy_ref,
    feat,
    feat_c,
    place,
    place_b,
    tensor_b,
    *scratch,
):
    names = len(scratch) // 2
    even, odd = (Scratch(*scratch[side * names : (side + 1) * names]) for side in range(2))
    eb = centers_ref.shape[2]
    width = w_emb_ref.shape[1]
    features = feat_in_ref.shape[0]
    inner_len = feat_in_ref.shape[1]
    table = inner_len + LANES
    highs = table // LANES
    span = tensor_b.shape[2]
    halves_n = tensor_b.shape[0]
    chans = w_chan_ref.shape[1]
    hpad = place_in_ref.shape[1]
    first_blocks = meta_ref[0, 0]
    total_blocks = meta_ref[1, 0]
    pairs = total_blocks // 2

    feat[:, 0:inner_len] = feat_in_ref[...]
    raw = dot(w_emb_ref[...], slab_ref[0:width, :])
    feat[:, inner_len:table] = half_silu(raw)
    feat[:, table:] = jnp.zeros((features, feat.shape[1] - table), bf16)
    for half in range(halves_n):
        feat_c[half, :, 0:span] = feat_in_ref[:, half * span : (half + 1) * span]
        feat_c[half, :, span:] = w_rad_ref[...]
    place[...] = place_in_ref[...]
    arrived = slab_ref[width:, :].astype(f32)
    joined = arrived[0:3] + arrived[3:6]
    joined = joined + jnp.where(rows_of((3, LANES)) == 2, lift_ref[0], 0.0)
    upper, lower = halves(joined)
    place[0:3, highs - 1, :] = upper
    place[3:6, highs - 1, :] = lower
    place_b[...] = jnp.zeros_like(place_b)
    place_b[0 : 6 * hpad, 0:LANES] = place[...].reshape(6 * hpad, LANES).astype(bf16)
    place_b[6 * hpad :, LANES:] = place[:, 0:8, :].reshape(48, LANES).astype(bf16)
    for own in (even, odd):
        own.hot[WINDOW + span + 32 :, :] = jnp.zeros((LANES - 32, eb), bf16)
        for ref in (own.extra, own.tensor, own.acc):
            ref[...] = jnp.zeros_like(ref)

    def half_of(b):
        return jnp.where(b >= first_blocks, 1, 0)

    def each_block(run):
        def step(pair, carry):
            run([(even, 2 * pair, pair), (odd, 2 * pair + 1, pair)])
            return carry

        lax.fori_loop(0, pairs, step, 0)

        @pl.when(total_blocks > 2 * pairs)
        def _():
            run([(even, 2 * pairs, pairs)])

    def locate(sides):
        for own_s, b, at in sides:
            slot_c = centers_ref[b]
            o = others_ref[b]
            c = jnp.maximum(slot_c, 0)
            c_high = lax.shift_right_logical(c, 7)
            o_high = lax.shift_right_logical(o, 7)
            hot_c = one_hot(lax.bitwise_and(c, LANES - 1), LANES).astype(bf16)
            hot_o = one_hot(lax.bitwise_and(o, LANES - 1), LANES).astype(bf16)
            lows = jnp.concatenate([hot_o, hot_c], axis=0)
            own_s.lows[at] = lows
            c_high16 = jnp.broadcast_to(c_high, (16, eb))
            center_hot = jnp.concatenate(
                [masked(hot_c, c_high16, high) for high in range(span // LANES)], axis=0
            )
            own_s.center_hot[at] = center_hot
            own_s.edge_hot[at] = center_hot.T
            both = dot(place_b[...], lows)
            picked = (both[0 : 3 * hpad] + both[3 * hpad : 6 * hpad]).reshape(3, hpad, eb)
            po = jnp.sum(picked * one_hot(o_high, hpad)[None], axis=1)
            picked = both[6 * hpad :]
            picked = (picked[0:24] + picked[24:48]).reshape(3, 8, eb)
            c_whole = c_high + half_of(b) * (span // LANES)
            pc = jnp.sum(picked * one_hot(c_whole, 8)[None], axis=1)
            sep = po - pc
            row = pl.ds(at, 1)
            for d in range(3):
                own_s.geo[d, row, :] = sep[d : d + 1]
            own_s.geo[6, row, :] = jnp.where(slot_c >= 0, 1.0, 0.0)

    each_block(locate)
    for own in (even, odd):
        rx, ry, rz = own.geo[0], own.geo[1], own.geo[2]
        squared = rx * rx + ry * ry + rz * rz
        inv_d = lax.rsqrt(squared + 0.25)
        x, y, z = rx * inv_d, ry * inv_d, rz * inv_d
        own.geo[3] = inv_d
        own.geo[4] = (squared + 0.25) * inv_d
        own.geo[5] = 1.0 / (1.0 + squared * squared * (1.0 / 16.0))
        own.geo[7] = squared
        for m, value in enumerate(harmonic_rows(x, y, z)[1:]):
            own.geo[8 + m] = value

    def geo_row(side, index):
        own_s, _, at = side
        return own_s.geo[index, pl.ds(at, 1), :]

    def harmonics(side):
        return [None] + [geo_row(side, 8 + m) for m in range(8)]

    def prepare(side):
        own_s, b, at = side
        hot = own_s.hot
        hot_o = own_s.lows[at, 0:LANES, :]
        o_high = lax.shift_right_logical(others_ref[b], 7) - 2 * meta_ref[2, b]
        o_high16 = jnp.broadcast_to(o_high, (16, eb))
        for high in range(WINDOW // LANES):
            rows = slice(high * LANES, (high + 1) * LANES)
            hot[rows, :] = masked(hot_o, o_high16, high)
        hot[WINDOW : WINDOW + span, :] = own_s.center_hot[at]
        mu = 0.5 + 0.4 * rows_of((8, eb)).astype(f32)
        u = (geo_row(side, 4) - mu) * 2.0
        upper, lower = halves(jnp.exp(-(u * u)) * geo_row(side, 5))
        radial = jnp.concatenate([upper, lower], axis=0).astype(bf16)
        hot[WINDOW + span : WINDOW + span + 16, :] = radial
        hot[WINDOW + span + 16 : WINDOW + span + 32, :] = radial

    def window(group):
        return feat[:, pl.ds(pl.multiple_of(group * 256, 256), WINDOW)]

    def windows_of(side):
        b = side[1]
        return (meta_ref[3, b] - meta_ref[2, b]) // (WINDOW // 256) + 1

    def further_windows(side):
        own_s, b, _ = side
        windows = windows_of(side)

        @pl.when(windows > 1)
        def _():
            o = others_ref[b]
            hot_o = one_hot(lax.bitwise_and(o, LANES - 1), LANES).astype(bf16)
            o_high16 = jnp.broadcast_to(lax.shift_right_logical(o, 7), (16, eb))

            def add(index, carry):
                group = meta_ref[2, b] + index * (WINDOW // 256)
                hot = jnp.concatenate(
                    [
                        masked(hot_o, o_high16 - 2 * group, high)
                        for high in range(WINDOW // LANES)
                    ],
                    axis=0,
                )
                own_s.extra[...] += dot(window(group), hot)
                return carry

            lax.fori_loop(1, windows, add, 0)

    def clear_windows(side):
        @pl.when(windows_of(side) > 1)
        def _():
            side[0].extra[...] = jnp.zeros_like(side[0].extra)

    def mix(side):
        own_s, b, _ = side
        tables = jnp.concatenate([window(meta_ref[2, b]), feat_c[half_of(b)]], axis=1)
        return dot(tables, own_s.hot[...]) + own_s.extra[...]

    def activate(side, mixed):
        own_s, _, at = side
        up = 1.0 + jnp.tanh(mixed)
        value = mixed * up
        latent = value.astype(bf16)
        own_s.slope[at] = (up + value * (2.0 - up)).astype(bf16)
        return latent

    def spread(side, latent):
        own_s, _, at = side
        own_s.latent[at] = latent
        chan = dot(w_chan_t_ref[...], latent) * geo_row(side, 6)
        own_s.chan[at] = chan
        return jnp.concatenate(
            [(chan if h is None else chan * h).astype(bf16) for h in harmonics(side)], axis=0
        )

    def gather_tensor(side):
        own_s, b, at = side
        return dot(tensor_b[half_of(b)], own_s.center_hot[at])

    def add_tensor(side, products):
        own_s, b, at = side
        own_s.tensor[half_of(b)] += dot(products, own_s.edge_hot[at])

    def first_pass(sides):
        for side in sides:
            further_windows(side)
        mixed = []
        for side in sides:
            prepare(side)
            mixed.append(mix(side))
        products = []
        for side, values in zip(sides, mixed):
            products.append(spread(side, activate(side, values)))
        for side, values in zip(sides, products):
            add_tensor(side, values)
        for side in sides:
            clear_windows(side)

    each_block(first_pass)
    tensor_b[...] = (0.125 * (even.tensor[...] + odd.tensor[...])).astype(bf16)
    for own in (even, odd):
        own.tensor[...] = jnp.zeros_like(own.tensor)

    def invariants(side, gathered):
        harm = harmonics(side)
        parts = [gathered[m * chans : (m + 1) * chans] for m in range(9)]
        bands = [parts[0], None, None]
        for m in range(1, 9):
            term = parts[m] * harm[m]
            band = BANDS[m]
            bands[band] = term if bands[band] is None else bands[band] + term
        return jnp.concatenate([band.astype(bf16) for band in bands], axis=0)

    def hidden(side, invariant):
        inputs = jnp.concatenate([side[0].latent[side[2]], invariant], axis=0)
        return dot(w_hidden_ref[...], inputs)

    def readout(side, pre):
        own_s, _, at = side
        up = 1.0 + jnp.tanh(pre)
        value = pre * up
        weight = jnp.concatenate([w_out_ref[...]] * (eb // LANES), axis=1)
        own_s.res[10, pl.ds(at, 1), :] = jnp.sum(value * weight, axis=0, keepdims=True)
        scale = 0.5 * geo_row(side, 5) * geo_row(side, 6)
        return ((up + value * (2.0 - up)) * (weight * scale)).astype(bf16)

    def unfold(side, back, gathered):
        own_s, _, at = side
        harm = harmonics(side)
        own_s.dlat[at] = back[0:features].astype(bf16)
        dbands = [
            back[features + band * chans : features + (band + 1) * chans] for band in range(3)
        ]
        for m in range(1, 9):
            part = gathered[m * chans : (m + 1) * chans]
            own_s.dharm[at, (m - 1) * 8 : m * 8, :] = fold8(dbands[BANDS[m]] * part)
        return jnp.concatenate(
            [
                (dbands[BANDS[m]] if harm[m] is None else dbands[BANDS[m]] * harm[m]).astype(bf16)
                for m in range(9)
            ],
            axis=0,
        )

    def second_pass(sides):
        gathered = [gather_tensor(side) for side in sides]
        pre = [hidden(side, invariants(side, g)) for side, g in zip(sides, gathered)]
        back = [dot(w_back_ref[...], readout(side, values)) for side, values in zip(sides, pre)]
        for side, values, g in zip(sides, back, gathered):
            add_tensor(side, unfold(side, values, g))

    each_block(second_pass)
    tensor_b[...] = (0.125 * (even.tensor[...] + odd.tensor[...])).astype(bf16)

    def channels_back(side, gathered):
        own_s, _, at = side
        harm = harmonics(side)
        chan = own_s.chan[at]
        dchan = gathered[0:chans]
        for m in range(1, 9):
            part = gathered[m * chans : (m + 1) * chans]
            dchan = dchan + part * harm[m]
            total = own_s.dharm[at, (m - 1) * 8 : m * 8, :] + fold8(part * chan)
            own_s.res[m - 1, pl.ds(at, 1), :] = jnp.sum(total, axis=0, keepdims=True)
        return (dchan * geo_row(side, 6)).astype(bf16)

    def radial_back(side, dchan):
        own_s, _, at = side
        dlat = own_s.dlat[at] + dot(w_chan_ref[...], dchan).astype(bf16)
        drad = dot(w_rbf_ref[...], dlat * own_s.slope[at])
        drad = drad[0:8] + drad[8:16]
        mu = 0.5 + 0.4 * rows_of((8, eb)).astype(f32)
        u = (geo_row(side, 4) - mu) * 2.0
        weighted = drad * jnp.exp(-(u * u))
        own_s.res[8, pl.ds(at, 1), :] = jnp.sum(weighted, axis=0, keepdims=True)
        own_s.res[9, pl.ds(at, 1), :] = jnp.sum(weighted * u, axis=0, keepdims=True)

    def third_pass(sides):
        gathered = [gather_tensor(side) for side in sides]
        for side, g in zip(sides, gathered):
            radial_back(side, channels_back(side, g))

    each_block(third_pass)

    for own in (even, odd):
        x, y, z = own.geo[8], own.geo[9], own.geo[10]
        inv_d, dist, env = own.geo[3], own.geo[4], own.geo[5]
        live, squared = own.geo[6], own.geo[7]
        dh = [None] + [own.res[m] for m in range(8)]
        summed = own.res[10]
        denv = own.res[8] + live * summed
        ddist = -4.0 * env * own.res[9]
        dx = dh[1] + ROOT3 * (y * dh[4] + z * dh[6] + x * dh[7])
        dy = dh[2] + ROOT3 * (x * dh[4] + z * dh[5] - y * dh[7])
        dz = dh[3] + ROOT3 * (y * dh[5] + x * dh[6]) + 3.0 * z * dh[8]
        ddist = ddist - (dx * x + dy * y + dz * z) * inv_d
        dsq = denv * (env * env * squared * -0.125) + ddist * (0.5 * inv_d)
        both = 2.0 * dsq * dist
        results = [dx * inv_d + both * x, dy * inv_d + both * y, dz * inv_d + both * z]
        results.append(summed * env * live)
        for index, value in enumerate(results):
            own.res[index], own.res[4 + index] = halves(value)

    def collect(sides):
        for own_s, b, at in sides:
            split = [own_s.res[index, pl.ds(at, 1), :] for index in range(8)]
            mask_o = one_hot(lax.shift_right_logical(others_ref[b], 7), hpad)
            values = jnp.concatenate(split, axis=0)
            c_high = lax.shift_right_arithmetic(centers_ref[b], 7)
            rows = jnp.concatenate(
                [mask_o * split[4 * part + d] for part in range(2) for d in range(3)]
                + [
                    values * jnp.where(c_high == high, 1.0, 0.0)
                    for high in range(span // LANES)
                ],
                axis=0,
            ).astype(bf16)
            own_s.acc[half_of(b)] += dot_t(rows, own_s.lows[at])

    each_block(collect)
    acc = [even.acc[half] + odd.acc[half] for half in range(halves_n)]
    sum_o = sum(value[0 : 6 * hpad, 0:LANES] for value in acc)
    sum_o = sum_o[0 : 3 * hpad] + sum_o[3 * hpad :]
    for d in range(3):
        grad_ref[d] = sum_o[d * hpad : (d + 1) * hpad]
        slab_grad_ref[d : d + 1, :] = sum_o[d * hpad + highs - 1 : d * hpad + highs]
    for half in range(halves_n):
        for part in range(span // LANES):
            high = half * (span // LANES) + part
            base = 6 * hpad + part * 8
            sum_c = acc[half][base : base + 4, LANES:] + acc[half][base + 4 : base + 8, LANES:]
            for d in range(3):
                grad_ref[d, high : high + 1, :] = (
                    sum_o[d * hpad + high : d * hpad + high + 1] - sum_c[d : d + 1]
                )
            energy_ref[:, high * LANES : (high + 1) * LANES] = sum_c[3:4]


def return_kernel(grad_ref, back_ref, picks_ref, own_ref, to_xm_ref, to_xp_ref, to_ym_ref, to_yp_ref):
    hpad = grad_ref.shape[1]
    z_rows = picks_ref[8:9, :]
    mask = one_hot(lax.shift_right_logical(z_rows, 7), hpad)
    low = one_hot(lax.bitwise_and(z_rows, LANES - 1), LANES).astype(bf16)
    pieces = [halves(back_ref[d : d + 1, :]) for d in range(3)]
    rows = jnp.concatenate(
        [mask * pieces[d][part] for part in range(2) for d in range(3)], axis=0
    ).astype(bf16)
    landed = dot_t(rows, low)
    landed = landed[0 : 3 * hpad] + landed[3 * hpad :]
    base = own_ref.shape[1] // 2
    for d in range(3):
        total = grad_ref[d] + landed[d * hpad : (d + 1) * hpad]
        own_ref[d] = total[0:8]
        for cycle, (p, q) in enumerate(cycle_cells):
            value = total[base + cycle : base + cycle + 1]
            if p in (0, 4):
                ref = to_xm_ref if p == 0 else to_xp_ref
                ref[q * 3 + d : q * 3 + d + 1, :] = value
            else:
                ref = to_ym_ref if q == 0 else to_yp_ref
                ref[(p - 1) * 3 + d : (p - 1) * 3 + d + 1, :] = value


def turn_kernel(from_xp_ref, from_xm_ref, to_ym_ref, to_yp_ref, send_ym_ref, send_yp_ref):
    for q, old, new in ((0, to_ym_ref, send_ym_ref), (4, to_yp_ref, send_yp_ref)):
        new[0:3, :] = old[0:3, :] + from_xm_ref[q * 3 : q * 3 + 3, :]
        new[3:6, :] = old[3:6, :]
        new[6:9, :] = old[6:9, :] + from_xp_ref[q * 3 : q * 3 + 3, :]


def force_kernel(
    own_ref, picks_ref, from_xp_ref, from_xm_ref, from_yp_ref, from_ym_ref, out_ref, rim_sum
):
    rim_sum[...] = jnp.zeros_like(rim_sum)
    for a, ref in ((2, from_xp_ref), (0, from_xm_ref)):
        for b in range(3):
            rim_sum[rim_cells.index((a, b)), 0:3, :] += ref[(b + 1) * 3 : (b + 2) * 3, :]
    for b, ref in ((2, from_yp_ref), (0, from_ym_ref)):
        for a in range(3):
            rim_sum[rim_cells.index((a, b)), 0:3, :] += ref[a * 3 : (a + 1) * 3, :]
    total = jnp.zeros((48, LANES), f32)
    for rim in range(8):
        index = picks_ref[rim : rim + 1, :]
        mask = one_hot(lax.shift_right_logical(index, 7), 8)
        low = one_hot(lax.bitwise_and(index, LANES - 1), LANES).astype(bf16)
        values = rim_sum[rim]
        pieces = [halves(values[d : d + 1, :]) for d in range(3)]
        rows = jnp.concatenate(
            [mask * pieces[d][part] for part in range(2) for d in range(3)], axis=0
        ).astype(bf16)
        total = total + dot_t(rows, low)
    total = total[0:24] + total[24:48]
    for d in range(3):
        for high in range(out_ref.shape[2] // LANES):
            value = own_ref[d, high : high + 1, :] + total[d * 8 + high : d * 8 + high + 1, :]
            out_ref[d, :, high * LANES : (high + 1) * LANES] = -value


def call(kernel, out_shape, args, scratch=(), smem=0, limit=12 * 1024 * 1024):
    vmem = pl.BlockSpec(memory_space=pltpu.VMEM)
    scalar = pl.BlockSpec(memory_space=pltpu.SMEM)
    return pl.pallas_call(
        kernel,
        out_shape=out_shape,
        in_specs=[scalar] * smem + [vmem] * (len(args) - smem),
        out_specs=jax.tree.map(lambda _: vmem, out_shape),
        scratch_shapes=list(scratch),
        compiler_params=pltpu.CompilerParams(vmem_limit_bytes=limit),
    )(*args)


def shifted(x, axis, step):
    count = lax.axis_size(axis)
    return lax.ppermute(x, axis, [((i + step) % count, i) for i in range(count)])


def swapped(x):
    count = lax.axis_size("gz")
    return lax.ppermute(x, "gz", [(i, i ^ 1) for i in range(count)])


def per_device(
    positions,
    attributes,
    edge_center,
    edge_other,
    edge_count,
    rim_rows,
    z_rows,
    w_emb,
    w_rbf,
    w_chan,
    w_lat,
    w_ten,
    w_out,
):
    pos = positions.reshape(3, 1, -1)
    attr = attributes[0, 0, 0]
    rim = rim_rows[0, 0, 0]
    zr = z_rows[0, 0]
    count = edge_count[0, 0]
    atoms, width = attr.shape
    edges = edge_center.shape[-1]
    features = w_emb.shape[1]
    chans = w_chan.shape[1]
    height = width + PARTS
    inner_len = atoms + 16 * LANES
    table = inner_len + LANES
    hpad = -(-(table // LANES) // 8) * 8
    eb = BLOCK
    span = 2 * LANES
    pairs = -(-(edges // eb + atoms // span - 1) // 2)
    slot_rows = -(-(2 * pairs * eb // LANES) // 8) * 8
    lift = (1 - 2 * lax.axis_index("gz")).astype(f32).reshape(1)
    big = 44 * 1024 * 1024

    shape = jax.ShapeDtypeStruct
    picks = jnp.concatenate([rim, zr], axis=0)
    own, *sent = call(
        pack_kernel,
        (shape((height, atoms), bf16),) + (shape((height, 3 * LANES), bf16),) * 4,
        (pos, attr, picks),
        [pltpu.VMEM((PARTS, atoms), f32)],
    )
    got = [
        shifted(x, "gx" if way[0] else "gy", way[0] + way[1]) for x, way in zip(sent, sides)
    ]
    lines = edges // LANES
    groups = -(-table // 256)
    ends = jnp.concatenate(
        [edge_center.reshape(lines, LANES), edge_other.reshape(lines, LANES)], axis=0
    )
    bucketed = call(
        bucket_kernel,
        (
            shape((slot_rows, LANES), jnp.int32),
            shape((slot_rows, LANES), jnp.int32),
            shape((4, LANES), jnp.int32),
        ),
        (count, ends),
        [
            pltpu.VMEM((2 * groups * lines, LANES), bf16),
            pltpu.VMEM((4 * slot_rows, edges), bf16),
            pltpu.VMEM((LANES, edges), bf16),
        ],
        smem=1,
        limit=24 * 1024 * 1024,
    )
    first, bucketed = lax.optimization_barrier((got[:2], bucketed))
    got = [*first, *got[2:]]
    centers, others, meta = bucketed
    centers = centers.reshape(-1, 1, eb)
    others = others.reshape(-1, 1, eb)
    to_plus, to_minus = call(
        corner_kernel,
        (shape((height, 2 * LANES), bf16),) * 2,
        (got[0], got[1]),
    )
    w_emb, w_rbf, to_plus = lax.optimization_barrier((w_emb, w_rbf, to_plus))
    prepared = call(
        weights_kernel,
        (
            shape((features, width), bf16),
            shape((features, LANES), bf16),
            shape((features, chans), bf16),
            shape((chans, features), bf16),
            shape((features, features + 3 * chans), bf16),
            shape((features + 3 * chans, features), bf16),
            shape((features, LANES), f32),
            shape((16, features), bf16),
        ),
        (
            jnp.concatenate([w_emb, w_lat, w_ten, w_chan.T], axis=0),
            jnp.concatenate([w_rbf, w_out[None]], axis=0),
        ),
        [pltpu.VMEM((LANES, features), f32)],
    )
    corners = [shifted(to_plus, "gx", -1), shifted(to_minus, "gx", 1)]
    corners, prepared = lax.optimization_barrier((corners, prepared))
    w_emb_t, w_rad, w_chan_r, w_chan_t, w_hidden, w_back, w_out_col, w_rbf2 = prepared
    inner, slab_send = call(
        slab_kernel,
        (shape((height, inner_len), bf16), shape((height, LANES), bf16)),
        (own, picks, *got, *corners),
        [pltpu.VMEM((PARTS, inner_len), f32)],
    )
    slab_got = swapped(slab_send)
    feat, place = call(
        embed_kernel,
        (shape((features, inner_len), bf16), shape((6, hpad, LANES), f32)),
        (inner, w_emb_t),
    )
    grads, slab_grad, energy = call(
        edge_kernel,
        (shape((3, hpad, LANES), f32), shape((3, LANES), f32), shape((1, atoms), f32)),
        (
            meta,
            lift,
            centers,
            others,
            feat,
            place,
            slab_got,
            w_emb_t,
            w_rad,
            w_chan_t,
            w_chan_r,
            w_hidden,
            w_back,
            w_out_col,
            w_rbf2,
        ),
        [
            pltpu.VMEM((features, (groups - 1) * 256 + WINDOW), bf16),
            pltpu.VMEM((atoms // span, features, span + LANES), bf16),
            pltpu.VMEM((6, hpad, LANES), f32),
            pltpu.VMEM((6 * hpad + 48, 2 * LANES), bf16),
            pltpu.VMEM((atoms // span, 9 * chans, span), bf16),
        ]
        + [
            pltpu.VMEM((WINDOW + span + LANES, eb), bf16),
            pltpu.VMEM((features, eb), f32),
            pltpu.VMEM((pairs, span, eb), bf16),
            pltpu.VMEM((pairs, eb, span), bf16),
            pltpu.VMEM((pairs, 2 * LANES, eb), bf16),
            pltpu.VMEM((pairs, features, eb), bf16),
            pltpu.VMEM((pairs, features, eb), bf16),
            pltpu.VMEM((pairs, chans, eb), f32),
            pltpu.VMEM((16, -(-pairs // 8) * 8, eb), f32),
            pltpu.VMEM((11, -(-pairs // 8) * 8, eb), f32),
            pltpu.VMEM((pairs, features, eb), bf16),
            pltpu.VMEM((pairs, 64, eb), f32),
            pltpu.VMEM((atoms // span, 9 * chans, span), f32),
            pltpu.VMEM((atoms // span, 6 * hpad + 8 * (span // LANES), 2 * LANES), f32),
        ]
        * 2,
        smem=2,
        limit=big,
    )
    slab_back = swapped(slab_grad)
    along_x, along_y = shape((15, LANES), f32), shape((9, LANES), f32)
    own_grad, to_xm, to_xp, to_ym, to_yp = call(
        return_kernel,
        (shape((3, 8, LANES), f32), along_x, along_x, along_y, along_y),
        (grads, slab_back, picks),
    )
    from_xp, from_xm = shifted(to_xm, "gx", 1), shifted(to_xp, "gx", -1)
    to_ym, to_yp = call(turn_kernel, (along_y, along_y), (from_xp, from_xm, to_ym, to_yp))
    from_yp, from_ym = shifted(to_ym, "gy", 1), shifted(to_yp, "gy", -1)
    forces = call(
        force_kernel,
        shape((3, 1, atoms), f32),
        (own_grad, picks, from_xp, from_xm, from_yp, from_ym),
        [pltpu.VMEM((8, 8, LANES), f32)],
    )
    return (energy.reshape(1, 1, 1, atoms), forces.reshape(1, 1, 1, 3, atoms))


def solution(mesh):
    return jax.shard_map(
        per_device,
        mesh=mesh,
        in_specs=(
            P("gx", "gy", "gz", None, None),
            P("gx", "gy", "gz", None, None),
            P("gx", "gy", "gz", None),
            P("gx", "gy", "gz", None),
            P("gx", "gy", "gz"),
            P("gx", "gy", "gz", None, None),
            P("gx", "gy", "gz", None),
            P(),
            P(),
            P(),
            P(),
            P(),
            P(),
        ),
        out_specs=(P("gx", "gy", "gz", None), P("gx", "gy", "gz", None, None)),
        check_vma=False,
    )
```

```python
import collections

import jax
import jax.numpy as jnp
from jax import lax
from jax.experimental import pallas as pl
from jax.experimental.pallas import tpu as pltpu
from jax.sharding import PartitionSpec as P

f32 = jnp.float32
bf16 = jnp.bfloat16
LANES = 128
PARTS = 16
BLOCK = 512
SETS = 4
SUMS = 2
WINDOW = 768
ROOT3 = 3.0**0.5
BANDS = (0, 1, 1, 1, 2, 2, 2, 2, 2)

rim_cells = [(0, 0), (0, 1), (0, 2), (1, 0), (1, 2), (2, 0), (2, 1), (2, 2)]
cycle_cells = [(p, q) for p in range(5) for q in range(5) if p in (0, 4) or q in (0, 4)]


def source_of(position):
    if position == 0:
        return (-1, 2)
    if position == 4:
        return (1, 0)
    return (0, position - 1)


routes = {}
for _cycle, (_p, _q) in enumerate(cycle_cells):
    (_sx, _a), (_sy, _b) = source_of(_p), source_of(_q)
    routes.setdefault((_sx, _sy), []).append((_cycle, rim_cells.index((_a, _b))))
sides = [(0, -1), (0, 1), (-1, 0), (1, 0)]


def dot(a, b):
    return lax.dot_general(a, b, (((1,), (0,)), ((), ())), preferred_element_type=f32)


def dot_t(a, b):
    return lax.dot_general(a, b, (((1,), (1,)), ((), ())), preferred_element_type=f32)


def rows_of(shape):
    return lax.broadcasted_iota(jnp.int32, shape, 0)


def one_hot(index, size):
    return jnp.where(rows_of((size, index.shape[1])) == index, 1.0, 0.0)


def halves(values):
    upper = values.astype(bf16).astype(f32)
    return upper, values - upper


def masked(hot_low, high16, value):
    mask = jnp.where(high16 == value, 1.0, 0.0).astype(bf16)
    size, lanes = hot_low.shape
    return (hot_low.reshape(size // 16, 16, lanes) * mask[None]).reshape(size, lanes)


def half_silu(x):
    half = 0.5 * x
    return (0.5 * (half * (1.0 + jnp.tanh(half)))).astype(bf16)


def pack_kernel(pos_ref, attr_ref, picks_ref, own_ref, *rest):
    sends, parts = rest[:4], rest[4]
    atoms, width = attr_ref.shape
    eye = jnp.where(
        rows_of((width, width)) == lax.broadcasted_iota(jnp.int32, (width, width), 1), 1.0, 0.0
    ).astype(bf16)
    own_ref[0:width, :] = dot_t(eye, attr_ref[...]).astype(bf16)
    parts[...] = jnp.zeros_like(parts)
    for d in range(3):
        parts[d : d + 1, :], parts[3 + d : 4 + d, :] = halves(pos_ref[d])
    own_ref[width : width + PARTS, :] = parts[...].astype(bf16)
    packed = own_ref[...]
    for rim in range(8):
        hot = one_hot(picks_ref[rim : rim + 1, :], atoms).astype(bf16)
        cell = dot(packed, hot).astype(bf16)
        for way, send in zip(sides, sends):
            for slot, (_, source) in enumerate(routes[way]):
                if source == rim:
                    send[:, slot * LANES : (slot + 1) * LANES] = cell


def corner_kernel(minus_ref, plus_ref, to_plus_ref, to_minus_ref):
    first, last = slice(0, LANES), slice(2 * LANES, 3 * LANES)
    for slot, ref in enumerate((minus_ref, plus_ref)):
        lanes = slice(slot * LANES, (slot + 1) * LANES)
        to_plus_ref[:, lanes] = ref[:, last]
        to_minus_ref[:, lanes] = ref[:, first]


def slab_kernel(own_ref, picks_ref, *rest):
    got, corners, (inner_ref, send_ref, parts) = rest[:4], rest[4:6], rest[6:]
    atoms = own_ref.shape[1]
    height = own_ref.shape[0]
    width = height - PARTS
    inner_len = inner_ref.shape[1]
    inner_ref[:, 0:atoms] = own_ref[...]
    parts[...] = jnp.zeros_like(parts)
    parts[0:6, 0:atoms] = own_ref[width:height, :].astype(f32)[0:6]
    arrivals = []
    for way, ref in zip(sides, got):
        for slot, (cycle, _) in enumerate(routes[way]):
            arrivals.append((way, ref, slot, cycle))
    for sx, ref in zip((-1, 1), corners):
        for slot, sy in enumerate((-1, 1)):
            arrivals.append(((sx, sy), ref, slot, routes[(sx, sy)][0][0]))
    for way, ref, slot, cycle in arrivals:
        lanes = slice(slot * LANES, (slot + 1) * LANES)
        into = slice(atoms + cycle * LANES, atoms + (cycle + 1) * LANES)
        inner_ref[0:width, into] = ref[0:width, lanes]
        arrived = ref[width:height, lanes].astype(f32)
        joined = arrived[0:3] + arrived[3:6]
        axis = rows_of((3, LANES))
        shift = jnp.where(axis == 0, float(way[0]), jnp.where(axis == 1, float(way[1]), 0.0))
        upper, lower = halves(joined + shift)
        parts[0:3, into] = upper
        parts[3:6, into] = lower
    inner_ref[width:height, :] = parts[...].astype(bf16)
    hot = one_hot(picks_ref[8:9, :], inner_len).astype(bf16)
    send_ref[...] = dot(inner_ref[...], hot).astype(bf16)


def unit(size):
    lanes = lax.broadcasted_iota(jnp.int32, (size, size), 1)
    return jnp.where(rows_of((size, size)) == lanes, 1.0, 0.0)


def weights_kernel(
    stacked_ref,
    small_ref,
    emb_t_ref,
    rad_ref,
    chan_ref,
    w_chan_t_ref,
    hidden_ref,
    back_ref,
    out_ref,
    rbf_ref,
    scratch,
):
    features = stacked_ref.shape[1]
    width = emb_t_ref.shape[1]
    inner = back_ref.shape[0]
    w_emb = stacked_ref[0:width]
    w_back = stacked_ref[width : width + inner]
    w_chan_t = stacked_ref[width + inner :]
    eye = unit(features)
    eye_b = eye.astype(bf16)
    emb_t_ref[...] = dot_t(eye_b, w_emb).astype(bf16)
    chan_ref[...] = dot_t(eye_b, w_chan_t).astype(bf16)
    w_chan_t_ref[...] = w_chan_t
    turned = (0.5 * dot_t(eye_b, w_back)).astype(bf16)
    hidden_ref[...] = turned
    back_ref[...] = w_back
    column = jnp.sum(eye * small_ref[8:9, :], axis=1, keepdims=True)
    out_ref[...] = jnp.broadcast_to(column, out_ref.shape)
    upper, lower = halves(0.5 * small_ref[0:8, :])
    rbf_ref[...] = jnp.concatenate([upper, lower], axis=0).astype(bf16)
    scratch[...] = jnp.zeros_like(scratch)
    for start, value in ((0, upper), (8, upper), (16, lower), (24, lower)):
        scratch[start : start + 8, :] = value
    rad_ref[...] = dot_t(eye_b, scratch[...].astype(bf16)).astype(bf16)


def embed_kernel(inner_ref, w_emb_ref, feat_ref, place_ref):
    width = w_emb_ref.shape[1]
    inner_len = inner_ref.shape[1]
    for first in range(0, inner_len, 512):
        raw = dot(w_emb_ref[...], inner_ref[0:width, first : first + 512])
        feat_ref[:, first : first + 512] = half_silu(raw)
    parts = inner_ref[width:, :].astype(f32)
    place_ref[...] = jnp.zeros_like(place_ref)
    for high in range(inner_len // LANES):
        place_ref[0:6, high, :] = parts[0:6, high * LANES : (high + 1) * LANES]


def bucket_kernel(count_ref, ends_ref, center_ref, other_ref, meta_ref, marks_s, rows_s, low_s):
    lines = ends_ref.shape[0] // 2
    keys = marks_s.shape[0] // lines
    groups = keys // 2
    count = count_ref[0]
    c, o = ends_ref[0:lines, :], ends_ref[lines:, :]
    shape = (lines, LANES)
    order = rows_of(shape) * LANES + lax.broadcasted_iota(jnp.int32, shape, 1)
    key = lax.shift_right_logical(c, 8) * groups + lax.shift_right_logical(o, 8)
    key = jnp.where(order < count, key, -1)
    for k in range(keys):
        marks_s[k * lines : (k + 1) * lines, :] = jnp.where(key == k, 1.0, 0.0).astype(bf16)
    square = (LANES, LANES)
    tri = jnp.where(rows_of(square) < lax.broadcasted_iota(jnp.int32, square, 1), 1.0, 0.0)
    tri = tri.astype(bf16)
    tall = (lines, lines)
    below = jnp.where(lax.broadcasted_iota(jnp.int32, tall, 1) < rows_of(tall), 1.0, 0.0)
    marks = marks_s[...]
    inside = dot(marks, tri)
    totals = dot(marks, jnp.ones(square, bf16))
    lane = lax.broadcasted_iota(jnp.int32, shape, 1)
    by_key = jnp.zeros(shape, f32)
    for k in range(keys):
        by_key = jnp.where(lane == k, totals[k * lines : (k + 1) * lines], by_key)
    before = dot(below.astype(bf16), by_key.astype(bf16))
    everything = jnp.broadcast_to(jnp.sum(by_key, axis=0, keepdims=True), (16, LANES))
    upper, lower = halves(everything)
    start = (dot(upper.astype(bf16), tri) + dot(lower.astype(bf16), tri))[0:1]
    row_lane = lane[0:1]
    first = jnp.sum(jnp.where(row_lane < groups, everything[0:1], 0.0), axis=1, keepdims=True)
    second = jnp.sum(jnp.where(row_lane >= groups, everything[0:1], 0.0), axis=1, keepdims=True)
    first_blocks = jnp.floor((first + (BLOCK - 1)) * (1.0 / BLOCK))
    blocks = first_blocks + jnp.floor((second + (BLOCK - 1)) * (1.0 / BLOCK))
    start = start + jnp.where(row_lane >= groups, first_blocks * BLOCK - first, 0.0)
    offset = before + start
    slot = jnp.full(shape, -1.0, f32)
    for k in range(keys):
        place = inside[k * lines : (k + 1) * lines] + offset[:, k : k + 1]
        slot = jnp.where(key == k, place, slot)
    slot = slot.astype(jnp.int32)
    slot_high = lax.shift_right_arithmetic(slot, 7)
    slot_low = lax.bitwise_and(slot, LANES - 1)
    highs = center_ref.shape[0]
    values = [
        jnp.ones(shape, f32),
        lax.bitwise_and(c, 255).astype(f32),
        lax.shift_right_logical(o, 7).astype(f32),
        lax.bitwise_and(o, LANES - 1).astype(f32),
    ]
    for line in range(lines):
        lanes = slice(line * LANES, (line + 1) * LANES)
        high = one_hot(slot_high[line : line + 1], highs)
        rows_s[:, lanes] = jnp.concatenate(
            [high * value[line : line + 1] for value in values], axis=0
        ).astype(bf16)
        low_s[:, lanes] = one_hot(slot_low[line : line + 1], LANES).astype(bf16)
    placed = dot_t(rows_s[...], low_s[...])
    center = placed[highs : 2 * highs] + placed[0:highs] - 1.0
    other = placed[2 * highs : 3 * highs] * float(LANES) + placed[3 * highs :]
    center_ref[...] = center.astype(jnp.int32)
    other_ref[...] = other.astype(jnp.int32)
    group = jnp.floor(other * (1.0 / 256.0))
    none = float(groups)
    low = jnp.min(jnp.where(center >= 0.0, group, none), axis=1, keepdims=True)
    high = jnp.max(jnp.where(center >= 0.0, group, -1.0), axis=1, keepdims=True)
    block = lax.broadcasted_iota(jnp.int32, (highs, LANES), 1)
    line_of = rows_of((highs, LANES)) // (BLOCK // LANES) == block
    low = jnp.min(jnp.where(line_of, low, none), axis=0, keepdims=True)
    high = jnp.max(jnp.where(line_of, high, -1.0), axis=0, keepdims=True)
    low = jnp.where(high < 0.0, 0.0, low)
    high = jnp.where(high < 0.0, 0.0, high)
    meta_ref[0:1, :] = jnp.broadcast_to(first_blocks, (1, LANES)).astype(jnp.int32)
    meta_ref[1:2, :] = jnp.broadcast_to(blocks, (1, LANES)).astype(jnp.int32)
    meta_ref[2:3, :] = low.astype(jnp.int32)
    meta_ref[3:4, :] = high.astype(jnp.int32)


def harmonic_rows(x, y, z):
    return [
        None,
        x,
        y,
        z,
        ROOT3 * x * y,
        ROOT3 * y * z,
        ROOT3 * z * x,
        0.5 * ROOT3 * (x * x - y * y),
        0.5 * (3.0 * z * z - 1.0),
    ]


def fold8(values):
    return jnp.sum(values.reshape(values.shape[0] // 8, 8, values.shape[1]), axis=0)


FIELDS = (
    ["hot", "extra", "center_hot", "lows", "latent", "slope", "chan"]
    + ["geo", "res", "dlat", "dharm", "tensor", "acc"]
)
Scratch = collections.namedtuple("Scratch", FIELDS)


def edge_kernel(
    meta_ref,
    lift_ref,
    centers_ref,
    others_ref,
    feat_in_ref,
    place_in_ref,
    slab_ref,
    w_emb_ref,
    w_rad_ref,
    w_chan_t_ref,
    w_chan_ref,
    w_hidden_ref,
    w_back_ref,
    w_out_ref,
    w_rbf_ref,
    grad_ref,
    slab_grad_ref,
    energy_ref,
    feat,
    feat_c,
    place,
    place_b,
    tensor_b,
    *scratch,
):
    names = len(FIELDS) - 2
    sums = [scratch[names * SETS + index :: SUMS] for index in range(SUMS)]
    sets = [
        Scratch(*scratch[index * names : (index + 1) * names], *sums[index % SUMS])
        for index in range(SETS)
    ]
    eb = centers_ref.shape[2]
    width = w_emb_ref.shape[1]
    features = feat_in_ref.shape[0]
    inner_len = feat_in_ref.shape[1]
    table = inner_len + LANES
    highs = table // LANES
    span = tensor_b.shape[2]
    halves_n = tensor_b.shape[0]
    chans = w_chan_ref.shape[1]
    hpad = place_in_ref.shape[1]
    first_blocks = meta_ref[0, 0]
    total_blocks = meta_ref[1, 0]
    rounds = total_blocks // SETS

    feat[:, 0:inner_len] = feat_in_ref[...]
    raw = dot(w_emb_ref[...], slab_ref[0:width, :])
    feat[:, inner_len:table] = half_silu(raw)
    feat[:, table:] = jnp.zeros((features, feat.shape[1] - table), bf16)
    for half in range(halves_n):
        feat_c[half, :, 0:span] = feat_in_ref[:, half * span : (half + 1) * span]
        feat_c[half, :, span:] = w_rad_ref[...]
    place[...] = place_in_ref[...]
    arrived = slab_ref[width:, :].astype(f32)
    joined = arrived[0:3] + arrived[3:6]
    joined = joined + jnp.where(rows_of((3, LANES)) == 2, lift_ref[0], 0.0)
    upper, lower = halves(joined)
    place[0:3, highs - 1, :] = upper
    place[3:6, highs - 1, :] = lower
    place_b[...] = jnp.zeros_like(place_b)
    place_b[0 : 6 * hpad, 0:LANES] = place[...].reshape(6 * hpad, LANES).astype(bf16)
    place_b[6 * hpad :, LANES:] = place[:, 0:8, :].reshape(48, LANES).astype(bf16)
    for own in sets:
        own.hot[WINDOW + span + 32 :, :] = jnp.zeros((LANES - 32, eb), bf16)
        for ref in (own.extra, own.tensor, own.acc):
            ref[...] = jnp.zeros_like(ref)

    def half_of(b):
        return jnp.where(b >= first_blocks, 1, 0)

    def each_block(run):
        def sides(at, picked):
            return [(sets[index], SETS * at + index, at) for index in picked]

        def step(at, carry):
            run(sides(at, range(SETS)))
            return carry

        lax.fori_loop(0, rounds, step, 0)
        rest = total_blocks - SETS * rounds

        @pl.when(rest == 1)
        def _():
            run(sides(rounds, [0]))

        @pl.when(rest > 1)
        def _():
            run(sides(rounds, [0, 1]))

        @pl.when(rest == 3)
        def _():
            run(sides(rounds, [2]))

    def locate(sides):
        for own_s, b, at in sides:
            slot_c = centers_ref[b]
            o = others_ref[b]
            c = jnp.maximum(slot_c, 0)
            c_high = lax.shift_right_logical(c, 7)
            o_high = lax.shift_right_logical(o, 7)
            hot_c = one_hot(lax.bitwise_and(c, LANES - 1), LANES).astype(bf16)
            hot_o = one_hot(lax.bitwise_and(o, LANES - 1), LANES).astype(bf16)
            lows = jnp.concatenate([hot_o, hot_c], axis=0)
            own_s.lows[at] = lows
            c_high16 = jnp.broadcast_to(c_high, (16, eb))
            own_s.center_hot[at] = jnp.concatenate(
                [masked(hot_c, c_high16, high) for high in range(span // LANES)], axis=0
            )
            both = dot(place_b[...], lows)
            picked = (both[0 : 3 * hpad] + both[3 * hpad : 6 * hpad]).reshape(3, hpad, eb)
            po = jnp.sum(picked * one_hot(o_high, hpad)[None], axis=1)
            picked = both[6 * hpad :]
            picked = (picked[0:24] + picked[24:48]).reshape(3, 8, eb)
            c_whole = c_high + half_of(b) * (span // LANES)
            pc = jnp.sum(picked * one_hot(c_whole, 8)[None], axis=1)
            sep = po - pc
            row = pl.ds(at, 1)
            for d in range(3):
                own_s.geo[d, row, :] = sep[d : d + 1]
            own_s.geo[6, row, :] = jnp.where(slot_c >= 0, 1.0, 0.0)

    each_block(locate)
    for own in sets:
        rx, ry, rz = own.geo[0], own.geo[1], own.geo[2]
        squared = rx * rx + ry * ry + rz * rz
        inv_d = lax.rsqrt(squared + 0.25)
        x, y, z = rx * inv_d, ry * inv_d, rz * inv_d
        own.geo[3] = inv_d
        own.geo[4] = (squared + 0.25) * inv_d
        own.geo[5] = 1.0 / (1.0 + squared * squared * (1.0 / 16.0))
        own.geo[7] = squared
        for m, value in enumerate(harmonic_rows(x, y, z)[1:]):
            own.geo[8 + m] = value

    def geo_row(side, index):
        own_s, _, at = side
        return own_s.geo[index, pl.ds(at, 1), :]

    def harmonics(side):
        return [None] + [geo_row(side, 8 + m) for m in range(8)]

    def prepare(side):
        own_s, b, at = side
        hot = own_s.hot
        hot_o = own_s.lows[at, 0:LANES, :]
        o_high = lax.shift_right_logical(others_ref[b], 7) - 2 * meta_ref[2, b]
        o_high16 = jnp.broadcast_to(o_high, (16, eb))
        for high in range(WINDOW // LANES):
            rows = slice(high * LANES, (high + 1) * LANES)
            hot[rows, :] = masked(hot_o, o_high16, high)
        hot[WINDOW : WINDOW + span, :] = own_s.center_hot[at]
        mu = 0.5 + 0.4 * rows_of((8, eb)).astype(f32)
        u = (geo_row(side, 4) - mu) * 2.0
        upper, lower = halves(jnp.exp(-(u * u)) * geo_row(side, 5))
        radial = jnp.concatenate([upper, lower], axis=0).astype(bf16)
        hot[WINDOW + span : WINDOW + span + 16, :] = radial
        hot[WINDOW + span + 16 : WINDOW + span + 32, :] = radial

    def window(group):
        return feat[:, pl.ds(pl.multiple_of(group * 256, 256), WINDOW)]

    def windows_of(side):
        b = side[1]
        return (meta_ref[3, b] - meta_ref[2, b]) // (WINDOW // 256) + 1

    def further_windows(side):
        own_s, b, _ = side
        windows = windows_of(side)

        @pl.when(windows > 1)
        def _():
            o = others_ref[b]
            hot_o = one_hot(lax.bitwise_and(o, LANES - 1), LANES).astype(bf16)
            o_high16 = jnp.broadcast_to(lax.shift_right_logical(o, 7), (16, eb))

            def add(index, carry):
                group = meta_ref[2, b] + index * (WINDOW // 256)
                hot = jnp.concatenate(
                    [
                        masked(hot_o, o_high16 - 2 * group, high)
                        for high in range(WINDOW // LANES)
                    ],
                    axis=0,
                )
                own_s.extra[...] += dot(window(group), hot)
                return carry

            lax.fori_loop(1, windows, add, 0)

    def clear_windows(side):
        @pl.when(windows_of(side) > 1)
        def _():
            side[0].extra[...] = jnp.zeros_like(side[0].extra)

    def mix(side):
        own_s, b, _ = side
        tables = jnp.concatenate([window(meta_ref[2, b]), feat_c[half_of(b)]], axis=1)
        return dot(tables, own_s.hot[...]) + own_s.extra[...]

    def activate(side, mixed):
        own_s, _, at = side
        up = 1.0 + jnp.tanh(mixed)
        value = mixed * up
        latent = value.astype(bf16)
        own_s.slope[at] = (up + value * (2.0 - up)).astype(bf16)
        return latent

    def spread(side, latent):
        own_s, _, at = side
        own_s.latent[at] = latent
        chan = dot(w_chan_t_ref[...], latent) * geo_row(side, 6)
        own_s.chan[at] = chan
        return jnp.concatenate(
            [(chan if h is None else chan * h).astype(bf16) for h in harmonics(side)], axis=0
        )

    def gather_tensor(side):
        own_s, b, at = side
        return dot(tensor_b[half_of(b)], own_s.center_hot[at])

    def add_tensor(side, products, hot):
        own_s, b, _ = side
        own_s.tensor[half_of(b)] += dot_t(products, hot)

    def first_pass(sides):
        for side in sides:
            further_windows(side)
        mixed = []
        for side in sides:
            prepare(side)
            mixed.append(mix(side))
        products = []
        for side, values in zip(sides, mixed):
            products.append(spread(side, activate(side, values)))
        for side, values in zip(sides, products):
            add_tensor(side, values, side[0].center_hot[side[2]])
        for side in sides:
            clear_windows(side)

    each_block(first_pass)
    tensor_b[...] = (0.125 * sum(own.tensor[...] for own in sets[:SUMS])).astype(bf16)
    for own in sets[:SUMS]:
        own.tensor[...] = jnp.zeros_like(own.tensor)

    def invariants(side, gathered):
        harm = harmonics(side)
        parts = [gathered[m * chans : (m + 1) * chans] for m in range(9)]
        bands = [parts[0], None, None]
        for m in range(1, 9):
            term = parts[m] * harm[m]
            band = BANDS[m]
            bands[band] = term if bands[band] is None else bands[band] + term
        return jnp.concatenate([band.astype(bf16) for band in bands], axis=0)

    def hidden(side, invariant):
        inputs = jnp.concatenate([side[0].latent[side[2]], invariant], axis=0)
        return dot(w_hidden_ref[...], inputs)

    def readout(side, pre):
        own_s, _, at = side
        up = 1.0 + jnp.tanh(pre)
        value = pre * up
        weight = jnp.concatenate([w_out_ref[...]] * (eb // LANES), axis=1)
        own_s.res[10, pl.ds(at, 1), :] = jnp.sum(value * weight, axis=0, keepdims=True)
        scale = 0.5 * geo_row(side, 5) * geo_row(side, 6)
        return ((up + value * (2.0 - up)) * (weight * scale)).astype(bf16)

    def unfold(side, back, gathered):
        own_s, _, at = side
        harm = harmonics(side)
        own_s.dlat[at] = back[0:features].astype(bf16)
        dbands = [
            back[features + band * chans : features + (band + 1) * chans] for band in range(3)
        ]
        for m in range(1, 9):
            part = gathered[m * chans : (m + 1) * chans]
            own_s.dharm[at, (m - 1) * 8 : m * 8, :] = fold8(dbands[BANDS[m]] * part)
        return jnp.concatenate(
            [
                (dbands[BANDS[m]] if harm[m] is None else dbands[BANDS[m]] * harm[m]).astype(bf16)
                for m in range(9)
            ],
            axis=0,
        )

    def second_pass(sides):
        gathered = [gather_tensor(side) for side in sides]
        pre = [hidden(side, invariants(side, g)) for side, g in zip(sides, gathered)]
        back = [dot(w_back_ref[...], readout(side, values)) for side, values in zip(sides, pre)]
        for side, values, g in zip(sides, back, gathered):
            add_tensor(side, unfold(side, values, g), side[0].center_hot[side[2]])

    each_block(second_pass)
    tensor_b[...] = (0.125 * sum(own.tensor[...] for own in sets[:SUMS])).astype(bf16)

    def channels_back(side, gathered):
        own_s, _, at = side
        harm = harmonics(side)
        chan = own_s.chan[at]
        dchan = gathered[0:chans]
        for m in range(1, 9):
            part = gathered[m * chans : (m + 1) * chans]
            dchan = dchan + part * harm[m]
            total = own_s.dharm[at, (m - 1) * 8 : m * 8, :] + fold8(part * chan)
            own_s.res[m - 1, pl.ds(at, 1), :] = jnp.sum(total, axis=0, keepdims=True)
        return (dchan * geo_row(side, 6)).astype(bf16)

    def radial_back(side, dchan):
        own_s, _, at = side
        dlat = own_s.dlat[at] + dot(w_chan_ref[...], dchan).astype(bf16)
        drad = dot(w_rbf_ref[...], dlat * own_s.slope[at])
        drad = drad[0:8] + drad[8:16]
        mu = 0.5 + 0.4 * rows_of((8, eb)).astype(f32)
        u = (geo_row(side, 4) - mu) * 2.0
        weighted = drad * jnp.exp(-(u * u))
        own_s.res[8, pl.ds(at, 1), :] = jnp.sum(weighted, axis=0, keepdims=True)
        own_s.res[9, pl.ds(at, 1), :] = jnp.sum(weighted * u, axis=0, keepdims=True)

    def third_pass(sides):
        gathered = [gather_tensor(side) for side in sides]
        for side, g in zip(sides, gathered):
            radial_back(side, channels_back(side, g))

    each_block(third_pass)

    for own in sets:
        x, y, z = own.geo[8], own.geo[9], own.geo[10]
        inv_d, dist, env = own.geo[3], own.geo[4], own.geo[5]
        live, squared = own.geo[6], own.geo[7]
        dh = [None] + [own.res[m] for m in range(8)]
        summed = own.res[10]
        denv = own.res[8] + live * summed
        ddist = -4.0 * env * own.res[9]
        dx = dh[1] + ROOT3 * (y * dh[4] + z * dh[6] + x * dh[7])
        dy = dh[2] + ROOT3 * (x * dh[4] + z * dh[5] - y * dh[7])
        dz = dh[3] + ROOT3 * (y * dh[5] + x * dh[6]) + 3.0 * z * dh[8]
        ddist = ddist - (dx * x + dy * y + dz * z) * inv_d
        dsq = denv * (env * env * squared * -0.125) + ddist * (0.5 * inv_d)
        both = 2.0 * dsq * dist
        results = [dx * inv_d + both * x, dy * inv_d + both * y, dz * inv_d + both * z]
        results.append(summed * env * live)
        for index, value in enumerate(results):
            own.res[index], own.res[4 + index] = halves(value)

    def collect(sides):
        for own_s, b, at in sides:
            split = [own_s.res[index, pl.ds(at, 1), :] for index in range(8)]
            mask_o = one_hot(lax.shift_right_logical(others_ref[b], 7), hpad)
            values = jnp.concatenate(split, axis=0)
            c_high = lax.shift_right_arithmetic(centers_ref[b], 7)
            rows = jnp.concatenate(
                [mask_o * split[4 * part + d] for part in range(2) for d in range(3)]
                + [
                    values * jnp.where(c_high == high, 1.0, 0.0)
                    for high in range(span // LANES)
                ],
                axis=0,
            ).astype(bf16)
            own_s.acc[half_of(b)] += dot_t(rows, own_s.lows[at])

    each_block(collect)
    acc = [sum(own.acc[half] for own in sets[:SUMS]) for half in range(halves_n)]
    sum_o = sum(value[0 : 6 * hpad, 0:LANES] for value in acc)
    sum_o = sum_o[0 : 3 * hpad] + sum_o[3 * hpad :]
    for d in range(3):
        grad_ref[d] = sum_o[d * hpad : (d + 1) * hpad]
        slab_grad_ref[d : d + 1, :] = sum_o[d * hpad + highs - 1 : d * hpad + highs]
    for half in range(halves_n):
        for part in range(span // LANES):
            high = half * (span // LANES) + part
            base = 6 * hpad + part * 8
            sum_c = acc[half][base : base + 4, LANES:] + acc[half][base + 4 : base + 8, LANES:]
            for d in range(3):
                grad_ref[d, high : high + 1, :] = (
                    sum_o[d * hpad + high : d * hpad + high + 1] - sum_c[d : d + 1]
                )
            energy_ref[:, high * LANES : (high + 1) * LANES] = sum_c[3:4]


def return_kernel(grad_ref, back_ref, picks_ref, own_ref, to_xm_ref, to_xp_ref, to_ym_ref, to_yp_ref):
    hpad = grad_ref.shape[1]
    z_rows = picks_ref[8:9, :]
    mask = one_hot(lax.shift_right_logical(z_rows, 7), hpad)
    low = one_hot(lax.bitwise_and(z_rows, LANES - 1), LANES).astype(bf16)
    pieces = [halves(back_ref[d : d + 1, :]) for d in range(3)]
    rows = jnp.concatenate(
        [mask * pieces[d][part] for part in range(2) for d in range(3)], axis=0
    ).astype(bf16)
    landed = dot_t(rows, low)
    landed = landed[0 : 3 * hpad] + landed[3 * hpad :]
    base = own_ref.shape[1] // 2
    for d in range(3):
        total = grad_ref[d] + landed[d * hpad : (d + 1) * hpad]
        own_ref[d] = total[0:8]
        for cycle, (p, q) in enumerate(cycle_cells):
            value = total[base + cycle : base + cycle + 1]
            if p in (0, 4):
                ref = to_xm_ref if p == 0 else to_xp_ref
                ref[q * 3 + d : q * 3 + d + 1, :] = value
            else:
                ref = to_ym_ref if q == 0 else to_yp_ref
                ref[(p - 1) * 3 + d : (p - 1) * 3 + d + 1, :] = value


def turn_kernel(from_xp_ref, from_xm_ref, to_ym_ref, to_yp_ref, send_ym_ref, send_yp_ref):
    for q, old, new in ((0, to_ym_ref, send_ym_ref), (4, to_yp_ref, send_yp_ref)):
        new[0:3, :] = old[0:3, :] + from_xm_ref[q * 3 : q * 3 + 3, :]
        new[3:6, :] = old[3:6, :]
        new[6:9, :] = old[6:9, :] + from_xp_ref[q * 3 : q * 3 + 3, :]


def force_kernel(
    own_ref, picks_ref, from_xp_ref, from_xm_ref, from_yp_ref, from_ym_ref, out_ref, rim_sum
):
    rim_sum[...] = jnp.zeros_like(rim_sum)
    for a, ref in ((2, from_xp_ref), (0, from_xm_ref)):
        for b in range(3):
            rim_sum[rim_cells.index((a, b)), 0:3, :] += ref[(b + 1) * 3 : (b + 2) * 3, :]
    for b, ref in ((2, from_yp_ref), (0, from_ym_ref)):
        for a in range(3):
            rim_sum[rim_cells.index((a, b)), 0:3, :] += ref[a * 3 : (a + 1) * 3, :]
    total = jnp.zeros((48, LANES), f32)
    for rim in range(8):
        index = picks_ref[rim : rim + 1, :]
        mask = one_hot(lax.shift_right_logical(index, 7), 8)
        low = one_hot(lax.bitwise_and(index, LANES - 1), LANES).astype(bf16)
        values = rim_sum[rim]
        pieces = [halves(values[d : d + 1, :]) for d in range(3)]
        rows = jnp.concatenate(
            [mask * pieces[d][part] for part in range(2) for d in range(3)], axis=0
        ).astype(bf16)
        total = total + dot_t(rows, low)
    total = total[0:24] + total[24:48]
    for d in range(3):
        for high in range(out_ref.shape[2] // LANES):
            value = own_ref[d, high : high + 1, :] + total[d * 8 + high : d * 8 + high + 1, :]
            out_ref[d, :, high * LANES : (high + 1) * LANES] = -value


def call(kernel, out_shape, args, scratch=(), smem=0, limit=12 * 1024 * 1024):
    vmem = pl.BlockSpec(memory_space=pltpu.VMEM)
    scalar = pl.BlockSpec(memory_space=pltpu.SMEM)
    return pl.pallas_call(
        kernel,
        out_shape=out_shape,
        in_specs=[scalar] * smem + [vmem] * (len(args) - smem),
        out_specs=jax.tree.map(lambda _: vmem, out_shape),
        scratch_shapes=list(scratch),
        compiler_params=pltpu.CompilerParams(vmem_limit_bytes=limit),
    )(*args)


def shifted(x, axis, step):
    count = lax.axis_size(axis)
    return lax.ppermute(x, axis, [((i + step) % count, i) for i in range(count)])


def swapped(x):
    count = lax.axis_size("gz")
    return lax.ppermute(x, "gz", [(i, i ^ 1) for i in range(count)])


def per_device(
    positions,
    attributes,
    edge_center,
    edge_other,
    edge_count,
    rim_rows,
    z_rows,
    w_emb,
    w_rbf,
    w_chan,
    w_lat,
    w_ten,
    w_out,
):
    pos = positions.reshape(3, 1, -1)
    attr = attributes[0, 0, 0]
    rim = rim_rows[0, 0, 0]
    zr = z_rows[0, 0]
    count = edge_count[0, 0]
    atoms, width = attr.shape
    edges = edge_center.shape[-1]
    features = w_emb.shape[1]
    chans = w_chan.shape[1]
    height = width + PARTS
    inner_len = atoms + 16 * LANES
    table = inner_len + LANES
    hpad = -(-(table // LANES) // 8) * 8
    eb = BLOCK
    span = 2 * LANES
    blocks = edges // eb + atoms // span - 1
    depth = -(-blocks // SETS)
    slot_rows = -(-(blocks * eb // LANES) // 8) * 8
    lift = (1 - 2 * lax.axis_index("gz")).astype(f32).reshape(1)
    big = 47 * 1024 * 1024

    shape = jax.ShapeDtypeStruct
    picks = jnp.concatenate([rim, zr], axis=0)
    own, *sent = call(
        pack_kernel,
        (shape((height, atoms), bf16),) + (shape((height, 3 * LANES), bf16),) * 4,
        (pos, attr, picks),
        [pltpu.VMEM((PARTS, atoms), f32)],
    )
    got = [
        shifted(x, "gx" if way[0] else "gy", way[0] + way[1]) for x, way in zip(sent, sides)
    ]
    lines = edges // LANES
    groups = -(-table // 256)
    ends = jnp.concatenate(
        [edge_center.reshape(lines, LANES), edge_other.reshape(lines, LANES)], axis=0
    )
    bucketed = call(
        bucket_kernel,
        (
            shape((slot_rows, LANES), jnp.int32),
            shape((slot_rows, LANES), jnp.int32),
            shape((4, LANES), jnp.int32),
        ),
        (count, ends),
        [
            pltpu.VMEM((2 * groups * lines, LANES), bf16),
            pltpu.VMEM((4 * slot_rows, edges), bf16),
            pltpu.VMEM((LANES, edges), bf16),
        ],
        smem=1,
        limit=24 * 1024 * 1024,
    )
    first, bucketed = lax.optimization_barrier((got[:2], bucketed))
    got = [*first, *got[2:]]
    centers, others, meta = bucketed
    centers = centers.reshape(-1, 1, eb)
    others = others.reshape(-1, 1, eb)
    to_plus, to_minus = call(
        corner_kernel,
        (shape((height, 2 * LANES), bf16),) * 2,
        (got[0], got[1]),
    )
    w_emb, w_rbf, to_plus = lax.optimization_barrier((w_emb, w_rbf, to_plus))
    prepared = call(
        weights_kernel,
        (
            shape((features, width), bf16),
            shape((features, LANES), bf16),
            shape((features, chans), bf16),
            shape((chans, features), bf16),
            shape((features, features + 3 * chans), bf16),
            shape((features + 3 * chans, features), bf16),
            shape((features, LANES), f32),
            shape((16, features), bf16),
        ),
        (
            jnp.concatenate([w_emb, w_lat, w_ten, w_chan.T], axis=0),
            jnp.concatenate([w_rbf, w_out[None]], axis=0),
        ),
        [pltpu.VMEM((LANES, features), f32)],
    )
    corners = [shifted(to_plus, "gx", -1), shifted(to_minus, "gx", 1)]
    corners, prepared = lax.optimization_barrier((corners, prepared))
    w_emb_t, w_rad, w_chan_r, w_chan_t, w_hidden, w_back, w_out_col, w_rbf2 = prepared
    inner, slab_send = call(
        slab_kernel,
        (shape((height, inner_len), bf16), shape((height, LANES), bf16)),
        (own, picks, *got, *corners),
        [pltpu.VMEM((PARTS, inner_len), f32)],
    )
    slab_got = swapped(slab_send)
    feat, place = call(
        embed_kernel,
        (shape((features, inner_len), bf16), shape((6, hpad, LANES), f32)),
        (inner, w_emb_t),
    )
    grads, slab_grad, energy = call(
        edge_kernel,
        (shape((3, hpad, LANES), f32), shape((3, LANES), f32), shape((1, atoms), f32)),
        (
            meta,
            lift,
            centers,
            others,
            feat,
            place,
            slab_got,
            w_emb_t,
            w_rad,
            w_chan_t,
            w_chan_r,
            w_hidden,
            w_back,
            w_out_col,
            w_rbf2,
        ),
        [
            pltpu.VMEM((features, (groups - 1) * 256 + WINDOW), bf16),
            pltpu.VMEM((atoms // span, features, span + LANES), bf16),
            pltpu.VMEM((6, hpad, LANES), f32),
            pltpu.VMEM((6 * hpad + 48, 2 * LANES), bf16),
            pltpu.VMEM((atoms // span, 9 * chans, span), bf16),
        ]
        + [
            pltpu.VMEM((WINDOW + span + LANES, eb), bf16),
            pltpu.VMEM((features, eb), f32),
            pltpu.VMEM((depth, span, eb), bf16),
            pltpu.VMEM((depth, 2 * LANES, eb), bf16),
            pltpu.VMEM((depth, features, eb), bf16),
            pltpu.VMEM((depth, features, eb), bf16),
            pltpu.VMEM((depth, chans, eb), f32),
            pltpu.VMEM((16, -(-depth // 8) * 8, eb), f32),
            pltpu.VMEM((11, -(-depth // 8) * 8, eb), f32),
            pltpu.VMEM((depth, features, eb), bf16),
            pltpu.VMEM((depth, 64, eb), f32),
        ]
        * SETS
        + [
            pltpu.VMEM((atoms // span, 9 * chans, span), f32),
        ]
        * SUMS
        + [
            pltpu.VMEM((atoms // span, 6 * hpad + 8 * (span // LANES), 2 * LANES), f32),
        ]
        * SUMS,
        smem=2,
        limit=big,
    )
    slab_back = swapped(slab_grad)
    along_x, along_y = shape((15, LANES), f32), shape((9, LANES), f32)
    own_grad, to_xm, to_xp, to_ym, to_yp = call(
        return_kernel,
        (shape((3, 8, LANES), f32), along_x, along_x, along_y, along_y),
        (grads, slab_back, picks),
    )
    from_xp, from_xm = shifted(to_xm, "gx", 1), shifted(to_xp, "gx", -1)
    to_ym, to_yp = call(turn_kernel, (along_y, along_y), (from_xp, from_xm, to_ym, to_yp))
    from_yp, from_ym = shifted(to_ym, "gy", 1), shifted(to_yp, "gy", -1)
    forces = call(
        force_kernel,
        shape((3, 1, atoms), f32),
        (own_grad, picks, from_xp, from_xm, from_yp, from_ym),
        [pltpu.VMEM((8, 8, LANES), f32)],
    )
    return (energy.reshape(1, 1, 1, atoms), forces.reshape(1, 1, 1, 3, atoms))


def solution(mesh):
    return jax.shard_map(
        per_device,
        mesh=mesh,
        in_specs=(
            P("gx", "gy", "gz", None, None),
            P("gx", "gy", "gz", None, None),
            P("gx", "gy", "gz", None),
            P("gx", "gy", "gz", None),
            P("gx", "gy", "gz"),
            P("gx", "gy", "gz", None, None),
            P("gx", "gy", "gz", None),
            P(),
            P(),
            P(),
            P(),
            P(),
            P(),
        ),
        out_specs=(P("gx", "gy", "gz", None), P("gx", "gy", "gz", None, None)),
        check_vma=False,
    )
```

```python
import collections

import jax
import jax.numpy as jnp
from jax import lax
from jax.experimental import pallas as pl
from jax.experimental.pallas import tpu as pltpu
from jax.sharding import PartitionSpec as P

f32 = jnp.float32
bf16 = jnp.bfloat16
LANES = 128
PARTS = 16
BLOCK = 512
SETS = 4
SUMS = 2
WINDOW = 768
ROOT3 = 3.0**0.5
BANDS = (0, 1, 1, 1, 2, 2, 2, 2, 2)

rim_cells = [(0, 0), (0, 1), (0, 2), (1, 0), (1, 2), (2, 0), (2, 1), (2, 2)]
cycle_cells = [(p, q) for p in range(5) for q in range(5) if p in (0, 4) or q in (0, 4)]


def source_of(position):
    if position == 0:
        return (-1, 2)
    if position == 4:
        return (1, 0)
    return (0, position - 1)


routes = {}
for _cycle, (_p, _q) in enumerate(cycle_cells):
    (_sx, _a), (_sy, _b) = source_of(_p), source_of(_q)
    routes.setdefault((_sx, _sy), []).append((_cycle, rim_cells.index((_a, _b))))
sides = [(0, -1), (0, 1), (-1, 0), (1, 0)]


def dot(a, b):
    return lax.dot_general(a, b, (((1,), (0,)), ((), ())), preferred_element_type=f32)


def dot_t(a, b):
    return lax.dot_general(a, b, (((1,), (1,)), ((), ())), preferred_element_type=f32)


def rows_of(shape):
    return lax.broadcasted_iota(jnp.int32, shape, 0)


def one_hot(index, size):
    return jnp.where(rows_of((size, index.shape[1])) == index, 1.0, 0.0)


def halves(values):
    upper = values.astype(bf16).astype(f32)
    return upper, values - upper


def masked(hot_low, high16, value):
    mask = jnp.where(high16 == value, 1.0, 0.0).astype(bf16)
    size, lanes = hot_low.shape
    return (hot_low.reshape(size // 16, 16, lanes) * mask[None]).reshape(size, lanes)


def half_silu(x):
    half = 0.5 * x
    return (0.5 * (half * (1.0 + jnp.tanh(half)))).astype(bf16)


def pack_kernel(pos_ref, attr_ref, picks_ref, own_ref, *rest):
    sends, parts = rest[:4], rest[4]
    atoms, width = attr_ref.shape
    eye = jnp.where(
        rows_of((width, width)) == lax.broadcasted_iota(jnp.int32, (width, width), 1), 1.0, 0.0
    ).astype(bf16)
    own_ref[0:width, :] = dot_t(eye, attr_ref[...]).astype(bf16)
    parts[...] = jnp.zeros_like(parts)
    for d in range(3):
        parts[d : d + 1, :], parts[3 + d : 4 + d, :] = halves(pos_ref[d])
    own_ref[width : width + PARTS, :] = parts[...].astype(bf16)
    packed = own_ref[...]
    for rim in range(8):
        hot = one_hot(picks_ref[rim : rim + 1, :], atoms).astype(bf16)
        cell = dot(packed, hot).astype(bf16)
        for way, send in zip(sides, sends):
            for slot, (_, source) in enumerate(routes[way]):
                if source == rim:
                    send[:, slot * LANES : (slot + 1) * LANES] = cell


def corner_kernel(minus_ref, plus_ref, to_plus_ref, to_minus_ref):
    first, last = slice(0, LANES), slice(2 * LANES, 3 * LANES)
    for slot, ref in enumerate((minus_ref, plus_ref)):
        lanes = slice(slot * LANES, (slot + 1) * LANES)
        to_plus_ref[:, lanes] = ref[:, last]
        to_minus_ref[:, lanes] = ref[:, first]


def slab_kernel(own_ref, picks_ref, *rest):
    got, corners, (inner_ref, send_ref, parts) = rest[:4], rest[4:6], rest[6:]
    atoms = own_ref.shape[1]
    height = own_ref.shape[0]
    width = height - PARTS
    inner_len = inner_ref.shape[1]
    inner_ref[:, 0:atoms] = own_ref[...]
    parts[...] = jnp.zeros_like(parts)
    parts[0:6, 0:atoms] = own_ref[width:height, :].astype(f32)[0:6]
    arrivals = []
    for way, ref in zip(sides, got):
        for slot, (cycle, _) in enumerate(routes[way]):
            arrivals.append((way, ref, slot, cycle))
    for sx, ref in zip((-1, 1), corners):
        for slot, sy in enumerate((-1, 1)):
            arrivals.append(((sx, sy), ref, slot, routes[(sx, sy)][0][0]))
    for way, ref, slot, cycle in arrivals:
        lanes = slice(slot * LANES, (slot + 1) * LANES)
        into = slice(atoms + cycle * LANES, atoms + (cycle + 1) * LANES)
        inner_ref[0:width, into] = ref[0:width, lanes]
        arrived = ref[width:height, lanes].astype(f32)
        joined = arrived[0:3] + arrived[3:6]
        axis = rows_of((3, LANES))
        shift = jnp.where(axis == 0, float(way[0]), jnp.where(axis == 1, float(way[1]), 0.0))
        upper, lower = halves(joined + shift)
        parts[0:3, into] = upper
        parts[3:6, into] = lower
    inner_ref[width:height, :] = parts[...].astype(bf16)
    hot = one_hot(picks_ref[8:9, :], inner_len).astype(bf16)
    send_ref[...] = dot(inner_ref[...], hot).astype(bf16)


def unit(size):
    lanes = lax.broadcasted_iota(jnp.int32, (size, size), 1)
    return jnp.where(rows_of((size, size)) == lanes, 1.0, 0.0)


def weights_kernel(
    stacked_ref,
    small_ref,
    emb_t_ref,
    rad_ref,
    chan_ref,
    w_chan_t_ref,
    hidden_ref,
    back_ref,
    out_ref,
    rbf_ref,
    scratch,
):
    features = stacked_ref.shape[1]
    width = emb_t_ref.shape[1]
    inner = back_ref.shape[0]
    w_emb = stacked_ref[0:width]
    w_back = stacked_ref[width : width + inner]
    w_chan_t = stacked_ref[width + inner :]
    eye = unit(features)
    eye_b = eye.astype(bf16)
    emb_t_ref[...] = dot_t(eye_b, w_emb).astype(bf16)
    chan_ref[...] = dot_t(eye_b, w_chan_t).astype(bf16)
    w_chan_t_ref[...] = w_chan_t
    turned = (0.5 * dot_t(eye_b, w_back)).astype(bf16)
    hidden_ref[...] = turned
    back_ref[...] = w_back
    column = jnp.sum(eye * small_ref[8:9, :], axis=1, keepdims=True)
    out_ref[...] = jnp.broadcast_to(column, out_ref.shape)
    upper, lower = halves(0.5 * small_ref[0:8, :])
    rbf_ref[...] = jnp.concatenate([upper, lower], axis=0).astype(bf16)
    scratch[...] = jnp.zeros_like(scratch)
    for start, value in ((0, upper), (8, upper), (16, lower), (24, lower)):
        scratch[start : start + 8, :] = value
    rad_ref[...] = dot_t(eye_b, scratch[...].astype(bf16)).astype(bf16)


def embed_kernel(inner_ref, w_emb_ref, feat_ref, place_ref):
    width = w_emb_ref.shape[1]
    inner_len = inner_ref.shape[1]
    for first in range(0, inner_len, 512):
        raw = dot(w_emb_ref[...], inner_ref[0:width, first : first + 512])
        feat_ref[:, first : first + 512] = half_silu(raw)
    parts = inner_ref[width:, :].astype(f32)
    place_ref[...] = jnp.zeros_like(place_ref)
    for high in range(inner_len // LANES):
        place_ref[0:6, high, :] = parts[0:6, high * LANES : (high + 1) * LANES]


def bucket_kernel(count_ref, ends_ref, center_ref, other_ref, meta_ref, marks_s, rows_s, low_s):
    lines = ends_ref.shape[0] // 2
    keys = marks_s.shape[0] // lines
    groups = keys // 2
    count = count_ref[0]
    c, o = ends_ref[0:lines, :], ends_ref[lines:, :]
    shape = (lines, LANES)
    order = rows_of(shape) * LANES + lax.broadcasted_iota(jnp.int32, shape, 1)
    key = lax.shift_right_logical(c, 8) * groups + lax.shift_right_logical(o, 8)
    key = jnp.where(order < count, key, -1)
    for k in range(keys):
        marks_s[k * lines : (k + 1) * lines, :] = jnp.where(key == k, 1.0, 0.0).astype(bf16)
    square = (LANES, LANES)
    tri = jnp.where(rows_of(square) < lax.broadcasted_iota(jnp.int32, square, 1), 1.0, 0.0)
    tri = tri.astype(bf16)
    tall = (lines, lines)
    below = jnp.where(lax.broadcasted_iota(jnp.int32, tall, 1) < rows_of(tall), 1.0, 0.0)
    marks = marks_s[...]
    inside = dot(marks, tri)
    totals = dot(marks, jnp.ones(square, bf16))
    lane = lax.broadcasted_iota(jnp.int32, shape, 1)
    by_key = jnp.zeros(shape, f32)
    for k in range(keys):
        by_key = jnp.where(lane == k, totals[k * lines : (k + 1) * lines], by_key)
    before = dot(below.astype(bf16), by_key.astype(bf16))
    everything = jnp.broadcast_to(jnp.sum(by_key, axis=0, keepdims=True), (16, LANES))
    upper, lower = halves(everything)
    start = (dot(upper.astype(bf16), tri) + dot(lower.astype(bf16), tri))[0:1]
    row_lane = lane[0:1]
    first = jnp.sum(jnp.where(row_lane < groups, everything[0:1], 0.0), axis=1, keepdims=True)
    second = jnp.sum(jnp.where(row_lane >= groups, everything[0:1], 0.0), axis=1, keepdims=True)
    first_blocks = jnp.floor((first + (BLOCK - 1)) * (1.0 / BLOCK))
    blocks = first_blocks + jnp.floor((second + (BLOCK - 1)) * (1.0 / BLOCK))
    start = start + jnp.where(row_lane >= groups, first_blocks * BLOCK - first, 0.0)
    offset = before + start
    slot = jnp.full(shape, -1.0, f32)
    for k in range(keys):
        place = inside[k * lines : (k + 1) * lines] + offset[:, k : k + 1]
        slot = jnp.where(key == k, place, slot)
    slot = slot.astype(jnp.int32)
    slot_high = lax.shift_right_arithmetic(slot, 7)
    slot_low = lax.bitwise_and(slot, LANES - 1)
    highs = center_ref.shape[0]
    values = [
        jnp.ones(shape, f32),
        lax.bitwise_and(c, 255).astype(f32),
        lax.shift_right_logical(o, 7).astype(f32),
        lax.bitwise_and(o, LANES - 1).astype(f32),
    ]
    for line in range(lines):
        lanes = slice(line * LANES, (line + 1) * LANES)
        high = one_hot(slot_high[line : line + 1], highs)
        rows_s[:, lanes] = jnp.concatenate(
            [high * value[line : line + 1] for value in values], axis=0
        ).astype(bf16)
        low_s[:, lanes] = one_hot(slot_low[line : line + 1], LANES).astype(bf16)
    placed = dot_t(rows_s[...], low_s[...])
    center = placed[highs : 2 * highs] + placed[0:highs] - 1.0
    other = placed[2 * highs : 3 * highs] * float(LANES) + placed[3 * highs :]
    center_ref[...] = center.astype(jnp.int32)
    other_ref[...] = other.astype(jnp.int32)
    group = jnp.floor(other * (1.0 / 256.0))
    none = float(groups)
    low = jnp.min(jnp.where(center >= 0.0, group, none), axis=1, keepdims=True)
    high = jnp.max(jnp.where(center >= 0.0, group, -1.0), axis=1, keepdims=True)
    block = lax.broadcasted_iota(jnp.int32, (highs, LANES), 1)
    line_of = rows_of((highs, LANES)) // (BLOCK // LANES) == block
    low = jnp.min(jnp.where(line_of, low, none), axis=0, keepdims=True)
    high = jnp.max(jnp.where(line_of, high, -1.0), axis=0, keepdims=True)
    low = jnp.where(high < 0.0, 0.0, low)
    high = jnp.where(high < 0.0, 0.0, high)
    rest_first = first - (first_blocks - 1.0) * BLOCK
    rest_second = second - (blocks - first_blocks - 1.0) * BLOCK
    sparse = jnp.where(rest_first < rest_second, first_blocks, blocks) - 1.0
    fewest = jnp.minimum(rest_first, rest_second)
    meta_ref[4:5, :] = jnp.broadcast_to(sparse, (1, LANES)).astype(jnp.int32)
    meta_ref[5:6, :] = jnp.broadcast_to(fewest, (1, LANES)).astype(jnp.int32)
    meta_ref[0:1, :] = jnp.broadcast_to(first_blocks, (1, LANES)).astype(jnp.int32)
    meta_ref[1:2, :] = jnp.broadcast_to(blocks, (1, LANES)).astype(jnp.int32)
    meta_ref[2:3, :] = low.astype(jnp.int32)
    meta_ref[3:4, :] = high.astype(jnp.int32)


def harmonic_rows(x, y, z):
    return [
        None,
        x,
        y,
        z,
        ROOT3 * x * y,
        ROOT3 * y * z,
        ROOT3 * z * x,
        0.5 * ROOT3 * (x * x - y * y),
        0.5 * (3.0 * z * z - 1.0),
    ]


def fold8(values):
    return jnp.sum(values.reshape(values.shape[0] // 8, 8, values.shape[1]), axis=0)


FIELDS = (
    ["hot", "extra", "center_hot", "lows", "latent", "slope", "chan"]
    + ["geo", "res", "dlat", "dharm", "tensor", "acc"]
)
Scratch = collections.namedtuple("Scratch", FIELDS)


def edge_kernel(
    meta_ref,
    lift_ref,
    centers_ref,
    others_ref,
    feat_in_ref,
    place_in_ref,
    slab_ref,
    w_emb_ref,
    w_rad_ref,
    w_chan_t_ref,
    w_chan_ref,
    w_hidden_ref,
    w_back_ref,
    w_out_ref,
    w_rbf_ref,
    grad_ref,
    slab_grad_ref,
    energy_ref,
    feat,
    feat_c,
    place,
    place_b,
    tensor_b,
    *scratch,
):
    names = len(FIELDS) - 2
    sums = [scratch[names * SETS + index :: SUMS] for index in range(SUMS)]
    sets = [
        Scratch(*scratch[index * names : (index + 1) * names], *sums[index % SUMS])
        for index in range(SETS)
    ]
    eb = centers_ref.shape[2]
    width = w_emb_ref.shape[1]
    features = feat_in_ref.shape[0]
    inner_len = feat_in_ref.shape[1]
    table = inner_len + LANES
    highs = table // LANES
    span = tensor_b.shape[2]
    halves_n = tensor_b.shape[0]
    chans = w_chan_ref.shape[1]
    hpad = place_in_ref.shape[1]
    first_blocks = meta_ref[0, 0]
    total_blocks = meta_ref[1, 0]
    rounds = total_blocks // SETS

    feat[:, 0:inner_len] = feat_in_ref[...]
    raw = dot(w_emb_ref[...], slab_ref[0:width, :])
    feat[:, inner_len:table] = half_silu(raw)
    feat[:, table:] = jnp.zeros((features, feat.shape[1] - table), bf16)
    for half in range(halves_n):
        feat_c[half, :, 0:span] = feat_in_ref[:, half * span : (half + 1) * span]
        feat_c[half, :, span:] = w_rad_ref[...]
    place[...] = place_in_ref[...]
    arrived = slab_ref[width:, :].astype(f32)
    joined = arrived[0:3] + arrived[3:6]
    joined = joined + jnp.where(rows_of((3, LANES)) == 2, lift_ref[0], 0.0)
    upper, lower = halves(joined)
    place[0:3, highs - 1, :] = upper
    place[3:6, highs - 1, :] = lower
    place_b[...] = jnp.zeros_like(place_b)
    place_b[0 : 6 * hpad, 0:LANES] = place[...].reshape(6 * hpad, LANES).astype(bf16)
    place_b[6 * hpad :, LANES:] = place[:, 0:8, :].reshape(48, LANES).astype(bf16)
    for own in sets:
        own.hot[WINDOW + span + 32 :, :] = jnp.zeros((LANES - 32, eb), bf16)
        for ref in (own.extra, own.tensor, own.acc):
            ref[...] = jnp.zeros_like(ref)

    def half_of(b):
        return jnp.where(b >= first_blocks, 1, 0)

    sparse, fewest = meta_ref[4, 0], meta_ref[5, 0]

    def each_block(run):
        def sides(at, picked, lanes=eb):
            listed = []
            for index in picked:
                turn = SETS * at + index
                b = turn + jnp.where(turn >= sparse, 1, 0)
                b = jnp.where(turn == total_blocks - 1, sparse, b)
                listed.append((sets[index], b, at, lanes))
            return listed

        def step(at, carry):
            run(sides(at, range(SETS)))
            return carry

        lax.fori_loop(0, rounds, step, 0)
        rest = total_blocks - SETS * rounds

        @pl.when(jnp.logical_and(rest == 1, fewest <= LANES))
        def _():
            run(sides(rounds, [0], LANES))

        @pl.when(jnp.logical_and(rest == 1, fewest > LANES))
        def _():
            run(sides(rounds, [0]))

        @pl.when(rest > 1)
        def _():
            run(sides(rounds, [0, 1]))

        @pl.when(rest == 3)
        def _():
            run(sides(rounds, [2]))

    def put_row(ref, index, at, value):
        spare = eb - value.shape[1]
        if spare:
            value = jnp.concatenate([value, jnp.zeros((1, spare), f32)], axis=1)
        ref[index, pl.ds(at, 1), :] = value

    def locate(sides):
        for own_s, b, at, w in sides:
            slot_c = centers_ref[b][:, 0:w]
            o = others_ref[b][:, 0:w]
            c = jnp.maximum(slot_c, 0)
            c_high = lax.shift_right_logical(c, 7)
            o_high = lax.shift_right_logical(o, 7)
            hot_c = one_hot(lax.bitwise_and(c, LANES - 1), LANES).astype(bf16)
            hot_o = one_hot(lax.bitwise_and(o, LANES - 1), LANES).astype(bf16)
            lows = jnp.concatenate([hot_o, hot_c], axis=0)
            own_s.lows[at, :, 0:w] = lows
            c_high16 = jnp.broadcast_to(c_high, (16, w))
            own_s.center_hot[at, :, 0:w] = jnp.concatenate(
                [masked(hot_c, c_high16, high) for high in range(span // LANES)], axis=0
            )
            both = dot(place_b[...], lows)
            picked = (both[0 : 3 * hpad] + both[3 * hpad : 6 * hpad]).reshape(3, hpad, w)
            po = jnp.sum(picked * one_hot(o_high, hpad)[None], axis=1)
            picked = both[6 * hpad :]
            picked = (picked[0:24] + picked[24:48]).reshape(3, 8, w)
            c_whole = c_high + half_of(b) * (span // LANES)
            pc = jnp.sum(picked * one_hot(c_whole, 8)[None], axis=1)
            sep = po - pc
            for d in range(3):
                put_row(own_s.geo, d, at, sep[d : d + 1])
            put_row(own_s.geo, 6, at, jnp.where(slot_c >= 0, 1.0, 0.0))

    each_block(locate)
    for own in sets:
        rx, ry, rz = own.geo[0], own.geo[1], own.geo[2]
        squared = rx * rx + ry * ry + rz * rz
        inv_d = lax.rsqrt(squared + 0.25)
        x, y, z = rx * inv_d, ry * inv_d, rz * inv_d
        own.geo[3] = inv_d
        own.geo[4] = (squared + 0.25) * inv_d
        own.geo[5] = 1.0 / (1.0 + squared * squared * (1.0 / 16.0))
        own.geo[7] = squared
        for m, value in enumerate(harmonic_rows(x, y, z)[1:]):
            own.geo[8 + m] = value

    def geo_row(side, index):
        own_s, _, at, w = side
        return own_s.geo[index, pl.ds(at, 1), :][:, 0:w]

    def harmonics(side):
        return [None] + [geo_row(side, 8 + m) for m in range(8)]

    def prepare(side):
        own_s, b, at, w = side
        hot = own_s.hot
        hot_o = own_s.lows[at, 0:LANES, 0:w]
        o_high = lax.shift_right_logical(others_ref[b][:, 0:w], 7) - 2 * meta_ref[2, b]
        o_high16 = jnp.broadcast_to(o_high, (16, w))
        for high in range(WINDOW // LANES):
            rows = slice(high * LANES, (high + 1) * LANES)
            hot[rows, 0:w] = masked(hot_o, o_high16, high)
        hot[WINDOW : WINDOW + span, 0:w] = own_s.center_hot[at, :, 0:w]
        mu = 0.5 + 0.4 * rows_of((8, w)).astype(f32)
        u = (geo_row(side, 4) - mu) * 2.0
        upper, lower = halves(jnp.exp(-(u * u)) * geo_row(side, 5))
        radial = jnp.concatenate([upper, lower], axis=0).astype(bf16)
        hot[WINDOW + span : WINDOW + span + 16, 0:w] = radial
        hot[WINDOW + span + 16 : WINDOW + span + 32, 0:w] = radial

    def window(group):
        return feat[:, pl.ds(pl.multiple_of(group * 256, 256), WINDOW)]

    def windows_of(side):
        b = side[1]
        return (meta_ref[3, b] - meta_ref[2, b]) // (WINDOW // 256) + 1

    def further_windows(side):
        own_s, b, _, w = side
        windows = windows_of(side)

        @pl.when(windows > 1)
        def _():
            o = others_ref[b][:, 0:w]
            hot_o = one_hot(lax.bitwise_and(o, LANES - 1), LANES).astype(bf16)
            o_high16 = jnp.broadcast_to(lax.shift_right_logical(o, 7), (16, w))

            def add(index, carry):
                group = meta_ref[2, b] + index * (WINDOW // 256)
                hot = jnp.concatenate(
                    [
                        masked(hot_o, o_high16 - 2 * group, high)
                        for high in range(WINDOW // LANES)
                    ],
                    axis=0,
                )
                own_s.extra[:, 0:w] += dot(window(group), hot)
                return carry

            lax.fori_loop(1, windows, add, 0)

    def clear_windows(side):
        @pl.when(windows_of(side) > 1)
        def _():
            side[0].extra[...] = jnp.zeros_like(side[0].extra)

    def mix(side):
        own_s, b, _, w = side
        tables = jnp.concatenate([window(meta_ref[2, b]), feat_c[half_of(b)]], axis=1)
        return dot(tables, own_s.hot[:, 0:w]) + own_s.extra[:, 0:w]

    def activate(side, mixed):
        own_s, _, at, w = side
        up = 1.0 + jnp.tanh(mixed)
        value = mixed * up
        latent = value.astype(bf16)
        own_s.slope[at, :, 0:w] = (up + value * (2.0 - up)).astype(bf16)
        return latent

    def spread(side, latent):
        own_s, _, at, w = side
        own_s.latent[at, :, 0:w] = latent
        chan = dot(w_chan_t_ref[...], latent) * geo_row(side, 6)
        own_s.chan[at, :, 0:w] = chan
        return jnp.concatenate(
            [(chan if h is None else chan * h).astype(bf16) for h in harmonics(side)], axis=0
        )

    def gather_tensor(side):
        own_s, b, at, w = side
        return dot(tensor_b[half_of(b)], own_s.center_hot[at, :, 0:w])

    def add_tensor(side, products, hot):
        own_s, b, _, w = side
        own_s.tensor[half_of(b)] += dot_t(products, hot)

    def first_pass(sides):
        for side in sides:
            further_windows(side)
        mixed = []
        for side in sides:
            prepare(side)
            mixed.append(mix(side))
        products = []
        for side, values in zip(sides, mixed):
            products.append(spread(side, activate(side, values)))
        for side, values in zip(sides, products):
            add_tensor(side, values, side[0].center_hot[side[2], :, 0 : side[3]])
        for side in sides:
            clear_windows(side)

    each_block(first_pass)
    tensor_b[...] = (0.125 * sum(own.tensor[...] for own in sets[:SUMS])).astype(bf16)
    for own in sets[:SUMS]:
        own.tensor[...] = jnp.zeros_like(own.tensor)

    def invariants(side, gathered):
        harm = harmonics(side)
        parts = [gathered[m * chans : (m + 1) * chans] for m in range(9)]
        bands = [parts[0], None, None]
        for m in range(1, 9):
            term = parts[m] * harm[m]
            band = BANDS[m]
            bands[band] = term if bands[band] is None else bands[band] + term
        return jnp.concatenate([band.astype(bf16) for band in bands], axis=0)

    def hidden(side, invariant):
        inputs = jnp.concatenate([side[0].latent[side[2], :, 0 : side[3]], invariant], axis=0)
        return dot(w_hidden_ref[...], inputs)

    def readout(side, pre):
        own_s, _, at, w = side
        up = 1.0 + jnp.tanh(pre)
        value = pre * up
        weight = jnp.concatenate([w_out_ref[...]] * (w // LANES), axis=1)
        put_row(own_s.res, 10, at, jnp.sum(value * weight, axis=0, keepdims=True))
        scale = 0.5 * geo_row(side, 5) * geo_row(side, 6)
        return ((up + value * (2.0 - up)) * (weight * scale)).astype(bf16)

    def unfold(side, back, gathered):
        own_s, _, at, w = side
        harm = harmonics(side)
        own_s.dlat[at, :, 0:w] = back[0:features].astype(bf16)
        dbands = [
            back[features + band * chans : features + (band + 1) * chans] for band in range(3)
        ]
        for m in range(1, 9):
            part = gathered[m * chans : (m + 1) * chans]
            own_s.dharm[at, (m - 1) * 8 : m * 8, 0:w] = fold8(dbands[BANDS[m]] * part)
        return jnp.concatenate(
            [
                (dbands[BANDS[m]] if harm[m] is None else dbands[BANDS[m]] * harm[m]).astype(bf16)
                for m in range(9)
            ],
            axis=0,
        )

    def second_pass(sides):
        gathered = [gather_tensor(side) for side in sides]
        pre = [hidden(side, invariants(side, g)) for side, g in zip(sides, gathered)]
        back = [dot(w_back_ref[...], readout(side, values)) for side, values in zip(sides, pre)]
        for side, values, g in zip(sides, back, gathered):
            add_tensor(side, unfold(side, values, g), side[0].center_hot[side[2], :, 0 : side[3]])

    each_block(second_pass)
    tensor_b[...] = (0.125 * sum(own.tensor[...] for own in sets[:SUMS])).astype(bf16)

    def channels_back(side, gathered):
        own_s, _, at, w = side
        harm = harmonics(side)
        chan = own_s.chan[at, :, 0:w]
        dchan = gathered[0:chans]
        for m in range(1, 9):
            part = gathered[m * chans : (m + 1) * chans]
            dchan = dchan + part * harm[m]
            total = own_s.dharm[at, (m - 1) * 8 : m * 8, 0:w] + fold8(part * chan)
            put_row(own_s.res, m - 1, at, jnp.sum(total, axis=0, keepdims=True))
        return (dchan * geo_row(side, 6)).astype(bf16)

    def radial_back(side, dchan):
        own_s, _, at, w = side
        dlat = own_s.dlat[at, :, 0:w] + dot(w_chan_ref[...], dchan).astype(bf16)
        drad = dot(w_rbf_ref[...], dlat * own_s.slope[at, :, 0:w])
        drad = drad[0:8] + drad[8:16]
        mu = 0.5 + 0.4 * rows_of((8, w)).astype(f32)
        u = (geo_row(side, 4) - mu) * 2.0
        weighted = drad * jnp.exp(-(u * u))
        put_row(own_s.res, 8, at, jnp.sum(weighted, axis=0, keepdims=True))
        put_row(own_s.res, 9, at, jnp.sum(weighted * u, axis=0, keepdims=True))

    def third_pass(sides):
        gathered = [gather_tensor(side) for side in sides]
        for side, g in zip(sides, gathered):
            radial_back(side, channels_back(side, g))

    each_block(third_pass)

    for own in sets:
        x, y, z = own.geo[8], own.geo[9], own.geo[10]
        inv_d, dist, env = own.geo[3], own.geo[4], own.geo[5]
        live, squared = own.geo[6], own.geo[7]
        dh = [None] + [own.res[m] for m in range(8)]
        summed = own.res[10]
        denv = own.res[8] + live * summed
        ddist = -4.0 * env * own.res[9]
        dx = dh[1] + ROOT3 * (y * dh[4] + z * dh[6] + x * dh[7])
        dy = dh[2] + ROOT3 * (x * dh[4] + z * dh[5] - y * dh[7])
        dz = dh[3] + ROOT3 * (y * dh[5] + x * dh[6]) + 3.0 * z * dh[8]
        ddist = ddist - (dx * x + dy * y + dz * z) * inv_d
        dsq = denv * (env * env * squared * -0.125) + ddist * (0.5 * inv_d)
        both = 2.0 * dsq * dist
        results = [dx * inv_d + both * x, dy * inv_d + both * y, dz * inv_d + both * z]
        results.append(summed * env * live)
        for index, value in enumerate(results):
            own.res[index], own.res[4 + index] = halves(value)

    def collect(sides):
        for own_s, b, at, w in sides:
            split = [own_s.res[index, pl.ds(at, 1), :][:, 0:w] for index in range(8)]
            mask_o = one_hot(lax.shift_right_logical(others_ref[b][:, 0:w], 7), hpad)
            values = jnp.concatenate(split, axis=0)
            c_high = lax.shift_right_arithmetic(centers_ref[b][:, 0:w], 7)
            rows = jnp.concatenate(
                [mask_o * split[4 * part + d] for part in range(2) for d in range(3)]
                + [
                    values * jnp.where(c_high == high, 1.0, 0.0)
                    for high in range(span // LANES)
                ],
                axis=0,
            ).astype(bf16)
            own_s.acc[half_of(b)] += dot_t(rows, own_s.lows[at, :, 0:w])

    each_block(collect)
    acc = [sum(own.acc[half] for own in sets[:SUMS]) for half in range(halves_n)]
    sum_o = sum(value[0 : 6 * hpad, 0:LANES] for value in acc)
    sum_o = sum_o[0 : 3 * hpad] + sum_o[3 * hpad :]
    for d in range(3):
        grad_ref[d] = sum_o[d * hpad : (d + 1) * hpad]
        slab_grad_ref[d : d + 1, :] = sum_o[d * hpad + highs - 1 : d * hpad + highs]
    for half in range(halves_n):
        for part in range(span // LANES):
            high = half * (span // LANES) + part
            base = 6 * hpad + part * 8
            sum_c = acc[half][base : base + 4, LANES:] + acc[half][base + 4 : base + 8, LANES:]
            for d in range(3):
                grad_ref[d, high : high + 1, :] = (
                    sum_o[d * hpad + high : d * hpad + high + 1] - sum_c[d : d + 1]
                )
            energy_ref[:, high * LANES : (high + 1) * LANES] = sum_c[3:4]


def return_kernel(grad_ref, back_ref, picks_ref, own_ref, to_xm_ref, to_xp_ref, to_ym_ref, to_yp_ref):
    hpad = grad_ref.shape[1]
    z_rows = picks_ref[8:9, :]
    mask = one_hot(lax.shift_right_logical(z_rows, 7), hpad)
    low = one_hot(lax.bitwise_and(z_rows, LANES - 1), LANES).astype(bf16)
    pieces = [halves(back_ref[d : d + 1, :]) for d in range(3)]
    rows = jnp.concatenate(
        [mask * pieces[d][part] for part in range(2) for d in range(3)], axis=0
    ).astype(bf16)
    landed = dot_t(rows, low)
    landed = landed[0 : 3 * hpad] + landed[3 * hpad :]
    base = own_ref.shape[1] // 2
    for d in range(3):
        total = grad_ref[d] + landed[d * hpad : (d + 1) * hpad]
        own_ref[d] = total[0:8]
        for cycle, (p, q) in enumerate(cycle_cells):
            value = total[base + cycle : base + cycle + 1]
            if p in (0, 4):
                ref = to_xm_ref if p == 0 else to_xp_ref
                ref[q * 3 + d : q * 3 + d + 1, :] = value
            else:
                ref = to_ym_ref if q == 0 else to_yp_ref
                ref[(p - 1) * 3 + d : (p - 1) * 3 + d + 1, :] = value


def turn_kernel(from_xp_ref, from_xm_ref, to_ym_ref, to_yp_ref, send_ym_ref, send_yp_ref):
    for q, old, new in ((0, to_ym_ref, send_ym_ref), (4, to_yp_ref, send_yp_ref)):
        new[0:3, :] = old[0:3, :] + from_xm_ref[q * 3 : q * 3 + 3, :]
        new[3:6, :] = old[3:6, :]
        new[6:9, :] = old[6:9, :] + from_xp_ref[q * 3 : q * 3 + 3, :]


def force_kernel(
    own_ref, picks_ref, from_xp_ref, from_xm_ref, from_yp_ref, from_ym_ref, out_ref, rim_sum
):
    rim_sum[...] = jnp.zeros_like(rim_sum)
    for a, ref in ((2, from_xp_ref), (0, from_xm_ref)):
        for b in range(3):
            rim_sum[rim_cells.index((a, b)), 0:3, :] += ref[(b + 1) * 3 : (b + 2) * 3, :]
    for b, ref in ((2, from_yp_ref), (0, from_ym_ref)):
        for a in range(3):
            rim_sum[rim_cells.index((a, b)), 0:3, :] += ref[a * 3 : (a + 1) * 3, :]
    total = jnp.zeros((48, LANES), f32)
    for rim in range(8):
        index = picks_ref[rim : rim + 1, :]
        mask = one_hot(lax.shift_right_logical(index, 7), 8)
        low = one_hot(lax.bitwise_and(index, LANES - 1), LANES).astype(bf16)
        values = rim_sum[rim]
        pieces = [halves(values[d : d + 1, :]) for d in range(3)]
        rows = jnp.concatenate(
            [mask * pieces[d][part] for part in range(2) for d in range(3)], axis=0
        ).astype(bf16)
        total = total + dot_t(rows, low)
    total = total[0:24] + total[24:48]
    for d in range(3):
        for high in range(out_ref.shape[2] // LANES):
            value = own_ref[d, high : high + 1, :] + total[d * 8 + high : d * 8 + high + 1, :]
            out_ref[d, :, high * LANES : (high + 1) * LANES] = -value


def call(kernel, out_shape, args, scratch=(), smem=0, limit=12 * 1024 * 1024):
    vmem = pl.BlockSpec(memory_space=pltpu.VMEM)
    scalar = pl.BlockSpec(memory_space=pltpu.SMEM)
    return pl.pallas_call(
        kernel,
        out_shape=out_shape,
        in_specs=[scalar] * smem + [vmem] * (len(args) - smem),
        out_specs=jax.tree.map(lambda _: vmem, out_shape),
        scratch_shapes=list(scratch),
        compiler_params=pltpu.CompilerParams(vmem_limit_bytes=limit),
    )(*args)


def shifted(x, axis, step):
    count = lax.axis_size(axis)
    return lax.ppermute(x, axis, [((i + step) % count, i) for i in range(count)])


def swapped(x):
    count = lax.axis_size("gz")
    return lax.ppermute(x, "gz", [(i, i ^ 1) for i in range(count)])


def per_device(
    positions,
    attributes,
    edge_center,
    edge_other,
    edge_count,
    rim_rows,
    z_rows,
    w_emb,
    w_rbf,
    w_chan,
    w_lat,
    w_ten,
    w_out,
):
    pos = positions.reshape(3, 1, -1)
    attr = attributes[0, 0, 0]
    rim = rim_rows[0, 0, 0]
    zr = z_rows[0, 0]
    count = edge_count[0, 0]
    atoms, width = attr.shape
    edges = edge_center.shape[-1]
    features = w_emb.shape[1]
    chans = w_chan.shape[1]
    height = width + PARTS
    inner_len = atoms + 16 * LANES
    table = inner_len + LANES
    hpad = -(-(table // LANES) // 8) * 8
    eb = BLOCK
    span = 2 * LANES
    blocks = edges // eb + atoms // span - 1
    depth = -(-blocks // SETS)
    slot_rows = -(-(blocks * eb // LANES) // 8) * 8
    lift = (1 - 2 * lax.axis_index("gz")).astype(f32).reshape(1)
    big = 47 * 1024 * 1024

    shape = jax.ShapeDtypeStruct
    picks = jnp.concatenate([rim, zr], axis=0)
    own, *sent = call(
        pack_kernel,
        (shape((height, atoms), bf16),) + (shape((height, 3 * LANES), bf16),) * 4,
        (pos, attr, picks),
        [pltpu.VMEM((PARTS, atoms), f32)],
    )
    got = [
        shifted(x, "gx" if way[0] else "gy", way[0] + way[1]) for x, way in zip(sent, sides)
    ]
    lines = edges // LANES
    groups = -(-table // 256)
    ends = jnp.concatenate(
        [edge_center.reshape(lines, LANES), edge_other.reshape(lines, LANES)], axis=0
    )
    bucketed = call(
        bucket_kernel,
        (
            shape((slot_rows, LANES), jnp.int32),
            shape((slot_rows, LANES), jnp.int32),
            shape((6, LANES), jnp.int32),
        ),
        (count, ends),
        [
            pltpu.VMEM((2 * groups * lines, LANES), bf16),
            pltpu.VMEM((4 * slot_rows, edges), bf16),
            pltpu.VMEM((LANES, edges), bf16),
        ],
        smem=1,
        limit=24 * 1024 * 1024,
    )
    first, bucketed = lax.optimization_barrier((got[:2], bucketed))
    got = [*first, *got[2:]]
    centers, others, meta = bucketed
    centers = centers.reshape(-1, 1, eb)
    others = others.reshape(-1, 1, eb)
    to_plus, to_minus = call(
        corner_kernel,
        (shape((height, 2 * LANES), bf16),) * 2,
        (got[0], got[1]),
    )
    w_emb, w_rbf, to_plus = lax.optimization_barrier((w_emb, w_rbf, to_plus))
    prepared = call(
        weights_kernel,
        (
            shape((features, width), bf16),
            shape((features, LANES), bf16),
            shape((features, chans), bf16),
            shape((chans, features), bf16),
            shape((features, features + 3 * chans), bf16),
            shape((features + 3 * chans, features), bf16),
            shape((features, LANES), f32),
            shape((16, features), bf16),
        ),
        (
            jnp.concatenate([w_emb, w_lat, w_ten, w_chan.T], axis=0),
            jnp.concatenate([w_rbf, w_out[None]], axis=0),
        ),
        [pltpu.VMEM((LANES, features), f32)],
    )
    corners = [shifted(to_plus, "gx", -1), shifted(to_minus, "gx", 1)]
    corners, prepared = lax.optimization_barrier((corners, prepared))
    w_emb_t, w_rad, w_chan_r, w_chan_t, w_hidden, w_back, w_out_col, w_rbf2 = prepared
    inner, slab_send = call(
        slab_kernel,
        (shape((height, inner_len), bf16), shape((height, LANES), bf16)),
        (own, picks, *got, *corners),
        [pltpu.VMEM((PARTS, inner_len), f32)],
    )
    slab_got = swapped(slab_send)
    feat, place = call(
        embed_kernel,
        (shape((features, inner_len), bf16), shape((6, hpad, LANES), f32)),
        (inner, w_emb_t),
    )
    grads, slab_grad, energy = call(
        edge_kernel,
        (shape((3, hpad, LANES), f32), shape((3, LANES), f32), shape((1, atoms), f32)),
        (
            meta,
            lift,
            centers,
            others,
            feat,
            place,
            slab_got,
            w_emb_t,
            w_rad,
            w_chan_t,
            w_chan_r,
            w_hidden,
            w_back,
            w_out_col,
            w_rbf2,
        ),
        [
            pltpu.VMEM((features, (groups - 1) * 256 + WINDOW), bf16),
            pltpu.VMEM((atoms // span, features, span + LANES), bf16),
            pltpu.VMEM((6, hpad, LANES), f32),
            pltpu.VMEM((6 * hpad + 48, 2 * LANES), bf16),
            pltpu.VMEM((atoms // span, 9 * chans, span), bf16),
        ]
        + [
            pltpu.VMEM((WINDOW + span + LANES, eb), bf16),
            pltpu.VMEM((features, eb), f32),
            pltpu.VMEM((depth, span, eb), bf16),
            pltpu.VMEM((depth, 2 * LANES, eb), bf16),
            pltpu.VMEM((depth, features, eb), bf16),
            pltpu.VMEM((depth, features, eb), bf16),
            pltpu.VMEM((depth, chans, eb), f32),
            pltpu.VMEM((16, -(-depth // 8) * 8, eb), f32),
            pltpu.VMEM((11, -(-depth // 8) * 8, eb), f32),
            pltpu.VMEM((depth, features, eb), bf16),
            pltpu.VMEM((depth, 64, eb), f32),
        ]
        * SETS
        + [
            pltpu.VMEM((atoms // span, 9 * chans, span), f32),
        ]
        * SUMS
        + [
            pltpu.VMEM((atoms // span, 6 * hpad + 8 * (span // LANES), 2 * LANES), f32),
        ]
        * SUMS,
        smem=2,
        limit=big,
    )
    slab_back = swapped(slab_grad)
    along_x, along_y = shape((15, LANES), f32), shape((9, LANES), f32)
    own_grad, to_xm, to_xp, to_ym, to_yp = call(
        return_kernel,
        (shape((3, 8, LANES), f32), along_x, along_x, along_y, along_y),
        (grads, slab_back, picks),
    )
    from_xp, from_xm = shifted(to_xm, "gx", 1), shifted(to_xp, "gx", -1)
    to_ym, to_yp = call(turn_kernel, (along_y, along_y), (from_xp, from_xm, to_ym, to_yp))
    from_yp, from_ym = shifted(to_ym, "gy", 1), shifted(to_yp, "gy", -1)
    forces = call(
        force_kernel,
        shape((3, 1, atoms), f32),
        (own_grad, picks, from_xp, from_xm, from_yp, from_ym),
        [pltpu.VMEM((8, 8, LANES), f32)],
    )
    return (energy.reshape(1, 1, 1, atoms), forces.reshape(1, 1, 1, 3, atoms))


def solution(mesh):
    return jax.shard_map(
        per_device,
        mesh=mesh,
        in_specs=(
            P("gx", "gy", "gz", None, None),
            P("gx", "gy", "gz", None, None),
            P("gx", "gy", "gz", None),
            P("gx", "gy", "gz", None),
            P("gx", "gy", "gz"),
            P("gx", "gy", "gz", None, None),
            P("gx", "gy", "gz", None),
            P(),
            P(),
            P(),
            P(),
            P(),
            P(),
        ),
        out_specs=(P("gx", "gy", "gz", None), P("gx", "gy", "gz", None, None)),
        check_vma=False,
    )
```
